32 devices in a mesh: slab: 8 (over z, core), clus: 4 (over y, x).
Axes of the slice: x: 2, y: 2, z: 4, core: 2. Of those that a mesh axis runs over, the one named last changes fastest.
Arguments:
- incident: float32 [8, 128, 200], P(None, ('slab', 'clus')), may hold values from -6 to 6
- history: float32 [16, 128, 200], P(None, ('slab', 'clus')), may hold values from -6 to 6
- near_blocks: bfloat16 [128, 12, 200, 200], P(('slab', 'clus')), may hold values from -0.09375 to 0.09375
- near_idx: int32 [128, 12], P(('slab', 'clus')), may hold values from 0 to 127, as said below
- near_cnt: int32 [128], P(('slab', 'clus')), may hold values from 3 to 12
- near_lag: int32 [128, 12], P(('slab', 'clus')), may hold values from 1 to 15
- near_frac: float32 [128, 12], P(('slab', 'clus')), may hold values from 0 to 1
- inverses: bfloat16 [128, 200, 200], P(('slab', 'clus')), may hold values from -0.4375 to 0.4375
- rays: bfloat16 [128, 512, 200], P(('slab', 'clus')), may hold values from -0.4375 to 0.4375
- shift: float32 [128, 512], P(('slab', 'clus')), may hold values from -1 to 1
- far_idx: int32 [32, 8], replicated, may hold values from 0 to 31, as said below
- far_lag: int32 [32, 8], replicated, may hold values from 1 to 16
- trans: bfloat16 [32, 8, 512], replicated, may hold values from -0.5 to 0.5
Outputs:
- currents: float32 [8, 128, 200], P(None, ('slab', 'clus'))
The draws below stay inside these ranges and needn't reach their ends.
Inputs may be any that keep to these rules, and one draw needn't show every extreme that they name: `near_idx`: every entry is a cluster whose slab (cluster number divided by 16) differs by at most one from the slab of the entry's row. `far_idx`: every entry is a group whose slab (group number divided by the number of devices along clus) differs by two or more from the slab of the entry's row.
All inputs are finite; a program needn't handle non-finite values.
Results may differ from the reference program's by a relative error of at most 0.0045.
Values sent between devices are 32-bit elements; how exact they have to be, the bound alone decides.
No kernel may reach another device: no remote copies, remote signals or barrier semaphores. Data moves between devices by JAX's collectives and lax.ppermute only.
A program may use at most 128 MiB of HBM per device.

```python
import jax
import jax.numpy as jnp
from jax import lax

U = 200
DIR = 512
CL_DEV = 4
NB = 12
NF = 8
LAGS = 16
STEPS = 8
SLAB_CL = 16
GROUPS = 32
NC = 128
N_SLAB = 8
N_CLUS = 4


def draw_near_idx(key, part):
    key = jax.random.fold_in(key, 7)
    first_key, second_key = jax.random.split(key)
    cluster = jnp.arange(NC, dtype=jnp.int32)[:, None]
    slab_of = cluster // SLAB_CL
    column = jnp.arange(NB, dtype=jnp.int32)[None, :]
    random_step = jax.random.randint(first_key, (NC, NB), -1, 2)
    offset = jnp.where(column == 0, 0, jnp.where(column == 1, -1, jnp.where(column == 2, 1, random_step)))
    target = jnp.clip(slab_of + offset, 0, N_SLAB - 1)
    member = jax.random.randint(second_key, (NC, NB), 0, SLAB_CL)
    return (target * SLAB_CL + member).astype(jnp.int32)


def draw_far_idx(key, part):
    key = jax.random.fold_in(key, 11)
    first_key, second_key = jax.random.split(key)
    own_slab = jnp.arange(GROUPS, dtype=jnp.int32)[:, None] // N_CLUS
    offset = jax.random.randint(first_key, (GROUPS, NF), 2, N_SLAB - 1)
    target = (own_slab + offset) % N_SLAB
    member = jax.random.randint(second_key, (GROUPS, NF), 0, N_CLUS)
    listed = (target * N_CLUS + member).astype(jnp.int32)
    return listed.at[0, 0].set(GROUPS - 1)


def place_ends(entries, rng, low, largest):
    spot = [jax.random.randint(jax.random.fold_in(rng, axis), (), 0, length) for axis, length in enumerate(entries.shape)]
    main_axis = entries.shape.index(max(entries.shape))
    beside = spot[:main_axis] + [(spot[main_axis] + 1) % entries.shape[main_axis]] + spot[main_axis + 1:]
    return entries.at[tuple(spot)].set(low).at[tuple(beside)].set(largest)


def shard_levels(own_key, shape, cuts, smallest, top_value):
    def one(position, shards_of):
        heights = jax.random.uniform(jax.random.fold_in(jax.random.fold_in(own_key, 6), position), (shards_of,), jnp.float32, smallest / len(cuts), top_value / len(cuts))
        return jnp.repeat(jnp.exp(heights), shape[position] // shards_of).reshape((-1,) + (1,) * (len(shape) - position - 1))

    loudness = one(*cuts[0])
    for cut in cuts[1:]:
        loudness = loudness * one(*cut)
    return loudness


def centred(key, dims, deviation, bound, cuts=(), kind=jnp.bfloat16):
    factor_of = shard_levels(key, dims, cuts, -0.22, 0.18) if cuts else 1.0
    array = jax.random.normal(key, dims, jnp.float32) * deviation * factor_of
    return jnp.minimum(jnp.maximum(array, -bound), bound).astype(kind)


def setup_inputs(seed: int = 0) -> dict:
    streams_of = jax.random.split(jax.random.key(seed), 14)
    incident = centred(streams_of[0], (STEPS, NC, U), 1.0, 6.0, ((1, 32),), jnp.float32)
    history = centred(streams_of[1], (LAGS, NC, U), 1.0, 6.0, ((1, 32),), jnp.float32)
    near_blocks = centred(streams_of[2], (NC, NB, U, U), (2 * U * NB) ** -0.5, 0.09375, ((0, 32),))
    near_idx = draw_near_idx(jax.random.fold_in(streams_of[13], 71), 0)
    near_cnt = place_ends(jax.random.randint(streams_of[4], (NC,), 3, NB + 1), jax.random.fold_in(streams_of[4], 1), 3, NB).astype(jnp.int32)
    near_lag = place_ends(jax.random.randint(streams_of[5], (NC, NB), 1, LAGS), jax.random.fold_in(streams_of[5], 1), 1, LAGS - 1).astype(jnp.int32)
    near_frac = jnp.clip(1.0 * jax.random.uniform(streams_of[6], (NC, NB), jnp.float32) ** shard_levels(streams_of[6], (NC, NB), ((0, 32),), -0.2, 0.2), 0.0, 1.0)
    inverses = centred(streams_of[7], (NC, U, U), U ** -0.5, 0.4375, ((0, 32),))
    rays = centred(streams_of[8], (NC, DIR, U), U ** -0.5, 0.4375, ((0, 32),))
    shift = jnp.clip(jax.random.uniform(streams_of[9], (NC, DIR), jnp.float32, -1.0, 1.0) * shard_levels(streams_of[9], (NC, DIR), ((0, 32),), -0.4, 0.0), -1.0, 1.0)
    far_idx = draw_far_idx(jax.random.fold_in(streams_of[13], 71), 0)
    far_lag = place_ends(jax.random.randint(streams_of[11], (GROUPS, NF), 1, LAGS + 1), jax.random.fold_in(streams_of[11], 1), 1, LAGS).astype(jnp.int32)
    trans = centred(streams_of[12], (GROUPS, NF, DIR), (4 * NF * CL_DEV) ** -0.5, 0.5)
    return {"incident": incident, "history": history, "near_blocks": near_blocks, "near_idx": near_idx, "near_cnt": near_cnt, "near_lag": near_lag, "near_frac": near_frac, "inverses": inverses, "rays": rays, "shift": shift, "far_idx": far_idx, "far_lag": far_lag, "trans": trans}


def rounded(value):
    return lax.optimization_barrier(value.astype(jnp.bfloat16)).astype(jnp.float32)


def group_spectra(rays, shift, current):
    def one_group(pieces):
        ray_block, shift_block, cur_block = pieces
        ray_vals = jnp.einsum("cdu,cu->cd", ray_block.astype(jnp.float32), rounded(cur_block))
        return jnp.sum(ray_vals * shift_block, axis=0)
    return lax.map(one_group, (rays.reshape(GROUPS, CL_DEV, DIR, U), shift.reshape(GROUPS, CL_DEV, DIR), current.reshape(GROUPS, CL_DEV, U)))


def reference(incident, history, near_blocks, near_idx, near_cnt, near_lag, near_frac, inverses, rays, shift, far_idx, far_lag, trans):
    timeline = jnp.concatenate([history, jnp.zeros((STEPS, NC, U), jnp.float32)], axis=0)
    spec_hist = jnp.stack([group_spectra(rays, shift, history[k]) for k in range(LAGS)], axis=0)
    spec_time = jnp.concatenate([spec_hist, jnp.zeros((STEPS, GROUPS, DIR), jnp.float32)], axis=0)
    live_slot = jnp.arange(NB)[None, :] < near_cnt[:, None]
    near_weight = near_frac[..., None]
    trans_wide = trans.astype(jnp.float32)
    blocks_shaped = near_blocks.reshape(GROUPS, CL_DEV, NB, U, U)
    rays_shaped = rays.reshape(GROUPS, CL_DEV, DIR, U)
    inverse_shaped = inverses.reshape(GROUPS, CL_DEV, U, U)
    outputs = []
    for step_index in range(STEPS):
        lag_slot = step_index - near_lag + LAGS
        first_lag = timeline[lag_slot, near_idx]
        second = timeline[lag_slot - 1, near_idx]
        blended = jnp.where(live_slot[..., None], (1.0 - near_weight) * first_lag + near_weight * second, 0.0)

        def near_group(pieces):
            block, vector = pieces
            return jnp.einsum("cjuv,cjv->cu", block.astype(jnp.float32), rounded(vector))
        near_field = lax.map(near_group, (blocks_shaped, blended.reshape(GROUPS, CL_DEV, NB, U))).reshape(NC, U)
        far_slot = step_index - far_lag + LAGS
        picked = spec_time[far_slot, far_idx]
        incoming = jnp.sum(trans_wide * picked, axis=1)
        inbound = jnp.repeat(incoming, CL_DEV, axis=0) * shift

        def far_group(pieces):
            ray_block, vector = pieces
            return jnp.einsum("cdu,cd->cu", ray_block.astype(jnp.float32), rounded(vector))
        far_field = lax.map(far_group, (rays_shaped, inbound.reshape(GROUPS, CL_DEV, DIR))).reshape(NC, U)
        right_side = incident[step_index] - near_field - far_field

        def solve_group(pieces):
            block, vector = pieces
            return jnp.einsum("cuv,cv->cu", block.astype(jnp.float32), rounded(vector))
        current = lax.map(solve_group, (inverse_shaped, right_side.reshape(GROUPS, CL_DEV, U))).reshape(NC, U)
        outputs.append(current)
        timeline = timeline.at[LAGS + step_index].set(current)
        spec_time = spec_time.at[LAGS + step_index].set(group_spectra(rays, shift, current))
    return jnp.stack(outputs, axis=0)
```

```python
import jax
import jax.numpy as jnp
from jax import lax
from jax.sharding import PartitionSpec as P


def local(
    incident,
    history,
    near_blocks,
    near_idx,
    near_cnt,
    near_lag,
    near_frac,
    inverses,
    rays,
    shift,
    far_idx,
    far_lag,
    trans,
):
    lag_count, local_count, unknowns = history.shape
    step_count = incident.shape[0]
    dir_count = rays.shape[1]
    slab_count = lax.axis_size("slab")
    clus_count = lax.axis_size("clus")
    group_count = slab_count * clus_count
    slab_index = lax.axis_index("slab")
    myself = slab_index * clus_count + lax.axis_index("clus")
    slot = local_count * unknowns
    half = group_count // 2
    order = [(i + half) % group_count for i in range(group_count)]
    group_slab = jnp.arange(group_count) // clus_count
    is_near = jnp.abs(group_slab - slab_index) <= 1

    gathered = lax.all_gather(history, "clus", axis=1, tiled=True)
    up = [(i, i + 1) for i in range(slab_count - 1)]
    down = [(b, a) for a, b in up]
    low = lax.ppermute(gathered, "slab", up)
    high = lax.ppermute(gathered, "slab", down)
    near_hist = jnp.concatenate([low, gathered, high], axis=1)
    slab_size = local_count * clus_count
    near_time = jnp.concatenate(
        [near_hist, jnp.zeros((step_count,) + near_hist.shape[1:], jnp.float32)], axis=0
    )
    near_local = near_idx - (slab_index - 1) * slab_size

    hist_rays = jnp.einsum(
        "cdu,tcu->tcd", rays, history.astype(jnp.bfloat16), preferred_element_type=jnp.float32
    )
    own_time = [jnp.sum(hist_rays[k] * shift, axis=0) for k in range(lag_count)]

    listed = far_idx == myself
    trans_wide = trans.astype(jnp.float32)
    weights = []
    for lag in range(1, lag_count + 1):
        chosen = (listed & (far_lag == lag))[..., None]
        weights.append(jnp.sum(jnp.where(chosen, trans_wide, 0.0), axis=1))

    live_slot = jnp.arange(near_idx.shape[1])[None, :] < near_cnt[:, None]
    near_weight = near_frac[..., None]
    outputs = []
    current = history[lag_count - 1]
    for step_index in range(step_count):
        outgoing = sum(
            weights[lag - 1] * own_time[step_index - lag + lag_count][None, :]
            for lag in range(1, lag_count + 1)
        )
        outgoing = jnp.pad(outgoing, ((0, 0), (0, slot - dir_count)))
        message = jnp.where(is_near[:, None], current.reshape(1, slot), outgoing)
        message = jnp.roll(message, -half, axis=0)
        arrived = lax.all_to_all(
            message, ("slab", "clus"), 0, 0, tiled=True, axis_index_groups=[order]
        )
        arrived = jnp.roll(arrived, half, axis=0)
        incoming = jnp.sum(jnp.where(is_near[:, None], 0.0, arrived[:, :dir_count]), axis=0)
        if step_index > 0:
            padded = jnp.pad(arrived, ((clus_count, clus_count), (0, 0)))
            fresh = lax.dynamic_slice_in_dim(
                padded, slab_index * clus_count, 3 * clus_count, axis=0
            ).reshape(3 * slab_size, unknowns)
            near_time = near_time.at[lag_count + step_index - 1].set(fresh)
        lag_slot = step_index - near_lag + lag_count
        first_lag = near_time[lag_slot, near_local]
        second = near_time[lag_slot - 1, near_local]
        blended = jnp.where(
            live_slot[..., None], (1.0 - near_weight) * first_lag + near_weight * second, 0.0
        ).astype(jnp.bfloat16)
        near_field = jnp.einsum(
            "cjuv,cjv->cu", near_blocks, blended, preferred_element_type=jnp.float32
        )
        inbound = (shift * incoming[None, :]).astype(jnp.bfloat16)
        far_field = jnp.einsum("cdu,cd->cu", rays, inbound, preferred_element_type=jnp.float32)
        right_side = (incident[step_index] - near_field - far_field).astype(jnp.bfloat16)
        current = jnp.einsum("cuv,cv->cu", inverses, right_side, preferred_element_type=jnp.float32)
        outputs.append(current)
        if step_index + 1 < step_count:
            ray_vals = jnp.einsum(
                "cdu,cu->cd", rays, current.astype(jnp.bfloat16), preferred_element_type=jnp.float32
            )
            own_time.append(jnp.sum(ray_vals * shift, axis=0))
    return jnp.stack(outputs, axis=0)


def solution(mesh):
    both = ("slab", "clus")
    in_specs = (
        P(None, both, None),
        P(None, both, None),
        P(both, None, None, None),
        P(both, None),
        P(both),
        P(both, None),
        P(both, None),
        P(both, None, None),
        P(both, None, None),
        P(both, None),
        P(),
        P(),
        P(),
    )
    out_specs = P(None, both, None)
    return jax.shard_map(local, mesh=mesh, in_specs=in_specs, out_specs=out_specs, check_vma=False)
```

```python
import functools

import jax
import jax.numpy as jnp
from jax import lax
from jax.experimental import pallas as pl
from jax.experimental.pallas import tpu as pltpu
from jax.sharding import PartitionSpec as P

LANE = 128
PACK = 16
KEPT = 6
CHUNK = 3
VMEM_LIMIT = 24 * 1024 * 1024
HBM = pl.BlockSpec(memory_space=pltpu.HBM)
ANY = pl.BlockSpec(memory_space=pl.ANY)
VMEM = pl.BlockSpec(memory_space=pltpu.VMEM)
SMEM = pl.BlockSpec(memory_space=pltpu.SMEM)


def rows_of(wide, count):
    return jnp.concatenate([wide[:, r * LANE : (r + 1) * LANE] for r in range(count)], axis=0)


def padded(wide, width):
    return jnp.concatenate(
        [wide, jnp.zeros((wide.shape[0], width - wide.shape[1]), wide.dtype)], axis=1
    )


def dot(left, right):
    return jnp.dot(left, right, preferred_element_type=jnp.float32)


def dot_t(left, right):
    return lax.dot_general(
        left, right, (((1,), (1,)), ((), ())), preferred_element_type=jnp.float32
    )


def pack_kernel(history, packed):
    lags, clusters, unknowns = history.shape
    halves = packed.shape[1] // clusters
    for half in range(halves):
        low, high = half * LANE, min(unknowns, (half + 1) * LANE)
        part = history[:, :, low:high]
        if high - low < LANE:
            part = jnp.concatenate(
                [part, jnp.zeros((lags, clusters, LANE - (high - low)), jnp.float32)], axis=2
            )
        packed[:, half * clusters : (half + 1) * clusters, :] = part


def in_hbm(*arrays):
    return [pltpu.with_memory_space_constraint(array, pltpu.HBM) for array in arrays]


def in_vmem(*arrays):
    return [pltpu.with_memory_space_constraint(array, pltpu.VMEM) for array in arrays]


def start_all(pairs, sems):
    copies = []
    for number, (source, target) in enumerate(pairs):
        copy = pltpu.make_async_copy(source, target, sems.at[number])
        copy.start()
        copies.append(copy)
    return copies


def wait_all(copies):
    for copy in copies:
        copy.wait()


def any_of(flags):
    found = flags[0]
    for flag in flags[1:]:
        found = found | flag
    return found


def row_of(cluster_number, clusters, halves):
    place = lax.rem(cluster_number, clusters)
    return (cluster_number - place) * halves + place


def begin_kernel(
    clus_count,
    rays_in, history_in, shift_in, trans_in, far_idx_in, far_lag_in, near_idx_in, near_cnt_in,
    near_lag_in, near_frac_in, blocks,
    spectra, message, weights, fresh_weights, kept, kept_weight, near_plan, old_plan,
    rays, history, shift, trans, far_idx, far_lag, near_idx, near_cnt, near_lag, near_frac, sem,
    sems,
):
    small = start_all(
        (
            (near_idx_in, near_idx), (near_cnt_in, near_cnt), (near_lag_in, near_lag),
            (near_frac_in, near_frac), (far_idx_in, far_idx), (far_lag_in, far_lag),
        ),
        sems,
    )
    large = start_all(
        ((history_in, history), (rays_in, rays), (shift_in, shift), (trans_in, trans)),
        sems.at[pl.ds(6, 4)],
    )
    lags, clusters, unknowns = history.shape
    dir_rows = spectra.shape[1]
    entries, groups = far_idx.shape
    slots = near_idx.shape[1]
    halves = message.shape[1] // clusters
    myself = lax.axis_index("slab") * clus_count + lax.axis_index("clus")

    def kept_copy(place, entry):
        source = blocks.at[lax.div(entry, slots), lax.rem(entry, slots)]
        return pltpu.make_async_copy(source, kept.at[place], sem)

    for place in range(3 * KEPT + 1):
        near_plan[place] = 0
    kept_weight[...] = jnp.zeros(kept_weight.shape, jnp.float32)
    message[...] = jnp.zeros(message.shape, jnp.float32)
    fresh_weights[...] = jnp.zeros(fresh_weights.shape, jnp.float32)
    wait_all(small)
    near_plan[0] = 0
    for cluster in range(clusters):
        fresh = [
            (slot < near_cnt[cluster]) & (near_lag[cluster, slot] == 1) for slot in range(slots)
        ]

        @pl.when(any_of(fresh))
        def _(cluster=cluster, fresh=fresh):
            for slot in range(slots):

                @pl.when(fresh[slot])
                def _(slot=slot):
                    count = near_plan[0]
                    entry = jnp.int32(cluster * slots + slot)
                    near_plan[3 * count + 1] = entry
                    near_plan[3 * count + 2] = jnp.int32(cluster)
                    near_plan[3 * count + 3] = row_of(near_idx[cluster, slot], clusters, halves)
                    row = jnp.zeros((1, kept_weight.shape[1]), jnp.float32)
                    kept_weight[pl.ds(count, 1), :] = row + (1.0 - near_frac[cluster, slot])
                    near_plan[0] = count + 1

                    @pl.when(count < KEPT)
                    def _():
                        kept_copy(count, entry).start()

    wait_all(large)
    total = jnp.zeros((lags, dir_rows * LANE), jnp.float32)
    for cluster in range(clusters):
        past = history[:, cluster, :].astype(jnp.bfloat16)
        total += dot(past, rays[cluster]) * shift[cluster : cluster + 1, :]
    for lag in range(lags):
        spectra[lag] = rows_of(total[lag : lag + 1], dir_rows)

    def one(group, counts):
        listed = [far_idx[column, group] == myself for column in range(entries)]

        def add(counts):
            place, old_count = counts
            for column in range(entries):
                lag = far_lag[column, group]

                @pl.when(listed[column])
                def _(place=place, lag=lag, column=column, old_count=old_count):
                    row = trans[group, column : column + 1, :].astype(jnp.float32)
                    weight = rows_of(row, dir_rows)
                    weights[place] = weight
                    message[group, :dir_rows, :] += weight * spectra[lags - lag]

                    @pl.when(lag == 1)
                    def _():
                        fresh_weights[group] += weight

                    @pl.when(lag > 1)
                    def _():
                        old_plan[3 * old_count + 1] = group
                        old_plan[3 * old_count + 2] = place
                        old_plan[3 * old_count + 3] = lag

                place = place + jnp.where(listed[column], 1, 0)
                old_count = old_count + jnp.where(listed[column] & (lag > 1), 1, 0)
            return place, old_count

        return lax.cond(any_of(listed), add, lambda counts: counts, counts)

    counts = lax.fori_loop(0, groups, one, (jnp.int32(0), jnp.int32(0)))
    old_plan[0] = counts[1]

    def finish(place, carry):
        kept_copy(place, near_plan[3 * place + 1]).wait()
        return carry

    lax.fori_loop(0, jnp.minimum(near_plan[0], KEPT), finish, 0)


def near_kernel(step, last, clus_count, lags, *refs):
    (
        near_idx_in, near_cnt_in, near_lag_in, near_frac_in, old_plan_in, incident_in, weights,
        past_spectra, blocks,
    ) = refs[:9]
    newer, refs = refs[9 : 9 + step], refs[9 + step :]
    if step:
        table_in, base, blended, known = refs[:4]
        refs = refs[4:]
    else:
        mid, core_swap, chip_swap, base, blended, known, table_out = refs[:7]
        refs = refs[7:]
    (
        table, held, tall, field, spectra, incident, near_idx, near_cnt, near_lag, near_frac,
        old_plan, sems, more_sems, out_sem,
    ) = refs
    clusters, slots = near_idx.shape
    unknowns = incident.shape[1]
    halves = tall.shape[2] // LANE
    side_rows = table.shape[1] // 3
    slab = lax.axis_index("slab")
    now = lags + max(step - 1, 0)
    chunks = [(first, min(CHUNK, slots - first)) for first in range(0, slots, CHUNK)]

    def block_copy(cluster, number):
        first, size = chunks[number]
        return pltpu.make_async_copy(
            blocks.at[cluster, pl.ds(first, size)],
            held.at[pl.ds(cluster * slots + first, size)],
            sems.at[cluster * len(chunks) + number],
        )

    if step:
        wide_pairs = [(table_in.at[pl.ds(0, now)], table.at[pl.ds(0, now)])]
    else:
        odd = lax.rem(slab, 2)
        wide_pairs = []
        for source, side in ((mid, 1), (core_swap, 2 - 2 * odd), (chip_swap, 2 * odd)):
            start = pl.multiple_of(side * side_rows, side_rows)
            wide_pairs.append((source, table.at[pl.ds(0, lags), pl.ds(start, side_rows)]))
    small = start_all(
        (
            (near_cnt_in, near_cnt), (near_idx_in, near_idx), (near_lag_in, near_lag),
            (near_frac_in, near_frac),
        ),
        more_sems,
    )
    wide = start_all(wide_pairs, more_sems.at[pl.ds(4, 3)])
    pairs = [(incident_in.at[step], incident)]
    if not last:
        pairs.append((old_plan_in, old_plan))
    others = start_all(pairs, more_sems.at[pl.ds(7, 2)])
    for cluster in range(clusters):
        block_copy(cluster, 0).start()
    tall[...] = jnp.zeros(tall.shape, jnp.float32)
    if not last:
        spectra[:lags] = past_spectra[...]
        for back, source in enumerate(newer):
            spectra[lags + back] = source[...]
        known[...] = jnp.zeros(known.shape, jnp.float32)
    wait_all(small)
    most = near_cnt[0]
    for cluster in range(1, clusters):
        most = jnp.maximum(most, near_cnt[cluster])
    for number in range(1, len(chunks)):
        for cluster in range(clusters):

            @pl.when(chunks[number][0] < near_cnt[cluster])
            def _():
                block_copy(cluster, number).start()

    wait_all(wide)
    if not step:
        keep = pltpu.make_async_copy(
            table.at[pl.ds(0, lags)], table_out.at[pl.ds(0, lags)], out_sem
        )
        keep.start()
    first_row = (slab - 1) * side_rows
    newest = lags + step - 2 if step else lags - 1
    for cluster in range(clusters):
        for slot in range(slots):
            row = row_of(near_idx[cluster, slot], clusters, halves) - first_row
            lag_slot = step - near_lag[cluster, slot] + lags
            frac = near_frac[cluster, slot]
            weight = jnp.where(lag_slot > newest, 0.0, 1.0 - frac)
            first_slot = jnp.minimum(lag_slot, newest)
            for half in range(halves):
                at = pl.ds(row + half * clusters, 1)
                tall[cluster, slot : slot + 1, half * LANE : (half + 1) * LANE] = (
                    weight * table[first_slot, at, :] + frac * table[lag_slot - 1, at, :]
                )
    for cluster in range(clusters):
        blended[cluster * slots : (cluster + 1) * slots, :] = tall[cluster, :slots, :]
    wait_all(others)
    if not last:

        def one(place, carry):
            before, total = carry
            group = old_plan[3 * place + 1]
            slot = step + 1 + lags - old_plan[3 * place + 3]
            term = weights[old_plan[3 * place + 2]] * spectra[slot]
            total = jnp.where(group == before, total, 0.0) + term
            known[group] = total
            return group, total

        lax.fori_loop(
            0, old_plan[0], one, (jnp.int32(-1), jnp.zeros(known.shape[1:], jnp.float32))
        )
    which = lax.broadcasted_iota(jnp.int32, (tall.shape[1], unknowns), 0)

    def part(number, cluster):
        first, size = chunks[number]
        values = tall[cluster].astype(jnp.bfloat16)[:, :unknowns]
        sums = jnp.zeros((tall.shape[1], unknowns), jnp.float32)
        for slot in range(first, first + size):
            counts = slot < near_cnt[cluster]
            if step:
                counts = counts & (near_lag[cluster, slot] > 1)
            product = dot_t(values, held[cluster * slots + slot])
            sums = jnp.where(which == jnp.where(counts, slot, -1), product, sums)
        return sums

    for cluster in range(clusters):
        block_copy(cluster, 0).wait()
    for cluster in range(clusters):
        field[cluster] = part(0, cluster)
    for number in range(1, len(chunks)):

        @pl.when(chunks[number][0] < most)
        def _():
            for cluster in range(clusters):

                @pl.when(chunks[number][0] < near_cnt[cluster])
                def _():
                    block_copy(cluster, number).wait()

            for cluster in range(clusters):
                field[cluster] += part(number, cluster)

    for cluster in range(clusters):
        total = jnp.sum(field[cluster], axis=0, keepdims=True)
        base[cluster : cluster + 1, :] = incident[cluster : cluster + 1, :] - total
    if not step:
        keep.wait()


def march_kernel(step, last, clus_count, slab_count, lags, *refs):
    (
        near_plan_in, base, blended, known, kept, kept_weight, rays, inverses, shift,
        fresh_weights, arrived, blocks,
    ) = refs[:12]
    if last:
        _, output = refs[12:14]
        refs = refs[14:]
    elif step:
        _, _, output, table, spectrum, message = refs[12:18]
        refs = refs[18:]
    else:
        output, spectrum, message = refs[12:15]
        refs = refs[15:]
    near_plan, current, values, extra, field, sem, sems = refs
    clusters, unknowns = base.shape
    slots = blocks.shape[1]
    groups, dir_rows = fresh_weights.shape[:2]
    rows_each = arrived.shape[0] // groups
    halves = rows_each // clusters
    side_rows = clus_count * rows_each
    slab = lax.axis_index("slab")
    which = lax.broadcasted_iota(jnp.int32, (clusters, unknowns), 0)
    plan_copy = pltpu.make_async_copy(near_plan_in, near_plan, sems.at[0])
    plan_copy.start()
    kept_copies = []
    if step and not last:
        for side in range(3):
            other = jnp.clip(slab + (side - 1), 0, slab_count - 1)
            copy = pltpu.make_async_copy(
                arrived.at[pl.ds(pl.multiple_of(other * side_rows, side_rows), side_rows)],
                table.at[lags + step - 1, pl.ds(side * side_rows, side_rows)],
                sems.at[1 + side],
            )
            copy.start()
            kept_copies.append(copy)

    def is_near(group):
        return jnp.abs(group // clus_count - slab) <= 1

    sums = [jnp.zeros((dir_rows, LANE), jnp.float32) for _ in range(4)]
    for group in range(groups):
        first = group * rows_each
        sums[group % 4] += jnp.where(is_near(group), 0.0, arrived[first : first + dir_rows, :])
    incoming = (sums[0] + sums[1]) + (sums[2] + sums[3])
    row_in = jnp.concatenate([incoming[r : r + 1] for r in range(dir_rows)], axis=1)
    inbound = (shift[...] * row_in).astype(jnp.bfloat16)
    far = jnp.zeros((clusters, unknowns), jnp.float32)
    for cluster in range(clusters):
        far = jnp.where(which == cluster, dot_t(inbound, rays[cluster]), far)
    remaining = base[...] - far

    def fresh_row(place):
        entry, row = near_plan[3 * place + 1], near_plan[3 * place + 3]
        newest = jnp.concatenate(
            [arrived[pl.ds(row + half * clusters, 1), :] for half in range(halves)], axis=1
        )
        return blended[pl.ds(entry, 1), :] + kept_weight[pl.ds(place, 1), :] * newest

    plan_copy.wait()
    if step:
        count = near_plan[0]
        values[...] = jnp.zeros(values.shape, jnp.float32)
        for place in range(KEPT):
            values[place : place + 1, :] = fresh_row(place)
        rows = values[...].astype(jnp.bfloat16)[:, :unknowns]
        for place in range(KEPT):
            product = dot_t(rows, kept[place])[place : place + 1]
            cluster = jnp.where(place < count, near_plan[3 * place + 2], -1)
            remaining = remaining - jnp.where(which == cluster, product, 0.0)
        field[...] = remaining

        @pl.when(count > KEPT)
        def _():
            def one(place, carry):
                entry = near_plan[3 * place + 1]
                cluster = near_plan[3 * place + 2]
                source = blocks.at[cluster, entry - cluster * slots]
                copy = pltpu.make_async_copy(source, extra, sem)
                copy.start()
                row = jnp.broadcast_to(fresh_row(place), (8, halves * LANE))
                copy.wait()
                product = dot_t(row.astype(jnp.bfloat16)[:, :unknowns], extra[...])
                field[pl.ds(cluster, 1), :] -= product[:1]
                return carry

            lax.fori_loop(KEPT, count, one, 0)

        remaining = field[...]

    right_side = remaining.astype(jnp.bfloat16)
    solved = jnp.zeros((clusters, unknowns), jnp.float32)
    for cluster in range(clusters):
        solved = jnp.where(which == cluster, dot_t(right_side, inverses[cluster]), solved)
    current[...] = solved
    out_copy = pltpu.make_async_copy(current, output.at[step], sems.at[4])
    out_copy.start()
    if not last:
        own = rows_of(padded(solved, halves * LANE), halves)
        rounded = solved.astype(jnp.bfloat16)
        which_dir = lax.broadcasted_iota(jnp.int32, (clusters, dir_rows * LANE), 0)
        ray_vals = jnp.zeros((clusters, dir_rows * LANE), jnp.float32)
        for cluster in range(clusters):
            ray_vals = jnp.where(which_dir == cluster, dot(rounded, rays[cluster]), ray_vals)
        newest = rows_of(jnp.sum(ray_vals * shift[...], axis=0, keepdims=True), dir_rows)
        spectrum[...] = newest
        for group in range(groups):
            far_sum = known[group] + fresh_weights[group] * newest
            message[group, :dir_rows, :] = jnp.where(is_near(group), own[:dir_rows], far_sum)
            message[group, dir_rows:, :] = own[dir_rows:]
    out_copy.wait()
    wait_all(kept_copies)


def exchange(block, axis, bit):
    count = lax.axis_size(axis)
    return lax.ppermute(block, axis, [(i, i ^ bit) for i in range(count)])


def local(
    incident,
    history,
    near_blocks,
    near_idx,
    near_cnt,
    near_lag,
    near_frac,
    inverses,
    rays,
    shift,
    far_idx,
    far_lag,
    trans,
):
    f32, i32, bf16 = jnp.float32, jnp.int32, jnp.bfloat16
    shaped = jax.ShapeDtypeStruct
    lags, clusters, unknowns = history.shape
    steps = incident.shape[0]
    slots = near_idx.shape[1]
    groups, entries, dirs = trans.shape
    dir_rows = dirs // LANE
    halves = pl.cdiv(unknowns, LANE)
    msg_rows = halves * clusters
    wide = halves * LANE
    near_entries = clusters * slots
    far_entries = groups * entries
    slab_count = lax.axis_size("slab")
    clus_count = lax.axis_size("clus")
    clus_index = lax.axis_index("clus")
    params = pltpu.CompilerParams(vmem_limit_bytes=VMEM_LIMIT)
    rays = jnp.swapaxes(rays, 1, 2)

    packed = pl.pallas_call(
        pack_kernel,
        out_shape=shaped((lags, msg_rows, LANE), f32),
        in_specs=[VMEM],
        out_specs=VMEM,
        compiler_params=params,
        name="pack_history",
    )(*in_hbm(history))
    pieces = [packed] + [exchange(packed, "clus", bit) for bit in range(1, clus_count)]
    stacked = jnp.stack(pieces, axis=0)
    mid = jnp.stack(
        [lax.dynamic_index_in_dim(stacked, clus_index ^ c, 0, False) for c in range(clus_count)],
        axis=1,
    )

    smem_lists = [
        pltpu.SMEM((clusters, slots), i32),
        pltpu.SMEM((clusters,), i32),
        pltpu.SMEM((clusters, slots), i32),
        pltpu.SMEM((clusters, slots), f32),
    ]
    dma = pltpu.SemaphoreType.DMA
    near_lists = in_hbm(near_idx, near_cnt, near_lag, near_frac)
    (blocks,) = in_hbm(near_blocks)
    spectra, message, weights, fresh_weights, kept, kept_weight, near_plan, old_plan = (
        pl.pallas_call(
            functools.partial(begin_kernel, clus_count),
            out_shape=(
                shaped((lags, dir_rows, LANE), f32),
                shaped((groups, msg_rows, LANE), f32),
                shaped((far_entries, dir_rows, LANE), f32),
                shaped((groups, dir_rows, LANE), f32),
                shaped((KEPT, unknowns, unknowns), bf16),
                shaped((near_entries, wide), f32),
                shaped((3 * near_entries + 4,), i32),
                shaped((3 * far_entries + 4,), i32),
            ),
            in_specs=[HBM] * 11,
            out_specs=[VMEM] * 6 + [SMEM] * 2,
            scratch_shapes=[
                pltpu.VMEM(rays.shape, bf16),
                pltpu.VMEM(history.shape, f32),
                pltpu.VMEM(shift.shape, f32),
                pltpu.VMEM(trans.shape, trans.dtype),
                pltpu.SMEM((entries, groups), i32),
                pltpu.SMEM((entries, groups), i32),
                *smem_lists,
                dma,
                dma((10,)),
            ],
            compiler_params=params,
            name="past_spectra",
        )(
            *in_hbm(rays, history, shift, trans, far_idx.T, far_lag.T),
            *near_lists,
            blocks,
        )
    )
    mid, message = lax.optimization_barrier((mid, message))
    mid = mid.reshape(lags, clus_count * msg_rows, LANE)
    core_swap = lax.ppermute(mid, "slab", [(i, i ^ 1) for i in range(slab_count)])
    chips = [(i, i + 1) for i in range(1, slab_count - 1, 2)]
    chip_swap = lax.ppermute(mid, "slab", chips + [(b, a) for a, b in chips])

    table_shape = (lags + steps, 3 * clus_count * msg_rows, LANE)
    tall_rows = -(-slots // PACK) * PACK
    newer = []
    for step in range(steps):
        last = step == steps - 1
        arrived = lax.all_to_all(message, ("slab", "clus"), 0, 0, tiled=True)
        arrived = arrived.reshape(groups * msg_rows, LANE)
        out_shape = [
            shaped((clusters, unknowns), f32),
            shaped((near_entries, wide), f32),
            shaped((groups, dir_rows, LANE), f32),
        ]
        currents_in = in_hbm(table) if step else in_hbm(mid, core_swap, chip_swap)
        results = pl.pallas_call(
            functools.partial(near_kernel, step, last, clus_count, lags),
            out_shape=out_shape if step else out_shape + [pltpu.HBM(table_shape, f32)],
            in_specs=[HBM] * 6 + [VMEM] * 2 + [HBM] + [VMEM] * step + [HBM] * len(currents_in),
            out_specs=[VMEM] * 3 + ([] if step else [HBM]),
            scratch_shapes=[
                pltpu.VMEM(table_shape, f32),
                pltpu.VMEM((near_entries, unknowns, unknowns), bf16),
                pltpu.VMEM((clusters, tall_rows, wide), f32),
                pltpu.VMEM((clusters, tall_rows, unknowns), f32),
                pltpu.VMEM((lags + steps, dir_rows, LANE), f32),
                pltpu.VMEM((clusters, unknowns), f32),
                *smem_lists,
                pltpu.SMEM(old_plan.shape, i32),
                dma((near_entries,)),
                dma((9,)),
                dma,
            ],
            compiler_params=params,
            cost_estimate=pl.CostEstimate(
                flops=2 * near_blocks.size, bytes_accessed=3 * near_blocks.size, transcendentals=0
            ),
            name=f"known_near_field_{step}",
        )(
            *near_lists,
            *in_hbm(old_plan, incident),
            *in_vmem(weights, spectra),
            blocks,
            *in_vmem(*newer),
            *currents_in,
        )
        base, blended, known = results[:3]
        if not step:
            table = results[3]
        out_shape = [pltpu.HBM(incident.shape, f32)]
        changed = []
        if step:
            changed.append(output)
        if step and not last:
            changed.append(table)
            out_shape.append(pltpu.HBM(table_shape, f32))
        whole = len(out_shape)
        if not last:
            out_shape += [shaped((dir_rows, LANE), f32), shaped(message.shape, f32)]
        results = pl.pallas_call(
            functools.partial(march_kernel, step, last, clus_count, slab_count, lags),
            out_shape=out_shape,
            in_specs=[HBM] + [VMEM] * 10 + [HBM] * (1 + len(changed)),
            out_specs=[HBM] * whole + [VMEM] * (len(out_shape) - whole),
            scratch_shapes=[
                pltpu.SMEM(near_plan.shape, i32),
                pltpu.VMEM((clusters, unknowns), f32),
                pltpu.VMEM((8, wide), f32),
                pltpu.VMEM((unknowns, unknowns), bf16),
                pltpu.VMEM((clusters, unknowns), f32),
                dma,
                dma((5,)),
            ],
            input_output_aliases={12 + number: number for number in range(len(changed))},
            compiler_params=params,
            name=f"march_{step}",
        )(
            *in_hbm(near_plan),
            *in_vmem(
                base, blended, known, kept, kept_weight, rays, inverses, shift, fresh_weights,
                arrived,
            ),
            blocks,
            *in_hbm(*changed),
        )
        output = results[0]
        if last:
            return output
        if step:
            table = results[1]
        spectrum, message = results[-2:]
        newer.append(spectrum)


def solution(mesh):
    both = ("slab", "clus")
    in_specs = (
        P(None, both, None),
        P(None, both, None),
        P(both, None, None, None),
        P(both, None),
        P(both),
        P(both, None),
        P(both, None),
        P(both, None, None),
        P(both, None, None),
        P(both, None),
        P(),
        P(),
        P(),
    )
    out_specs = P(None, both, None)
    return jax.shard_map(local, mesh=mesh, in_specs=in_specs, out_specs=out_specs, check_vma=False)
```

```python
import functools

import jax
import jax.numpy as jnp
from jax import lax
from jax.experimental import pallas as pl
from jax.experimental.pallas import tpu as pltpu
from jax.sharding import PartitionSpec as P

LANE = 128
PACK = 16
KEPT = 6
CHUNK = 3
VMEM_LIMIT = 24 * 1024 * 1024
HBM = pl.BlockSpec(memory_space=pltpu.HBM)
ANY = pl.BlockSpec(memory_space=pl.ANY)
VMEM = pl.BlockSpec(memory_space=pltpu.VMEM)
SMEM = pl.BlockSpec(memory_space=pltpu.SMEM)


def rows_of(wide, count):
    return jnp.concatenate([wide[:, r * LANE : (r + 1) * LANE] for r in range(count)], axis=0)


def padded(wide, width):
    return jnp.concatenate(
        [wide, jnp.zeros((wide.shape[0], width - wide.shape[1]), wide.dtype)], axis=1
    )


def dot(left, right):
    return jnp.dot(left, right, preferred_element_type=jnp.float32)


def dot_t(left, right):
    return lax.dot_general(
        left, right, (((1,), (1,)), ((), ())), preferred_element_type=jnp.float32
    )


def pack_kernel(history, packed):
    lags, clusters, unknowns = history.shape
    halves = packed.shape[1] // clusters
    for half in range(halves):
        low, high = half * LANE, min(unknowns, (half + 1) * LANE)
        part = history[:, :, low:high]
        if high - low < LANE:
            part = jnp.concatenate(
                [part, jnp.zeros((lags, clusters, LANE - (high - low)), jnp.float32)], axis=2
            )
        packed[:, half * clusters : (half + 1) * clusters, :] = part


def in_hbm(*arrays):
    return [pltpu.with_memory_space_constraint(array, pltpu.HBM) for array in arrays]


def in_vmem(*arrays):
    return [pltpu.with_memory_space_constraint(array, pltpu.VMEM) for array in arrays]


def start_all(pairs, sems):
    copies = []
    for number, (source, target) in enumerate(pairs):
        copy = pltpu.make_async_copy(source, target, sems.at[number])
        copy.start()
        copies.append(copy)
    return copies


def wait_all(copies):
    for copy in copies:
        copy.wait()


def any_of(flags):
    found = flags[0]
    for flag in flags[1:]:
        found = found | flag
    return found


def row_of(cluster_number, clusters, halves):
    place = lax.rem(cluster_number, clusters)
    return (cluster_number - place) * halves + place


def begin_kernel(
    clus_count,
    rays_in, history_in, shift_in, trans_in, far_idx_in, far_lag_in, near_idx_in, near_cnt_in,
    near_lag_in, near_frac_in, blocks,
    spectra, message, weights, fresh_weights, kept, kept_weight, kept_plan, near_plan, old_plan,
    rays, history, shift, trans, far_idx, far_lag, near_idx, near_cnt, near_lag, near_frac,
    far_list, sem, sems,
):
    small = start_all(
        (
            (far_idx_in, far_idx), (far_lag_in, far_lag), (trans_in, trans),
            (near_idx_in, near_idx), (near_cnt_in, near_cnt), (near_lag_in, near_lag),
            (near_frac_in, near_frac),
        ),
        sems,
    )
    large = start_all(
        ((history_in, history), (shift_in, shift), (rays_in, rays)), sems.at[pl.ds(7, 3)]
    )
    lags, clusters, unknowns = history.shape
    dir_rows = spectra.shape[1]
    entries, groups = far_idx.shape
    slots = near_idx.shape[1]
    halves = message.shape[1] // clusters
    myself = lax.axis_index("slab") * clus_count + lax.axis_index("clus")

    def kept_copy(place, entry):
        source = blocks.at[lax.div(entry, slots), lax.rem(entry, slots)]
        return pltpu.make_async_copy(source, kept.at[place], sem)

    for place in range(3 * KEPT + 1):
        near_plan[place] = 0
    kept_weight[...] = jnp.zeros(kept_weight.shape, jnp.float32)
    kept_plan[...] = jnp.zeros(kept_plan.shape, jnp.int32)
    lane = lax.broadcasted_iota(jnp.int32, (1, LANE), 1)
    message[...] = jnp.zeros(message.shape, jnp.float32)
    fresh_weights[...] = jnp.zeros(fresh_weights.shape, jnp.float32)
    wait_all(small)
    near_plan[0] = 0
    for cluster in range(clusters):
        fresh = [
            (slot < near_cnt[cluster]) & (near_lag[cluster, slot] == 1) for slot in range(slots)
        ]

        @pl.when(any_of(fresh))
        def _(cluster=cluster, fresh=fresh):
            for slot in range(slots):

                @pl.when(fresh[slot])
                def _(slot=slot):
                    count = near_plan[0]
                    entry = jnp.int32(cluster * slots + slot)
                    place = row_of(near_idx[cluster, slot], clusters, halves)
                    near_plan[3 * count + 1] = entry
                    near_plan[3 * count + 2] = jnp.int32(cluster)
                    near_plan[3 * count + 3] = place
                    row = jnp.zeros((1, kept_weight.shape[1]), jnp.float32)
                    kept_weight[pl.ds(count, 1), :] = row + (1.0 - near_frac[cluster, slot])
                    near_plan[0] = count + 1

                    @pl.when(count < KEPT)
                    def _():
                        kept_copy(count, entry).start()
                        fields = jnp.where(lane == 0, entry, jnp.where(lane == 1, cluster, place))
                        kept_plan[pl.ds(count, 1), :] = fields

    kept_plan[...] = jnp.where(
        lax.broadcasted_iota(jnp.int32, kept_plan.shape, 1) == 3, near_plan[0], kept_plan[...]
    )
    def one(group, counts):
        listed = [far_idx[column, group] == myself for column in range(entries)]

        def add(counts):
            place, old_count = counts
            for column in range(entries):
                lag = far_lag[column, group]

                @pl.when(listed[column])
                def _(place=place, lag=lag, column=column, old_count=old_count):
                    row = trans[group, column : column + 1, :].astype(jnp.float32)
                    weight = rows_of(row, dir_rows)
                    weights[place] = weight
                    far_list[2 * place] = group
                    far_list[2 * place + 1] = lag

                    @pl.when(lag == 1)
                    def _():
                        fresh_weights[group] += weight

                    @pl.when(lag > 1)
                    def _():
                        old_plan[3 * old_count + 1] = group
                        old_plan[3 * old_count + 2] = place
                        old_plan[3 * old_count + 3] = lag

                place = place + jnp.where(listed[column], 1, 0)
                old_count = old_count + jnp.where(listed[column] & (lag > 1), 1, 0)
            return place, old_count

        return lax.cond(any_of(listed), add, lambda counts: counts, counts)

    counts = lax.fori_loop(0, groups, one, (jnp.int32(0), jnp.int32(0)))
    old_plan[0] = counts[1]

    wait_all(large)
    total = jnp.zeros((lags, dir_rows * LANE), jnp.float32)
    for cluster in range(clusters):
        past = history[:, cluster, :].astype(jnp.bfloat16)
        total += dot(past, rays[cluster]) * shift[cluster : cluster + 1, :]
    for lag in range(lags):
        spectra[lag] = rows_of(total[lag : lag + 1], dir_rows)

    def add_past(place, carry):
        group, lag = far_list[2 * place], far_list[2 * place + 1]
        message[group, :dir_rows, :] += weights[place] * spectra[lags - lag]
        return carry

    lax.fori_loop(0, counts[0], add_past, 0)

    def finish(place, carry):
        kept_copy(place, near_plan[3 * place + 1]).wait()
        return carry

    lax.fori_loop(0, jnp.minimum(near_plan[0], KEPT), finish, 0)


def near_kernel(step, last, clus_count, lags, *refs):
    (
        near_idx_in, near_cnt_in, near_lag_in, near_frac_in, old_plan_in, incident_in, weights,
        past_spectra, blocks,
    ) = refs[:9]
    newer, refs = refs[9 : 9 + step], refs[9 + step :]
    if step:
        table_in, base, blended, known = refs[:4]
        refs = refs[4:]
    else:
        mid, core_swap, chip_swap, base, blended, known, table_out = refs[:7]
        refs = refs[7:]
    (
        table, held, tall, field, spectra, incident, near_idx, near_cnt, near_lag, near_frac,
        old_plan, sems, more_sems, out_sem,
    ) = refs
    clusters, slots = near_idx.shape
    unknowns = incident.shape[1]
    halves = tall.shape[2] // LANE
    side_rows = table.shape[1] // 3
    slab = lax.axis_index("slab")
    now = lags + max(step - 1, 0)
    chunks = [(first, min(CHUNK, slots - first)) for first in range(0, slots, CHUNK)]

    def block_copy(cluster, number):
        first, size = chunks[number]
        return pltpu.make_async_copy(
            blocks.at[cluster, pl.ds(first, size)],
            held.at[pl.ds(cluster * slots + first, size)],
            sems.at[cluster * len(chunks) + number],
        )

    if step:
        wide_pairs = [(table_in.at[pl.ds(0, now)], table.at[pl.ds(0, now)])]
    else:
        odd = lax.rem(slab, 2)
        wide_pairs = []
        for source, side in ((mid, 1), (core_swap, 2 - 2 * odd), (chip_swap, 2 * odd)):
            start = pl.multiple_of(side * side_rows, side_rows)
            wide_pairs.append((source, table.at[pl.ds(0, lags), pl.ds(start, side_rows)]))
    small = start_all(
        (
            (near_cnt_in, near_cnt), (near_idx_in, near_idx), (near_lag_in, near_lag),
            (near_frac_in, near_frac),
        ),
        more_sems,
    )
    wide = start_all(wide_pairs, more_sems.at[pl.ds(4, 3)])
    pairs = [(incident_in.at[step], incident)]
    if not last:
        pairs.append((old_plan_in, old_plan))
    others = start_all(pairs, more_sems.at[pl.ds(7, 2)])
    for cluster in range(clusters):
        block_copy(cluster, 0).start()
    tall[...] = jnp.zeros(tall.shape, jnp.float32)
    if not last:
        spectra[:lags] = past_spectra[...]
        for back, source in enumerate(newer):
            spectra[lags + back] = source[...]
        known[...] = jnp.zeros(known.shape, jnp.float32)
    wait_all(small)
    most = near_cnt[0]
    for cluster in range(1, clusters):
        most = jnp.maximum(most, near_cnt[cluster])
    for number in range(1, len(chunks)):
        for cluster in range(clusters):

            @pl.when(chunks[number][0] < near_cnt[cluster])
            def _():
                block_copy(cluster, number).start()

    wait_all(wide)
    if not step:
        keep = pltpu.make_async_copy(
            table.at[pl.ds(0, lags)], table_out.at[pl.ds(0, lags)], out_sem
        )
        keep.start()
    first_row = (slab - 1) * side_rows
    newest = lags + step - 2 if step else lags - 1
    for cluster in range(clusters):
        for slot in range(slots):
            row = row_of(near_idx[cluster, slot], clusters, halves) - first_row
            lag_slot = step - near_lag[cluster, slot] + lags
            frac = near_frac[cluster, slot]
            weight = jnp.where(lag_slot > newest, 0.0, 1.0 - frac)
            first_slot = jnp.minimum(lag_slot, newest)
            for half in range(halves):
                at = pl.ds(row + half * clusters, 1)
                tall[cluster, slot : slot + 1, half * LANE : (half + 1) * LANE] = (
                    weight * table[first_slot, at, :] + frac * table[lag_slot - 1, at, :]
                )
    for cluster in range(clusters):
        blended[cluster * slots : (cluster + 1) * slots, :] = tall[cluster, :slots, :]
    wait_all(others)
    if not last:

        def one(place, carry):
            before, total = carry
            group = old_plan[3 * place + 1]
            slot = step + 1 + lags - old_plan[3 * place + 3]
            term = weights[old_plan[3 * place + 2]] * spectra[slot]
            total = jnp.where(group == before, total, 0.0) + term
            known[group] = total
            return group, total

        lax.fori_loop(
            0, old_plan[0], one, (jnp.int32(-1), jnp.zeros(known.shape[1:], jnp.float32))
        )
    which = lax.broadcasted_iota(jnp.int32, (tall.shape[1], unknowns), 0)

    def part(number, cluster):
        first, size = chunks[number]
        values = tall[cluster].astype(jnp.bfloat16)[:, :unknowns]
        sums = jnp.zeros((tall.shape[1], unknowns), jnp.float32)
        for slot in range(first, first + size):
            counts = slot < near_cnt[cluster]
            if step:
                counts = counts & (near_lag[cluster, slot] > 1)
            product = dot_t(values, held[cluster * slots + slot])
            sums = jnp.where(which == jnp.where(counts, slot, -1), product, sums)
        return sums

    for cluster in range(clusters):
        block_copy(cluster, 0).wait()
    for cluster in range(clusters):
        field[cluster] = part(0, cluster)
    for number in range(1, len(chunks)):

        @pl.when(chunks[number][0] < most)
        def _():
            for cluster in range(clusters):

                @pl.when(chunks[number][0] < near_cnt[cluster])
                def _():
                    block_copy(cluster, number).wait()

            for cluster in range(clusters):
                field[cluster] += part(number, cluster)

    for cluster in range(clusters):
        total = jnp.sum(field[cluster], axis=0, keepdims=True)
        base[cluster : cluster + 1, :] = incident[cluster : cluster + 1, :] - total
    if not step:
        keep.wait()


def march_kernel(step, last, clus_count, slab_count, lags, *refs):
    (
        near_plan_in, kept_plan, base, blended, known, kept, kept_weight, rays, inverses, shift,
        fresh_weights, arrived, blocks,
    ) = refs[:13]
    if last:
        _, output = refs[13:15]
        refs = refs[15:]
    elif step:
        _, _, output, table, spectrum, message = refs[13:19]
        refs = refs[19:]
    else:
        output, spectrum, message = refs[13:16]
        refs = refs[16:]
    near_plan, current, values, extra, field, sem, sems = refs
    clusters, unknowns = base.shape
    slots = blocks.shape[1]
    groups, dir_rows = fresh_weights.shape[:2]
    rows_each = arrived.shape[0] // groups
    halves = rows_each // clusters
    side_rows = clus_count * rows_each
    slab = lax.axis_index("slab")
    which = lax.broadcasted_iota(jnp.int32, (clusters, unknowns), 0)
    kept_copies = []
    if step and not last:
        for side in range(3):
            other = jnp.clip(slab + (side - 1), 0, slab_count - 1)
            copy = pltpu.make_async_copy(
                arrived.at[pl.ds(pl.multiple_of(other * side_rows, side_rows), side_rows)],
                table.at[lags + step - 1, pl.ds(side * side_rows, side_rows)],
                sems.at[1 + side],
            )
            copy.start()
            kept_copies.append(copy)

    def is_near(group):
        return jnp.abs(group // clus_count - slab) <= 1

    sums = [jnp.zeros((dir_rows, LANE), jnp.float32) for _ in range(4)]
    for group in range(groups):
        first = group * rows_each
        sums[group % 4] += jnp.where(is_near(group), 0.0, arrived[first : first + dir_rows, :])
    incoming = (sums[0] + sums[1]) + (sums[2] + sums[3])
    row_in = jnp.concatenate([incoming[r : r + 1] for r in range(dir_rows)], axis=1)
    inbound = (shift[...] * row_in).astype(jnp.bfloat16)
    far = jnp.zeros((clusters, unknowns), jnp.float32)
    for cluster in range(clusters):
        far = jnp.where(which == cluster, dot_t(inbound, rays[cluster]), far)
    remaining = base[...] - far

    def fresh_row(place, entry, row):
        newest = jnp.concatenate(
            [arrived[pl.ds(row + half * clusters, 1), :] for half in range(halves)], axis=1
        )
        return blended[pl.ds(entry, 1), :] + kept_weight[pl.ds(place, 1), :] * newest

    if step:
        plan = kept_plan[...]
        count = plan[0, 3]
        values[...] = jnp.zeros(values.shape, jnp.float32)
        for place in range(KEPT):
            values[place : place + 1, :] = fresh_row(place, plan[place, 0], plan[place, 2])
        rows = values[...].astype(jnp.bfloat16)[:, :unknowns]
        for place in range(KEPT):
            product = dot_t(rows, kept[place])[place : place + 1]
            cluster = jnp.where(place < count, plan[place, 1], -1)
            remaining = remaining - jnp.where(which == cluster, product, 0.0)
        field[...] = remaining

        @pl.when(count > KEPT)
        def _():
            plan_copy = pltpu.make_async_copy(near_plan_in, near_plan, sems.at[0])
            plan_copy.start()
            plan_copy.wait()

            def one(place, carry):
                entry = near_plan[3 * place + 1]
                cluster = near_plan[3 * place + 2]
                source = blocks.at[cluster, entry - cluster * slots]
                copy = pltpu.make_async_copy(source, extra, sem)
                copy.start()
                row = fresh_row(place, entry, near_plan[3 * place + 3])
                row = jnp.broadcast_to(row, (8, halves * LANE))
                copy.wait()
                product = dot_t(row.astype(jnp.bfloat16)[:, :unknowns], extra[...])
                field[pl.ds(cluster, 1), :] -= product[:1]
                return carry

            lax.fori_loop(KEPT, count, one, 0)

        remaining = field[...]

    right_side = remaining.astype(jnp.bfloat16)
    solved = jnp.zeros((clusters, unknowns), jnp.float32)
    for cluster in range(clusters):
        solved = jnp.where(which == cluster, dot_t(right_side, inverses[cluster]), solved)
    current[...] = solved
    out_copy = pltpu.make_async_copy(current, output.at[step], sems.at[4])
    out_copy.start()
    if not last:
        own = rows_of(padded(solved, halves * LANE), halves)
        rounded = solved.astype(jnp.bfloat16)
        which_dir = lax.broadcasted_iota(jnp.int32, (clusters, dir_rows * LANE), 0)
        ray_vals = jnp.zeros((clusters, dir_rows * LANE), jnp.float32)
        for cluster in range(clusters):
            ray_vals = jnp.where(which_dir == cluster, dot(rounded, rays[cluster]), ray_vals)
        newest = rows_of(jnp.sum(ray_vals * shift[...], axis=0, keepdims=True), dir_rows)
        spectrum[...] = newest
        for group in range(groups):
            far_sum = known[group] + fresh_weights[group] * newest
            message[group, :dir_rows, :] = jnp.where(is_near(group), own[:dir_rows], far_sum)
            message[group, dir_rows:, :] = own[dir_rows:]
    out_copy.wait()
    wait_all(kept_copies)


def exchange(block, axis, bit):
    count = lax.axis_size(axis)
    return lax.ppermute(block, axis, [(i, i ^ bit) for i in range(count)])


def local(
    incident,
    history,
    near_blocks,
    near_idx,
    near_cnt,
    near_lag,
    near_frac,
    inverses,
    rays,
    shift,
    far_idx,
    far_lag,
    trans,
):
    f32, i32, bf16 = jnp.float32, jnp.int32, jnp.bfloat16
    shaped = jax.ShapeDtypeStruct
    lags, clusters, unknowns = history.shape
    steps = incident.shape[0]
    slots = near_idx.shape[1]
    groups, entries, dirs = trans.shape
    dir_rows = dirs // LANE
    halves = pl.cdiv(unknowns, LANE)
    msg_rows = halves * clusters
    wide = halves * LANE
    near_entries = clusters * slots
    far_entries = groups * entries
    slab_count = lax.axis_size("slab")
    clus_count = lax.axis_size("clus")
    clus_index = lax.axis_index("clus")
    params = pltpu.CompilerParams(vmem_limit_bytes=VMEM_LIMIT)
    rays = jnp.swapaxes(rays, 1, 2)

    packed = pl.pallas_call(
        pack_kernel,
        out_shape=shaped((lags, msg_rows, LANE), f32),
        in_specs=[VMEM],
        out_specs=VMEM,
        compiler_params=params,
        name="pack_history",
    )(*in_hbm(history))
    pieces = [packed] + [exchange(packed, "clus", bit) for bit in range(1, clus_count)]
    stacked = jnp.stack(pieces, axis=0)
    mid = jnp.stack(
        [lax.dynamic_index_in_dim(stacked, clus_index ^ c, 0, False) for c in range(clus_count)],
        axis=1,
    )

    smem_lists = [
        pltpu.SMEM((clusters, slots), i32),
        pltpu.SMEM((clusters,), i32),
        pltpu.SMEM((clusters, slots), i32),
        pltpu.SMEM((clusters, slots), f32),
    ]
    dma = pltpu.SemaphoreType.DMA
    near_lists = in_hbm(near_idx, near_cnt, near_lag, near_frac)
    (blocks,) = in_hbm(near_blocks)
    spectra, message, weights, fresh_weights, kept, kept_weight, kept_plan, near_plan, old_plan = (
        pl.pallas_call(
            functools.partial(begin_kernel, clus_count),
            out_shape=(
                shaped((lags, dir_rows, LANE), f32),
                shaped((groups, msg_rows, LANE), f32),
                shaped((far_entries, dir_rows, LANE), f32),
                shaped((groups, dir_rows, LANE), f32),
                shaped((KEPT, unknowns, unknowns), bf16),
                shaped((near_entries, wide), f32),
                shaped((8, LANE), i32),
                pltpu.HBM((3 * near_entries + 4,), i32),
                pltpu.HBM((3 * far_entries + 4,), i32),
            ),
            in_specs=[HBM] * 11,
            out_specs=[VMEM] * 7 + [SMEM] * 2,
            scratch_shapes=[
                pltpu.VMEM(rays.shape, bf16),
                pltpu.VMEM(history.shape, f32),
                pltpu.VMEM(shift.shape, f32),
                pltpu.VMEM(trans.shape, trans.dtype),
                pltpu.SMEM((entries, groups), i32),
                pltpu.SMEM((entries, groups), i32),
                *smem_lists,
                pltpu.SMEM((2 * far_entries + 2,), i32),
                dma,
                dma((10,)),
            ],
            compiler_params=params,
            name="past_spectra",
        )(
            *in_hbm(rays, history, shift, trans, far_idx.T, far_lag.T),
            *near_lists,
            blocks,
        )
    )
    mid, message = lax.optimization_barrier((mid, message))
    mid = mid.reshape(lags, clus_count * msg_rows, LANE)
    core_swap = lax.ppermute(mid, "slab", [(i, i ^ 1) for i in range(slab_count)])
    chips = [(i, i + 1) for i in range(1, slab_count - 1, 2)]
    chip_swap = lax.ppermute(mid, "slab", chips + [(b, a) for a, b in chips])

    table_shape = (lags + steps, 3 * clus_count * msg_rows, LANE)
    tall_rows = -(-slots // PACK) * PACK
    newer = []
    for step in range(steps):
        last = step == steps - 1
        arrived = lax.all_to_all(message, ("slab", "clus"), 0, 0, tiled=True)
        arrived = arrived.reshape(groups * msg_rows, LANE)
        out_shape = [
            shaped((clusters, unknowns), f32),
            shaped((near_entries, wide), f32),
            shaped((groups, dir_rows, LANE), f32),
        ]
        currents_in = in_hbm(table) if step else in_hbm(mid, core_swap, chip_swap)
        results = pl.pallas_call(
            functools.partial(near_kernel, step, last, clus_count, lags),
            out_shape=out_shape if step else out_shape + [pltpu.HBM(table_shape, f32)],
            in_specs=[HBM] * 6 + [VMEM] * 2 + [HBM] + [VMEM] * step + [HBM] * len(currents_in),
            out_specs=[VMEM] * 3 + ([] if step else [HBM]),
            scratch_shapes=[
                pltpu.VMEM(table_shape, f32),
                pltpu.VMEM((near_entries, unknowns, unknowns), bf16),
                pltpu.VMEM((clusters, tall_rows, wide), f32),
                pltpu.VMEM((clusters, tall_rows, unknowns), f32),
                pltpu.VMEM((lags + steps, dir_rows, LANE), f32),
                pltpu.VMEM((clusters, unknowns), f32),
                *smem_lists,
                pltpu.SMEM(old_plan.shape, i32),
                dma((near_entries,)),
                dma((9,)),
                dma,
            ],
            compiler_params=params,
            cost_estimate=pl.CostEstimate(
                flops=2 * near_blocks.size, bytes_accessed=3 * near_blocks.size, transcendentals=0
            ),
            name=f"known_near_field_{step}",
        )(
            *near_lists,
            *in_hbm(old_plan, incident),
            *in_vmem(weights, spectra),
            blocks,
            *in_vmem(*newer),
            *currents_in,
        )
        base, blended, known = results[:3]
        if not step:
            table = results[3]
        out_shape = [pltpu.HBM(incident.shape, f32)]
        changed = []
        if step:
            changed.append(output)
        if step and not last:
            changed.append(table)
            out_shape.append(pltpu.HBM(table_shape, f32))
        whole = len(out_shape)
        if not last:
            out_shape += [shaped((dir_rows, LANE), f32), shaped(message.shape, f32)]
        results = pl.pallas_call(
            functools.partial(march_kernel, step, last, clus_count, slab_count, lags),
            out_shape=out_shape,
            in_specs=[HBM] + [VMEM] * 11 + [HBM] * (1 + len(changed)),
            out_specs=[HBM] * whole + [VMEM] * (len(out_shape) - whole),
            scratch_shapes=[
                pltpu.SMEM(near_plan.shape, i32),
                pltpu.VMEM((clusters, unknowns), f32),
                pltpu.VMEM((8, wide), f32),
                pltpu.VMEM((unknowns, unknowns), bf16),
                pltpu.VMEM((clusters, unknowns), f32),
                dma,
                dma((5,)),
            ],
            input_output_aliases={13 + number: number for number in range(len(changed))},
            compiler_params=params,
            name=f"march_{step}",
        )(
            *in_hbm(near_plan),
            *in_vmem(
                kept_plan, base, blended, known, kept, kept_weight, rays, inverses, shift,
                fresh_weights, arrived,
            ),
            blocks,
            *in_hbm(*changed),
        )
        output = results[0]
        if last:
            return output
        if step:
            table = results[1]
        spectrum, message = results[-2:]
        newer.append(spectrum)


def solution(mesh):
    both = ("slab", "clus")
    in_specs = (
        P(None, both, None),
        P(None, both, None),
        P(both, None, None, None),
        P(both, None),
        P(both),
        P(both, None),
        P(both, None),
        P(both, None, None),
        P(both, None, None),
        P(both, None),
        P(),
        P(),
        P(),
    )
    out_specs = P(None, both, None)
    return jax.shard_map(local, mesh=mesh, in_specs=in_specs, out_specs=out_specs, check_vma=False)
```

```python
import functools

import jax
import jax.numpy as jnp
from jax import lax
from jax.experimental import pallas as pl
from jax.experimental.pallas import tpu as pltpu
from jax.sharding import PartitionSpec as P

LANE = 128
PACK = 16
KEPT = 8
CHUNK = 3
VMEM_LIMIT = 24 * 1024 * 1024
HBM = pl.BlockSpec(memory_space=pltpu.HBM)
ANY = pl.BlockSpec(memory_space=pl.ANY)
VMEM = pl.BlockSpec(memory_space=pltpu.VMEM)
SMEM = pl.BlockSpec(memory_space=pltpu.SMEM)


def rows_of(wide, count):
    return jnp.concatenate([wide[:, r * LANE : (r + 1) * LANE] for r in range(count)], axis=0)


def padded(wide, width):
    return jnp.concatenate(
        [wide, jnp.zeros((wide.shape[0], width - wide.shape[1]), wide.dtype)], axis=1
    )


def dot(left, right):
    return jnp.dot(left, right, preferred_element_type=jnp.float32)


def dot_t(left, right):
    return lax.dot_general(
        left, right, (((1,), (1,)), ((), ())), preferred_element_type=jnp.float32
    )


def pack_kernel(history, packed):
    lags, clusters, unknowns = history.shape
    halves = packed.shape[1] // clusters
    for half in range(halves):
        low, high = half * LANE, min(unknowns, (half + 1) * LANE)
        part = history[:, :, low:high]
        if high - low < LANE:
            part = jnp.concatenate(
                [part, jnp.zeros((lags, clusters, LANE - (high - low)), jnp.float32)], axis=2
            )
        packed[:, half * clusters : (half + 1) * clusters, :] = part


def in_hbm(*arrays):
    return [pltpu.with_memory_space_constraint(array, pltpu.HBM) for array in arrays]


def in_vmem(*arrays):
    return [pltpu.with_memory_space_constraint(array, pltpu.VMEM) for array in arrays]


def start_all(pairs, sems):
    copies = []
    for number, (source, target) in enumerate(pairs):
        copy = pltpu.make_async_copy(source, target, sems.at[number])
        copy.start()
        copies.append(copy)
    return copies


def wait_all(copies):
    for copy in copies:
        copy.wait()


def any_of(flags):
    found = flags[0]
    for flag in flags[1:]:
        found = found | flag
    return found


def row_of(cluster_number, clusters, halves):
    place = lax.rem(cluster_number, clusters)
    return (cluster_number - place) * halves + place


def begin_kernel(
    clus_count,
    rays_in, history_in, shift_in, trans_in, far_idx_in, far_lag_in, near_idx_in, near_cnt_in,
    near_lag_in, near_frac_in, blocks,
    spectra, message, weights, fresh_weights, kept, kept_weight, kept_plan, near_plan, old_plan,
    rays, history, shift, trans, far_idx, far_lag, near_idx, near_cnt, near_lag, near_frac,
    far_list, sem, sems,
):
    small = start_all(
        (
            (far_idx_in, far_idx), (far_lag_in, far_lag), (trans_in, trans),
            (near_idx_in, near_idx), (near_cnt_in, near_cnt), (near_lag_in, near_lag),
            (near_frac_in, near_frac),
        ),
        sems,
    )
    large = start_all(
        ((history_in, history), (shift_in, shift), (rays_in, rays)), sems.at[pl.ds(7, 3)]
    )
    lags, clusters, unknowns = history.shape
    dir_rows = spectra.shape[1]
    entries, groups = far_idx.shape
    slots = near_idx.shape[1]
    halves = message.shape[1] // clusters
    myself = lax.axis_index("slab") * clus_count + lax.axis_index("clus")

    def kept_copy(place, entry):
        source = blocks.at[lax.div(entry, slots), lax.rem(entry, slots)]
        return pltpu.make_async_copy(source, kept.at[place], sem)

    for place in range(3 * KEPT + 1):
        near_plan[place] = 0
    kept_weight[...] = jnp.zeros(kept_weight.shape, jnp.float32)
    kept_plan[...] = jnp.zeros(kept_plan.shape, jnp.int32)
    lane = lax.broadcasted_iota(jnp.int32, (1, LANE), 1)
    message[...] = jnp.zeros(message.shape, jnp.float32)
    fresh_weights[...] = jnp.zeros(fresh_weights.shape, jnp.float32)
    wait_all(small)
    near_plan[0] = 0
    for cluster in range(clusters):
        fresh = [
            (slot < near_cnt[cluster]) & (near_lag[cluster, slot] == 1) for slot in range(slots)
        ]

        @pl.when(any_of(fresh))
        def _(cluster=cluster, fresh=fresh):
            for slot in range(slots):

                @pl.when(fresh[slot])
                def _(slot=slot):
                    count = near_plan[0]
                    entry = jnp.int32(cluster * slots + slot)
                    place = row_of(near_idx[cluster, slot], clusters, halves)
                    near_plan[3 * count + 1] = entry
                    near_plan[3 * count + 2] = jnp.int32(cluster)
                    near_plan[3 * count + 3] = place
                    row = jnp.zeros((1, kept_weight.shape[1]), jnp.float32)
                    kept_weight[pl.ds(count, 1), :] = row + (1.0 - near_frac[cluster, slot])
                    near_plan[0] = count + 1

                    @pl.when(count < KEPT)
                    def _():
                        kept_copy(count, entry).start()
                        fields = jnp.where(lane == 0, entry, jnp.where(lane == 1, cluster, place))
                        kept_plan[pl.ds(count, 1), :] = fields

    kept_plan[...] = jnp.where(
        lax.broadcasted_iota(jnp.int32, kept_plan.shape, 1) == 3, near_plan[0], kept_plan[...]
    )
    def one(group, counts):
        listed = [far_idx[column, group] == myself for column in range(entries)]

        def add(counts):
            place, old_count = counts
            for column in range(entries):
                lag = far_lag[column, group]

                @pl.when(listed[column])
                def _(place=place, lag=lag, column=column, old_count=old_count):
                    row = trans[group, column : column + 1, :].astype(jnp.float32)
                    weight = rows_of(row, dir_rows)
                    weights[place] = weight
                    far_list[2 * place] = group
                    far_list[2 * place + 1] = lag

                    @pl.when(lag == 1)
                    def _():
                        fresh_weights[group] += weight

                    @pl.when(lag > 1)
                    def _():
                        old_plan[3 * old_count + 1] = group
                        old_plan[3 * old_count + 2] = place
                        old_plan[3 * old_count + 3] = lag

                place = place + jnp.where(listed[column], 1, 0)
                old_count = old_count + jnp.where(listed[column] & (lag > 1), 1, 0)
            return place, old_count

        return lax.cond(any_of(listed), add, lambda counts: counts, counts)

    counts = lax.fori_loop(0, groups, one, (jnp.int32(0), jnp.int32(0)))
    old_plan[0] = counts[1]

    wait_all(large)
    total = jnp.zeros((lags, dir_rows * LANE), jnp.float32)
    for cluster in range(clusters):
        past = history[:, cluster, :].astype(jnp.bfloat16)
        total += dot(past, rays[cluster]) * shift[cluster : cluster + 1, :]
    for lag in range(lags):
        spectra[lag] = rows_of(total[lag : lag + 1], dir_rows)

    def add_past(place, carry):
        group, lag = far_list[2 * place], far_list[2 * place + 1]
        message[group, :dir_rows, :] += weights[place] * spectra[lags - lag]
        return carry

    lax.fori_loop(0, counts[0], add_past, 0)

    def finish(place, carry):
        kept_copy(place, near_plan[3 * place + 1]).wait()
        return carry

    lax.fori_loop(0, jnp.minimum(near_plan[0], KEPT), finish, 0)


def near_kernel(step, last, clus_count, lags, *refs):
    (
        near_idx_in, near_cnt_in, near_lag_in, near_frac_in, old_plan_in, incident_in, weights,
        past_spectra, blocks,
    ) = refs[:9]
    newer, refs = refs[9 : 9 + step], refs[9 + step :]
    if step:
        table_in, base, blended, known = refs[:4]
        refs = refs[4:]
    else:
        mid, core_swap, chip_swap, base, blended, known, table_out = refs[:7]
        refs = refs[7:]
    (
        table, held, tall, field, spectra, incident, near_idx, near_cnt, near_lag, near_frac,
        old_plan, sems, more_sems, out_sem,
    ) = refs
    clusters, slots = near_idx.shape
    unknowns = incident.shape[1]
    halves = tall.shape[2] // LANE
    side_rows = table.shape[1] // 3
    slab = lax.axis_index("slab")
    now = lags + max(step - 1, 0)
    chunks = [(first, min(CHUNK, slots - first)) for first in range(0, slots, CHUNK)]

    def block_copy(cluster, number):
        first, size = chunks[number]
        return pltpu.make_async_copy(
            blocks.at[cluster, pl.ds(first, size)],
            held.at[pl.ds(cluster * slots + first, size)],
            sems.at[cluster * len(chunks) + number],
        )

    if step:
        wide_pairs = [(table_in.at[pl.ds(0, now)], table.at[pl.ds(0, now)])]
    else:
        odd = lax.rem(slab, 2)
        wide_pairs = []
        for source, side in ((mid, 1), (core_swap, 2 - 2 * odd), (chip_swap, 2 * odd)):
            start = pl.multiple_of(side * side_rows, side_rows)
            wide_pairs.append((source, table.at[pl.ds(0, lags), pl.ds(start, side_rows)]))
    small = start_all(
        (
            (near_cnt_in, near_cnt), (near_idx_in, near_idx), (near_lag_in, near_lag),
            (near_frac_in, near_frac),
        ),
        more_sems,
    )
    wide = start_all(wide_pairs, more_sems.at[pl.ds(4, 3)])
    pairs = [(incident_in.at[step], incident)]
    if not last:
        pairs.append((old_plan_in, old_plan))
    others = start_all(pairs, more_sems.at[pl.ds(7, 2)])
    for cluster in range(clusters):
        block_copy(cluster, 0).start()
    tall[...] = jnp.zeros(tall.shape, jnp.float32)
    if not last:
        spectra[:lags] = past_spectra[...]
        for back, source in enumerate(newer):
            spectra[lags + back] = source[...]
        known[...] = jnp.zeros(known.shape, jnp.float32)
    wait_all(small)
    most = near_cnt[0]
    for cluster in range(1, clusters):
        most = jnp.maximum(most, near_cnt[cluster])
    for number in range(1, len(chunks)):
        for cluster in range(clusters):

            @pl.when(chunks[number][0] < near_cnt[cluster])
            def _():
                block_copy(cluster, number).start()

    wait_all(wide)
    if not step:
        keep = pltpu.make_async_copy(
            table.at[pl.ds(0, lags)], table_out.at[pl.ds(0, lags)], out_sem
        )
        keep.start()
    first_row = (slab - 1) * side_rows
    newest = lags + step - 2 if step else lags - 1
    for cluster in range(clusters):
        for slot in range(slots):
            row = row_of(near_idx[cluster, slot], clusters, halves) - first_row
            lag_slot = step - near_lag[cluster, slot] + lags
            frac = near_frac[cluster, slot]
            weight = jnp.where(lag_slot > newest, 0.0, 1.0 - frac)
            first_slot = jnp.minimum(lag_slot, newest)
            for half in range(halves):
                at = pl.ds(row + half * clusters, 1)
                tall[cluster, slot : slot + 1, half * LANE : (half + 1) * LANE] = (
                    weight * table[first_slot, at, :] + frac * table[lag_slot - 1, at, :]
                )
    for cluster in range(clusters):
        blended[cluster * slots : (cluster + 1) * slots, :] = tall[cluster, :slots, :]
    wait_all(others)
    if not last:

        def one(place, carry):
            before, total = carry
            group = old_plan[3 * place + 1]
            slot = step + 1 + lags - old_plan[3 * place + 3]
            term = weights[old_plan[3 * place + 2]] * spectra[slot]
            total = jnp.where(group == before, total, 0.0) + term
            known[group] = total
            return group, total

        lax.fori_loop(
            0, old_plan[0], one, (jnp.int32(-1), jnp.zeros(known.shape[1:], jnp.float32))
        )
    which = lax.broadcasted_iota(jnp.int32, (tall.shape[1], unknowns), 0)

    def part(number, cluster):
        first, size = chunks[number]
        values = tall[cluster].astype(jnp.bfloat16)[:, :unknowns]
        sums = jnp.zeros((tall.shape[1], unknowns), jnp.float32)
        for slot in range(first, first + size):
            counts = slot < near_cnt[cluster]
            if step:
                counts = counts & (near_lag[cluster, slot] > 1)
            product = dot_t(values, held[cluster * slots + slot])
            sums = jnp.where(which == jnp.where(counts, slot, -1), product, sums)
        return sums

    for cluster in range(clusters):
        block_copy(cluster, 0).wait()
    for cluster in range(clusters):
        field[cluster] = part(0, cluster)
    for number in range(1, len(chunks)):

        @pl.when(chunks[number][0] < most)
        def _():
            for cluster in range(clusters):

                @pl.when(chunks[number][0] < near_cnt[cluster])
                def _():
                    block_copy(cluster, number).wait()

            for cluster in range(clusters):
                field[cluster] += part(number, cluster)

    for cluster in range(clusters):
        total = jnp.sum(field[cluster], axis=0, keepdims=True)
        base[cluster : cluster + 1, :] = incident[cluster : cluster + 1, :] - total
    if not step:
        keep.wait()


def march_kernel(step, last, clus_count, slab_count, lags, *refs):
    (
        near_plan_in, kept_plan, base, blended, known, kept, kept_weight, rays, inverses, shift,
        fresh_weights, arrived, blocks,
    ) = refs[:13]
    if last:
        _, output = refs[13:15]
        refs = refs[15:]
    elif step:
        _, _, output, table, spectrum, message = refs[13:19]
        refs = refs[19:]
    else:
        output, spectrum, message = refs[13:16]
        refs = refs[16:]
    near_plan, current, values, extra, field, sem, sems = refs
    clusters, unknowns = base.shape
    slots = blocks.shape[1]
    groups, dir_rows = fresh_weights.shape[:2]
    rows_each = arrived.shape[0] // groups
    halves = rows_each // clusters
    side_rows = clus_count * rows_each
    slab = lax.axis_index("slab")
    which = lax.broadcasted_iota(jnp.int32, (clusters, unknowns), 0)
    kept_copies = []
    if step and not last:
        for side in range(3):
            other = jnp.clip(slab + (side - 1), 0, slab_count - 1)
            copy = pltpu.make_async_copy(
                arrived.at[pl.ds(pl.multiple_of(other * side_rows, side_rows), side_rows)],
                table.at[lags + step - 1, pl.ds(side * side_rows, side_rows)],
                sems.at[1 + side],
            )
            copy.start()
            kept_copies.append(copy)

    def is_near(group):
        return jnp.abs(group // clus_count - slab) <= 1

    sums = [jnp.zeros((dir_rows, LANE), jnp.float32) for _ in range(4)]
    for group in range(groups):
        first = group * rows_each
        sums[group % 4] += jnp.where(is_near(group), 0.0, arrived[first : first + dir_rows, :])
    incoming = (sums[0] + sums[1]) + (sums[2] + sums[3])
    row_in = jnp.concatenate([incoming[r : r + 1] for r in range(dir_rows)], axis=1)
    inbound = (shift[...] * row_in).astype(jnp.bfloat16)
    far = jnp.zeros((clusters, unknowns), jnp.float32)
    for cluster in range(clusters):
        far = jnp.where(which == cluster, dot_t(inbound, rays[cluster]), far)
    remaining = base[...] - far

    def fresh_row(place, entry, row):
        newest = jnp.concatenate(
            [arrived[pl.ds(row + half * clusters, 1), :] for half in range(halves)], axis=1
        )
        return blended[pl.ds(entry, 1), :] + kept_weight[pl.ds(place, 1), :] * newest

    if step:
        plan = kept_plan[...]
        count = plan[0, 3]
        values[...] = jnp.zeros(values.shape, jnp.float32)
        for place in range(KEPT):
            values[place : place + 1, :] = fresh_row(place, plan[place, 0], plan[place, 2])
        rows = values[...].astype(jnp.bfloat16)[:, :unknowns]
        for place in range(KEPT):
            product = dot_t(rows, kept[place])[place : place + 1]
            cluster = jnp.where(place < count, plan[place, 1], -1)
            remaining = remaining - jnp.where(which == cluster, product, 0.0)
        field[...] = remaining

        @pl.when(count > KEPT)
        def _():
            plan_copy = pltpu.make_async_copy(near_plan_in, near_plan, sems.at[0])
            plan_copy.start()
            plan_copy.wait()

            def one(place, carry):
                entry = near_plan[3 * place + 1]
                cluster = near_plan[3 * place + 2]
                source = blocks.at[cluster, entry - cluster * slots]
                copy = pltpu.make_async_copy(source, extra, sem)
                copy.start()
                row = fresh_row(place, entry, near_plan[3 * place + 3])
                row = jnp.broadcast_to(row, (8, halves * LANE))
                copy.wait()
                product = dot_t(row.astype(jnp.bfloat16)[:, :unknowns], extra[...])
                field[pl.ds(cluster, 1), :] -= product[:1]
                return carry

            lax.fori_loop(KEPT, count, one, 0)

        remaining = field[...]

    right_side = remaining.astype(jnp.bfloat16)
    solved = jnp.zeros((clusters, unknowns), jnp.float32)
    for cluster in range(clusters):
        solved = jnp.where(which == cluster, dot_t(right_side, inverses[cluster]), solved)
    current[...] = solved
    out_copy = pltpu.make_async_copy(current, output.at[step], sems.at[4])
    out_copy.start()
    if not last:
        own = rows_of(padded(solved, halves * LANE), halves)
        rounded = solved.astype(jnp.bfloat16)
        which_dir = lax.broadcasted_iota(jnp.int32, (clusters, dir_rows * LANE), 0)
        ray_vals = jnp.zeros((clusters, dir_rows * LANE), jnp.float32)
        for cluster in range(clusters):
            ray_vals = jnp.where(which_dir == cluster, dot(rounded, rays[cluster]), ray_vals)
        newest = rows_of(jnp.sum(ray_vals * shift[...], axis=0, keepdims=True), dir_rows)
        spectrum[...] = newest
        for group in range(groups):
            far_sum = known[group] + fresh_weights[group] * newest
            message[group, :dir_rows, :] = jnp.where(is_near(group), own[:dir_rows], far_sum)
            message[group, dir_rows:, :] = own[dir_rows:]
    out_copy.wait()
    wait_all(kept_copies)


def exchange(block, axis, bit):
    count = lax.axis_size(axis)
    return lax.ppermute(block, axis, [(i, i ^ bit) for i in range(count)])


def local(
    incident,
    history,
    near_blocks,
    near_idx,
    near_cnt,
    near_lag,
    near_frac,
    inverses,
    rays,
    shift,
    far_idx,
    far_lag,
    trans,
):
    f32, i32, bf16 = jnp.float32, jnp.int32, jnp.bfloat16
    shaped = jax.ShapeDtypeStruct
    lags, clusters, unknowns = history.shape
    steps = incident.shape[0]
    slots = near_idx.shape[1]
    groups, entries, dirs = trans.shape
    dir_rows = dirs // LANE
    halves = pl.cdiv(unknowns, LANE)
    msg_rows = halves * clusters
    wide = halves * LANE
    near_entries = clusters * slots
    far_entries = groups * entries
    slab_count = lax.axis_size("slab")
    clus_count = lax.axis_size("clus")
    clus_index = lax.axis_index("clus")
    params = pltpu.CompilerParams(vmem_limit_bytes=VMEM_LIMIT)
    rays = jnp.swapaxes(rays, 1, 2)

    packed = pl.pallas_call(
        pack_kernel,
        out_shape=shaped((lags, msg_rows, LANE), f32),
        in_specs=[VMEM],
        out_specs=VMEM,
        compiler_params=params,
        name="pack_history",
    )(*in_hbm(history))
    pieces = [packed] + [exchange(packed, "clus", bit) for bit in range(1, clus_count)]
    stacked = jnp.stack(pieces, axis=0)
    mid = jnp.stack(
        [lax.dynamic_index_in_dim(stacked, clus_index ^ c, 0, False) for c in range(clus_count)],
        axis=1,
    )

    smem_lists = [
        pltpu.SMEM((clusters, slots), i32),
        pltpu.SMEM((clusters,), i32),
        pltpu.SMEM((clusters, slots), i32),
        pltpu.SMEM((clusters, slots), f32),
    ]
    dma = pltpu.SemaphoreType.DMA
    near_lists = in_hbm(near_idx, near_cnt, near_lag, near_frac)
    (blocks,) = in_hbm(near_blocks)
    spectra, message, weights, fresh_weights, kept, kept_weight, kept_plan, near_plan, old_plan = (
        pl.pallas_call(
            functools.partial(begin_kernel, clus_count),
            out_shape=(
                shaped((lags, dir_rows, LANE), f32),
                shaped((groups, msg_rows, LANE), f32),
                shaped((far_entries, dir_rows, LANE), f32),
                shaped((groups, dir_rows, LANE), f32),
                shaped((KEPT, unknowns, unknowns), bf16),
                shaped((near_entries, wide), f32),
                shaped((8, LANE), i32),
                pltpu.HBM((3 * near_entries + 4,), i32),
                pltpu.HBM((3 * far_entries + 4,), i32),
            ),
            in_specs=[HBM] * 11,
            out_specs=[VMEM] * 7 + [SMEM] * 2,
            scratch_shapes=[
                pltpu.VMEM(rays.shape, bf16),
                pltpu.VMEM(history.shape, f32),
                pltpu.VMEM(shift.shape, f32),
                pltpu.VMEM(trans.shape, trans.dtype),
                pltpu.SMEM((entries, groups), i32),
                pltpu.SMEM((entries, groups), i32),
                *smem_lists,
                pltpu.SMEM((2 * far_entries + 2,), i32),
                dma,
                dma((10,)),
            ],
            compiler_params=params,
            name="past_spectra",
        )(
            *in_hbm(rays, history, shift, trans, far_idx.T, far_lag.T),
            *near_lists,
            blocks,
        )
    )
    mid, message = lax.optimization_barrier((mid, message))
    mid = mid.reshape(lags, clus_count * msg_rows, LANE)
    core_swap = lax.ppermute(mid, "slab", [(i, i ^ 1) for i in range(slab_count)])
    chips = [(i, i + 1) for i in range(1, slab_count - 1, 2)]
    chip_swap = lax.ppermute(mid, "slab", chips + [(b, a) for a, b in chips])

    table_shape = (lags + steps, 3 * clus_count * msg_rows, LANE)
    tall_rows = -(-slots // PACK) * PACK
    newer = []
    for step in range(steps):
        last = step == steps - 1
        arrived = lax.all_to_all(message, ("slab", "clus"), 0, 0, tiled=True)
        arrived = arrived.reshape(groups * msg_rows, LANE)
        out_shape = [
            shaped((clusters, unknowns), f32),
            shaped((near_entries, wide), f32),
            shaped((groups, dir_rows, LANE), f32),
        ]
        currents_in = in_hbm(table) if step else in_hbm(mid, core_swap, chip_swap)
        results = pl.pallas_call(
            functools.partial(near_kernel, step, last, clus_count, lags),
            out_shape=out_shape if step else out_shape + [pltpu.HBM(table_shape, f32)],
            in_specs=[HBM] * 6 + [VMEM] * 2 + [HBM] + [VMEM] * step + [HBM] * len(currents_in),
            out_specs=[VMEM] * 3 + ([] if step else [HBM]),
            scratch_shapes=[
                pltpu.VMEM(table_shape, f32),
                pltpu.VMEM((near_entries, unknowns, unknowns), bf16),
                pltpu.VMEM((clusters, tall_rows, wide), f32),
                pltpu.VMEM((clusters, tall_rows, unknowns), f32),
                pltpu.VMEM((lags + steps, dir_rows, LANE), f32),
                pltpu.VMEM((clusters, unknowns), f32),
                *smem_lists,
                pltpu.SMEM(old_plan.shape, i32),
                dma((near_entries,)),
                dma((9,)),
                dma,
            ],
            compiler_params=params,
            cost_estimate=pl.CostEstimate(
                flops=2 * near_blocks.size, bytes_accessed=3 * near_blocks.size, transcendentals=0
            ),
            name=f"known_near_field_{step}",
        )(
            *near_lists,
            *in_hbm(old_plan, incident),
            *in_vmem(weights, spectra),
            blocks,
            *in_vmem(*newer),
            *currents_in,
        )
        base, blended, known = results[:3]
        if not step:
            table = results[3]
        out_shape = [pltpu.HBM(incident.shape, f32)]
        changed = []
        if step:
            changed.append(output)
        if step and not last:
            changed.append(table)
            out_shape.append(pltpu.HBM(table_shape, f32))
        whole = len(out_shape)
        if not last:
            out_shape += [shaped((dir_rows, LANE), f32), pltpu.VMEM(message.shape, f32)]
        results = pl.pallas_call(
            functools.partial(march_kernel, step, last, clus_count, slab_count, lags),
            out_shape=out_shape,
            in_specs=[HBM] + [VMEM] * 11 + [HBM] * (1 + len(changed)),
            out_specs=[HBM] * whole + [VMEM] * (len(out_shape) - whole),
            scratch_shapes=[
                pltpu.SMEM(near_plan.shape, i32),
                pltpu.VMEM((clusters, unknowns), f32),
                pltpu.VMEM((8, wide), f32),
                pltpu.VMEM((unknowns, unknowns), bf16),
                pltpu.VMEM((clusters, unknowns), f32),
                dma,
                dma((5,)),
            ],
            input_output_aliases={13 + number: number for number in range(len(changed))},
            compiler_params=params,
            name=f"march_{step}",
        )(
            *in_hbm(near_plan),
            *in_vmem(
                kept_plan, base, blended, known, kept, kept_weight, rays, inverses, shift,
                fresh_weights, arrived,
            ),
            blocks,
            *in_hbm(*changed),
        )
        output = results[0]
        if last:
            return output
        if step:
            table = results[1]
        spectrum, message = results[-2:]
        newer.append(spectrum)


def solution(mesh):
    both = ("slab", "clus")
    in_specs = (
        P(None, both, None),
        P(None, both, None),
        P(both, None, None, None),
        P(both, None),
        P(both),
        P(both, None),
        P(both, None),
        P(both, None, None),
        P(both, None, None),
        P(both, None),
        P(),
        P(),
        P(),
    )
    out_specs = P(None, both, None)
    return jax.shard_map(local, mesh=mesh, in_specs=in_specs, out_specs=out_specs, check_vma=False)
```

```python
import functools

import jax
import jax.numpy as jnp
from jax import lax
from jax.experimental import pallas as pl
from jax.experimental.pallas import tpu as pltpu
from jax.sharding import PartitionSpec as P

LANE = 128
PACK = 16
KEPT = 8
CHUNK = 3
VMEM_LIMIT = 24 * 1024 * 1024
HBM = pl.BlockSpec(memory_space=pltpu.HBM)
ANY = pl.BlockSpec(memory_space=pl.ANY)
VMEM = pl.BlockSpec(memory_space=pltpu.VMEM)
SMEM = pl.BlockSpec(memory_space=pltpu.SMEM)


def rows_of(wide, count):
    return jnp.concatenate([wide[:, r * LANE : (r + 1) * LANE] for r in range(count)], axis=0)


def padded(wide, width):
    return jnp.concatenate(
        [wide, jnp.zeros((wide.shape[0], width - wide.shape[1]), wide.dtype)], axis=1
    )


def dot(left, right):
    return jnp.dot(left, right, preferred_element_type=jnp.float32)


def dot_t(left, right):
    return lax.dot_general(
        left, right, (((1,), (1,)), ((), ())), preferred_element_type=jnp.float32
    )


def pack_kernel(history, copies_out, packed, sems):
    lags, clusters, unknowns = history.shape
    halves = packed.shape[1] // clusters
    for half in range(halves):
        low, high = half * LANE, min(unknowns, (half + 1) * LANE)
        part = history[:, :, low:high]
        if high - low < LANE:
            part = jnp.concatenate(
                [part, jnp.zeros((lags, clusters, LANE - (high - low)), jnp.float32)], axis=2
            )
        packed[:, half * clusters : (half + 1) * clusters, :] = part
    peers = copies_out.shape[0]
    wait_all(start_all([(packed, copies_out.at[peer]) for peer in range(peers)], sems))


def in_hbm(*arrays):
    return [pltpu.with_memory_space_constraint(array, pltpu.HBM) for array in arrays]


def in_vmem(*arrays):
    return [pltpu.with_memory_space_constraint(array, pltpu.VMEM) for array in arrays]


def start_all(pairs, sems):
    copies = []
    for number, (source, target) in enumerate(pairs):
        copy = pltpu.make_async_copy(source, target, sems.at[number])
        copy.start()
        copies.append(copy)
    return copies


def wait_all(copies):
    for copy in copies:
        copy.wait()


def any_of(flags):
    found = flags[0]
    for flag in flags[1:]:
        found = found | flag
    return found


def row_of(cluster_number, clusters, halves):
    place = lax.rem(cluster_number, clusters)
    return (cluster_number - place) * halves + place


def begin_kernel(
    clus_count,
    rays_in, history_in, shift_in, trans_in, far_idx_in, far_lag_in, near_idx_in, near_cnt_in,
    near_lag_in, near_frac_in, blocks,
    spectra, message, weights, fresh_weights, kept, kept_weight, kept_plan, near_plan, old_plan,
    rays, history, shift, trans, far_idx, far_lag, near_idx, near_cnt, near_lag, near_frac,
    far_list, sem, sems,
):
    small = start_all(
        (
            (far_idx_in, far_idx), (far_lag_in, far_lag), (trans_in, trans),
            (near_idx_in, near_idx), (near_cnt_in, near_cnt), (near_lag_in, near_lag),
            (near_frac_in, near_frac),
        ),
        sems,
    )
    large = start_all(
        ((history_in, history), (shift_in, shift), (rays_in, rays)), sems.at[pl.ds(7, 3)]
    )
    lags, clusters, unknowns = history.shape
    dir_rows = spectra.shape[1]
    entries, groups = far_idx.shape
    slots = near_idx.shape[1]
    halves = message.shape[1] // clusters
    myself = lax.axis_index("slab") * clus_count + lax.axis_index("clus")

    def kept_copy(place, entry):
        source = blocks.at[lax.div(entry, slots), lax.rem(entry, slots)]
        return pltpu.make_async_copy(source, kept.at[place], sem)

    for place in range(3 * KEPT + 1):
        near_plan[place] = 0
    kept_weight[...] = jnp.zeros(kept_weight.shape, jnp.float32)
    kept_plan[...] = jnp.zeros(kept_plan.shape, jnp.int32)
    lane = lax.broadcasted_iota(jnp.int32, (1, LANE), 1)
    message[...] = jnp.zeros(message.shape, jnp.float32)
    fresh_weights[...] = jnp.zeros(fresh_weights.shape, jnp.float32)
    wait_all(small)
    near_plan[0] = 0
    for cluster in range(clusters):
        fresh = [
            (slot < near_cnt[cluster]) & (near_lag[cluster, slot] == 1) for slot in range(slots)
        ]

        @pl.when(any_of(fresh))
        def _(cluster=cluster, fresh=fresh):
            for slot in range(slots):

                @pl.when(fresh[slot])
                def _(slot=slot):
                    count = near_plan[0]
                    entry = jnp.int32(cluster * slots + slot)
                    place = row_of(near_idx[cluster, slot], clusters, halves)
                    near_plan[3 * count + 1] = entry
                    near_plan[3 * count + 2] = jnp.int32(cluster)
                    near_plan[3 * count + 3] = place
                    row = jnp.zeros((1, kept_weight.shape[1]), jnp.float32)
                    kept_weight[pl.ds(count, 1), :] = row + (1.0 - near_frac[cluster, slot])
                    near_plan[0] = count + 1

                    @pl.when(count < KEPT)
                    def _():
                        kept_copy(count, entry).start()
                        fields = jnp.where(lane == 0, entry, jnp.where(lane == 1, cluster, place))
                        kept_plan[pl.ds(count, 1), :] = fields

    kept_plan[...] = jnp.where(
        lax.broadcasted_iota(jnp.int32, kept_plan.shape, 1) == 3, near_plan[0], kept_plan[...]
    )
    def one(group, counts):
        listed = [far_idx[column, group] == myself for column in range(entries)]

        def add(counts):
            place, old_count = counts
            for column in range(entries):
                lag = far_lag[column, group]

                @pl.when(listed[column])
                def _(place=place, lag=lag, column=column, old_count=old_count):
                    row = trans[group, column : column + 1, :].astype(jnp.float32)
                    weight = rows_of(row, dir_rows)
                    weights[place] = weight
                    far_list[2 * place] = group
                    far_list[2 * place + 1] = lag

                    @pl.when(lag == 1)
                    def _():
                        fresh_weights[group] += weight

                    @pl.when(lag > 1)
                    def _():
                        old_plan[3 * old_count + 1] = group
                        old_plan[3 * old_count + 2] = place
                        old_plan[3 * old_count + 3] = lag

                place = place + jnp.where(listed[column], 1, 0)
                old_count = old_count + jnp.where(listed[column] & (lag > 1), 1, 0)
            return place, old_count

        return lax.cond(any_of(listed), add, lambda counts: counts, counts)

    counts = lax.fori_loop(0, groups, one, (jnp.int32(0), jnp.int32(0)))
    old_plan[0] = counts[1]

    wait_all(large)
    total = jnp.zeros((lags, dir_rows * LANE), jnp.float32)
    for cluster in range(clusters):
        past = history[:, cluster, :].astype(jnp.bfloat16)
        total += dot(past, rays[cluster]) * shift[cluster : cluster + 1, :]
    for lag in range(lags):
        spectra[lag] = rows_of(total[lag : lag + 1], dir_rows)

    def add_past(place, carry):
        group, lag = far_list[2 * place], far_list[2 * place + 1]
        message[group, :dir_rows, :] += weights[place] * spectra[lags - lag]
        return carry

    lax.fori_loop(0, counts[0], add_past, 0)

    def finish(place, carry):
        kept_copy(place, near_plan[3 * place + 1]).wait()
        return carry

    lax.fori_loop(0, jnp.minimum(near_plan[0], KEPT), finish, 0)


def near_kernel(step, last, clus_count, lags, *refs):
    (
        near_idx_in, near_cnt_in, near_lag_in, near_frac_in, old_plan_in, incident_in, weights,
        past_spectra, blocks,
    ) = refs[:9]
    newer, refs = refs[9 : 9 + step], refs[9 + step :]
    if step:
        table_in, base, blended, known = refs[:4]
        refs = refs[4:]
    else:
        plane, chip_swap, base, blended, known, table_out = refs[:6]
        refs = refs[6:]
    (
        table, held, tall, field, spectra, incident, near_idx, near_cnt, near_lag, near_frac,
        old_plan, sems, more_sems, wide_sems, out_sem,
    ) = refs
    clusters, slots = near_idx.shape
    unknowns = incident.shape[1]
    halves = tall.shape[2] // LANE
    side_rows = table.shape[1] // 3
    slab = lax.axis_index("slab")
    now = lags + max(step - 1, 0)
    chunks = [(first, min(CHUNK, slots - first)) for first in range(0, slots, CHUNK)]

    def block_copy(cluster, number):
        first, size = chunks[number]
        return pltpu.make_async_copy(
            blocks.at[cluster, pl.ds(first, size)],
            held.at[pl.ds(cluster * slots + first, size)],
            sems.at[cluster * len(chunks) + number],
        )

    if step:
        wide_pairs = [(table_in.at[pl.ds(0, now)], table.at[pl.ds(0, now)])]
    else:
        odd = lax.rem(slab, 2)
        sides = [1 + core - odd for core in range(2)] + [2 * odd]
        each = side_rows // clus_count
        wide_pairs = []
        for number in range(3 * clus_count):
            source = plane if number < 2 * clus_count else chip_swap
            core, member = divmod(number, clus_count)
            start = pl.multiple_of(sides[core] * side_rows + member * each, each)
            wide_pairs.append(
                (
                    source.at[number % source.shape[0]],
                    table.at[pl.ds(0, lags), pl.ds(start, each)],
                )
            )
    small = start_all(
        (
            (near_cnt_in, near_cnt), (near_idx_in, near_idx), (near_lag_in, near_lag),
            (near_frac_in, near_frac),
        ),
        more_sems,
    )
    wide = start_all(wide_pairs, wide_sems)
    pairs = [(incident_in.at[step], incident)]
    if not last:
        pairs.append((old_plan_in, old_plan))
    others = start_all(pairs, more_sems.at[pl.ds(4, 2)])
    for cluster in range(clusters):
        block_copy(cluster, 0).start()
    tall[...] = jnp.zeros(tall.shape, jnp.float32)
    if not last:
        spectra[:lags] = past_spectra[...]
        for back, source in enumerate(newer):
            spectra[lags + back] = source[...]
        known[...] = jnp.zeros(known.shape, jnp.float32)
    wait_all(small)
    most = near_cnt[0]
    for cluster in range(1, clusters):
        most = jnp.maximum(most, near_cnt[cluster])
    for number in range(1, len(chunks)):
        for cluster in range(clusters):

            @pl.when(chunks[number][0] < near_cnt[cluster])
            def _():
                block_copy(cluster, number).start()

    wait_all(wide)
    if not step:
        keep = pltpu.make_async_copy(
            table.at[pl.ds(0, lags)], table_out.at[pl.ds(0, lags)], out_sem
        )
        keep.start()
    first_row = (slab - 1) * side_rows
    newest = lags + step - 2 if step else lags - 1
    for cluster in range(clusters):
        for slot in range(slots):
            row = row_of(near_idx[cluster, slot], clusters, halves) - first_row
            lag_slot = step - near_lag[cluster, slot] + lags
            frac = near_frac[cluster, slot]
            weight = jnp.where(lag_slot > newest, 0.0, 1.0 - frac)
            first_slot = jnp.minimum(lag_slot, newest)
            for half in range(halves):
                at = pl.ds(row + half * clusters, 1)
                tall[cluster, slot : slot + 1, half * LANE : (half + 1) * LANE] = (
                    weight * table[first_slot, at, :] + frac * table[lag_slot - 1, at, :]
                )
    for cluster in range(clusters):
        blended[cluster * slots : (cluster + 1) * slots, :] = tall[cluster, :slots, :]
    wait_all(others)
    if not last:

        def one(place, carry):
            before, total = carry
            group = old_plan[3 * place + 1]
            slot = step + 1 + lags - old_plan[3 * place + 3]
            term = weights[old_plan[3 * place + 2]] * spectra[slot]
            total = jnp.where(group == before, total, 0.0) + term
            known[group] = total
            return group, total

        lax.fori_loop(
            0, old_plan[0], one, (jnp.int32(-1), jnp.zeros(known.shape[1:], jnp.float32))
        )
    which = lax.broadcasted_iota(jnp.int32, (tall.shape[1], unknowns), 0)

    def part(number, cluster):
        first, size = chunks[number]
        values = tall[cluster].astype(jnp.bfloat16)[:, :unknowns]
        sums = jnp.zeros((tall.shape[1], unknowns), jnp.float32)
        for slot in range(first, first + size):
            counts = slot < near_cnt[cluster]
            if step:
                counts = counts & (near_lag[cluster, slot] > 1)
            product = dot_t(values, held[cluster * slots + slot])
            sums = jnp.where(which == jnp.where(counts, slot, -1), product, sums)
        return sums

    for cluster in range(clusters):
        block_copy(cluster, 0).wait()
    for cluster in range(clusters):
        field[cluster] = part(0, cluster)
    for number in range(1, len(chunks)):

        @pl.when(chunks[number][0] < most)
        def _():
            for cluster in range(clusters):

                @pl.when(chunks[number][0] < near_cnt[cluster])
                def _():
                    block_copy(cluster, number).wait()

            for cluster in range(clusters):
                field[cluster] += part(number, cluster)

    for cluster in range(clusters):
        total = jnp.sum(field[cluster], axis=0, keepdims=True)
        base[cluster : cluster + 1, :] = incident[cluster : cluster + 1, :] - total
    if not step:
        keep.wait()


def march_kernel(step, last, clus_count, slab_count, lags, *refs):
    (
        near_plan_in, kept_plan, base, blended, known, kept, kept_weight, rays, inverses, shift,
        fresh_weights, arrived, blocks,
    ) = refs[:13]
    if last:
        _, output = refs[13:15]
        refs = refs[15:]
    elif step:
        _, _, output, table, spectrum, message = refs[13:19]
        refs = refs[19:]
    else:
        output, spectrum, message = refs[13:16]
        refs = refs[16:]
    near_plan, current, values, extra, field, sem, sems = refs
    clusters, unknowns = base.shape
    slots = blocks.shape[1]
    groups, dir_rows = fresh_weights.shape[:2]
    rows_each = arrived.shape[0] // groups
    halves = rows_each // clusters
    side_rows = clus_count * rows_each
    slab = lax.axis_index("slab")
    which = lax.broadcasted_iota(jnp.int32, (clusters, unknowns), 0)
    kept_copies = []
    if step and not last:
        for side in range(3):
            other = jnp.clip(slab + (side - 1), 0, slab_count - 1)
            copy = pltpu.make_async_copy(
                arrived.at[pl.ds(pl.multiple_of(other * side_rows, side_rows), side_rows)],
                table.at[lags + step - 1, pl.ds(side * side_rows, side_rows)],
                sems.at[1 + side],
            )
            copy.start()
            kept_copies.append(copy)

    def is_near(group):
        return jnp.abs(group // clus_count - slab) <= 1

    sums = [jnp.zeros((dir_rows, LANE), jnp.float32) for _ in range(4)]
    for group in range(groups):
        first = group * rows_each
        sums[group % 4] += jnp.where(is_near(group), 0.0, arrived[first : first + dir_rows, :])
    incoming = (sums[0] + sums[1]) + (sums[2] + sums[3])
    row_in = jnp.concatenate([incoming[r : r + 1] for r in range(dir_rows)], axis=1)
    inbound = (shift[...] * row_in).astype(jnp.bfloat16)
    far = jnp.zeros((clusters, unknowns), jnp.float32)
    for cluster in range(clusters):
        far = jnp.where(which == cluster, dot_t(inbound, rays[cluster]), far)
    remaining = base[...] - far

    def fresh_row(place, entry, row):
        newest = jnp.concatenate(
            [arrived[pl.ds(row + half * clusters, 1), :] for half in range(halves)], axis=1
        )
        return blended[pl.ds(entry, 1), :] + kept_weight[pl.ds(place, 1), :] * newest

    if step:
        plan = kept_plan[...]
        count = plan[0, 3]
        values[...] = jnp.zeros(values.shape, jnp.float32)
        for place in range(KEPT):
            values[place : place + 1, :] = fresh_row(place, plan[place, 0], plan[place, 2])
        rows = values[...].astype(jnp.bfloat16)[:, :unknowns]
        for place in range(KEPT):
            product = dot_t(rows, kept[place])[place : place + 1]
            cluster = jnp.where(place < count, plan[place, 1], -1)
            remaining = remaining - jnp.where(which == cluster, product, 0.0)
        field[...] = remaining

        @pl.when(count > KEPT)
        def _():
            plan_copy = pltpu.make_async_copy(near_plan_in, near_plan, sems.at[0])
            plan_copy.start()
            plan_copy.wait()

            def one(place, carry):
                entry = near_plan[3 * place + 1]
                cluster = near_plan[3 * place + 2]
                source = blocks.at[cluster, entry - cluster * slots]
                copy = pltpu.make_async_copy(source, extra, sem)
                copy.start()
                row = fresh_row(place, entry, near_plan[3 * place + 3])
                row = jnp.broadcast_to(row, (8, halves * LANE))
                copy.wait()
                product = dot_t(row.astype(jnp.bfloat16)[:, :unknowns], extra[...])
                field[pl.ds(cluster, 1), :] -= product[:1]
                return carry

            lax.fori_loop(KEPT, count, one, 0)

        remaining = field[...]

    right_side = remaining.astype(jnp.bfloat16)
    solved = jnp.zeros((clusters, unknowns), jnp.float32)
    for cluster in range(clusters):
        solved = jnp.where(which == cluster, dot_t(right_side, inverses[cluster]), solved)
    current[...] = solved
    out_copy = pltpu.make_async_copy(current, output.at[step], sems.at[4])
    out_copy.start()
    if not last:
        own = rows_of(padded(solved, halves * LANE), halves)
        rounded = solved.astype(jnp.bfloat16)
        which_dir = lax.broadcasted_iota(jnp.int32, (clusters, dir_rows * LANE), 0)
        ray_vals = jnp.zeros((clusters, dir_rows * LANE), jnp.float32)
        for cluster in range(clusters):
            ray_vals = jnp.where(which_dir == cluster, dot(rounded, rays[cluster]), ray_vals)
        newest = rows_of(jnp.sum(ray_vals * shift[...], axis=0, keepdims=True), dir_rows)
        spectrum[...] = newest
        for group in range(groups):
            far_sum = known[group] + fresh_weights[group] * newest
            message[group, :dir_rows, :] = jnp.where(is_near(group), own[:dir_rows], far_sum)
            message[group, dir_rows:, :] = own[dir_rows:]
    out_copy.wait()
    wait_all(kept_copies)


def local(
    incident,
    history,
    near_blocks,
    near_idx,
    near_cnt,
    near_lag,
    near_frac,
    inverses,
    rays,
    shift,
    far_idx,
    far_lag,
    trans,
):
    f32, i32, bf16 = jnp.float32, jnp.int32, jnp.bfloat16
    shaped = jax.ShapeDtypeStruct
    lags, clusters, unknowns = history.shape
    steps = incident.shape[0]
    slots = near_idx.shape[1]
    groups, entries, dirs = trans.shape
    dir_rows = dirs // LANE
    halves = pl.cdiv(unknowns, LANE)
    msg_rows = halves * clusters
    wide = halves * LANE
    near_entries = clusters * slots
    far_entries = groups * entries
    slab_count = lax.axis_size("slab")
    clus_count = lax.axis_size("clus")
    params = pltpu.CompilerParams(vmem_limit_bytes=VMEM_LIMIT)
    rays = jnp.swapaxes(rays, 1, 2)

    dma = pltpu.SemaphoreType.DMA
    peers = 2 * clus_count
    packed = pl.pallas_call(
        pack_kernel,
        out_shape=shaped((peers, lags, msg_rows, LANE), f32),
        in_specs=[VMEM],
        out_specs=HBM,
        scratch_shapes=[pltpu.VMEM((lags, msg_rows, LANE), f32), dma((peers,))],
        compiler_params=params,
        name="pack_history",
    )(*in_hbm(history))
    planes = [list(range(first, first + peers)) for first in range(0, groups, peers)]
    plane = lax.all_to_all(
        packed, ("slab", "clus"), 0, 0, tiled=True, axis_index_groups=planes
    )
    own_side = lax.rem(lax.axis_index("slab"), 2) * clus_count
    own = lax.dynamic_slice_in_dim(plane, own_side, clus_count, axis=0)

    smem_lists = [
        pltpu.SMEM((clusters, slots), i32),
        pltpu.SMEM((clusters,), i32),
        pltpu.SMEM((clusters, slots), i32),
        pltpu.SMEM((clusters, slots), f32),
    ]
    near_lists = in_hbm(near_idx, near_cnt, near_lag, near_frac)
    (blocks,) = in_hbm(near_blocks)
    spectra, message, weights, fresh_weights, kept, kept_weight, kept_plan, near_plan, old_plan = (
        pl.pallas_call(
            functools.partial(begin_kernel, clus_count),
            out_shape=(
                shaped((lags, dir_rows, LANE), f32),
                shaped((groups, msg_rows, LANE), f32),
                shaped((far_entries, dir_rows, LANE), f32),
                shaped((groups, dir_rows, LANE), f32),
                shaped((KEPT, unknowns, unknowns), bf16),
                shaped((near_entries, wide), f32),
                shaped((8, LANE), i32),
                pltpu.HBM((3 * near_entries + 4,), i32),
                pltpu.HBM((3 * far_entries + 4,), i32),
            ),
            in_specs=[HBM] * 11,
            out_specs=[VMEM] * 7 + [SMEM] * 2,
            scratch_shapes=[
                pltpu.VMEM(rays.shape, bf16),
                pltpu.VMEM(history.shape, f32),
                pltpu.VMEM(shift.shape, f32),
                pltpu.VMEM(trans.shape, trans.dtype),
                pltpu.SMEM((entries, groups), i32),
                pltpu.SMEM((entries, groups), i32),
                *smem_lists,
                pltpu.SMEM((2 * far_entries + 2,), i32),
                dma,
                dma((10,)),
            ],
            compiler_params=params,
            name="past_spectra",
        )(
            *in_hbm(rays, history, shift, trans, far_idx.T, far_lag.T),
            *near_lists,
            blocks,
        )
    )
    own, message = lax.optimization_barrier((own, message))
    chips = [(i, i + 1) for i in range(1, slab_count - 1, 2)]
    chip_swap = lax.ppermute(own, "slab", chips + [(b, a) for a, b in chips])

    table_shape = (lags + steps, 3 * clus_count * msg_rows, LANE)
    tall_rows = -(-slots // PACK) * PACK
    newer = []
    for step in range(steps):
        last = step == steps - 1
        arrived = lax.all_to_all(message, ("slab", "clus"), 0, 0, tiled=True)
        arrived = arrived.reshape(groups * msg_rows, LANE)
        out_shape = [
            shaped((clusters, unknowns), f32),
            shaped((near_entries, wide), f32),
            shaped((groups, dir_rows, LANE), f32),
        ]
        currents_in = in_hbm(table) if step else in_hbm(plane, chip_swap)
        results = pl.pallas_call(
            functools.partial(near_kernel, step, last, clus_count, lags),
            out_shape=out_shape if step else out_shape + [pltpu.HBM(table_shape, f32)],
            in_specs=[HBM] * 6 + [VMEM] * 2 + [HBM] + [VMEM] * step + [HBM] * len(currents_in),
            out_specs=[VMEM] * 3 + ([] if step else [HBM]),
            scratch_shapes=[
                pltpu.VMEM(table_shape, f32),
                pltpu.VMEM((near_entries, unknowns, unknowns), bf16),
                pltpu.VMEM((clusters, tall_rows, wide), f32),
                pltpu.VMEM((clusters, tall_rows, unknowns), f32),
                pltpu.VMEM((lags + steps, dir_rows, LANE), f32),
                pltpu.VMEM((clusters, unknowns), f32),
                *smem_lists,
                pltpu.SMEM(old_plan.shape, i32),
                dma((near_entries,)),
                dma((6,)),
                dma((3 * clus_count,)),
                dma,
            ],
            compiler_params=params,
            cost_estimate=pl.CostEstimate(
                flops=2 * near_blocks.size, bytes_accessed=3 * near_blocks.size, transcendentals=0
            ),
            name=f"known_near_field_{step}",
        )(
            *near_lists,
            *in_hbm(old_plan, incident),
            *in_vmem(weights, spectra),
            blocks,
            *in_vmem(*newer),
            *currents_in,
        )
        base, blended, known = results[:3]
        if not step:
            table = results[3]
        out_shape = [pltpu.HBM(incident.shape, f32)]
        changed = []
        if step:
            changed.append(output)
        if step and not last:
            changed.append(table)
            out_shape.append(pltpu.HBM(table_shape, f32))
        whole = len(out_shape)
        if not last:
            out_shape += [shaped((dir_rows, LANE), f32), shaped(message.shape, f32)]
        results = pl.pallas_call(
            functools.partial(march_kernel, step, last, clus_count, slab_count, lags),
            out_shape=out_shape,
            in_specs=[HBM] + [VMEM] * 11 + [HBM] * (1 + len(changed)),
            out_specs=[HBM] * whole + [VMEM] * (len(out_shape) - whole),
            scratch_shapes=[
                pltpu.SMEM(near_plan.shape, i32),
                pltpu.VMEM((clusters, unknowns), f32),
                pltpu.VMEM((8, wide), f32),
                pltpu.VMEM((unknowns, unknowns), bf16),
                pltpu.VMEM((clusters, unknowns), f32),
                dma,
                dma((5,)),
            ],
            input_output_aliases={13 + number: number for number in range(len(changed))},
            compiler_params=params,
            name=f"march_{step}",
        )(
            *in_hbm(near_plan),
            *in_vmem(
                kept_plan, base, blended, known, kept, kept_weight, rays, inverses, shift,
                fresh_weights, arrived,
            ),
            blocks,
            *in_hbm(*changed),
        )
        output = results[0]
        if last:
            return output
        if step:
            table = results[1]
        spectrum, message = results[-2:]
        newer.append(spectrum)


def solution(mesh):
    both = ("slab", "clus")
    in_specs = (
        P(None, both, None),
        P(None, both, None),
        P(both, None, None, None),
        P(both, None),
        P(both),
        P(both, None),
        P(both, None),
        P(both, None, None),
        P(both, None, None),
        P(both, None),
        P(),
        P(),
        P(),
    )
    out_specs = P(None, both, None)
    return jax.shard_map(local, mesh=mesh, in_specs=in_specs, out_specs=out_specs, check_vma=False)
```

```python
import functools

import jax
import jax.numpy as jnp
from jax import lax
from jax.experimental import pallas as pl
from jax.experimental.pallas import tpu as pltpu
from jax.sharding import PartitionSpec as P

LANE = 128
PACK = 16
KEPT = 8
CHUNK = 3
VMEM_LIMIT = 24 * 1024 * 1024
HBM = pl.BlockSpec(memory_space=pltpu.HBM)
ANY = pl.BlockSpec(memory_space=pl.ANY)
VMEM = pl.BlockSpec(memory_space=pltpu.VMEM)
SMEM = pl.BlockSpec(memory_space=pltpu.SMEM)


def rows_of(wide, count):
    return jnp.concatenate([wide[:, r * LANE : (r + 1) * LANE] for r in range(count)], axis=0)


def padded(wide, width):
    return jnp.concatenate(
        [wide, jnp.zeros((wide.shape[0], width - wide.shape[1]), wide.dtype)], axis=1
    )


def dot(left, right):
    return jnp.dot(left, right, preferred_element_type=jnp.float32)


def dot_t(left, right):
    return lax.dot_general(
        left, right, (((1,), (1,)), ((), ())), preferred_element_type=jnp.float32
    )


def pack_kernel(history, packed):
    lags, clusters, unknowns = history.shape
    halves = packed.shape[1] // clusters
    for half in range(halves):
        low, high = half * LANE, min(unknowns, (half + 1) * LANE)
        part = history[:, :, low:high]
        if high - low < LANE:
            part = jnp.concatenate(
                [part, jnp.zeros((lags, clusters, LANE - (high - low)), jnp.float32)], axis=2
            )
        packed[:, half * clusters : (half + 1) * clusters, :] = part


def join_tails(tails, size):
    lane = lax.broadcasted_iota(jnp.int32, (1, LANE), 1)
    spare = LANE - size
    rest = tails[3:4]
    return jnp.concatenate(
        [
            jnp.where(lane < size, tails[0:1], pltpu.roll(rest, size, 1)),
            jnp.where(lane < size, tails[1:2], pltpu.roll(rest, size - spare, 1)),
            tails[2:3],
        ],
        axis=0,
    )


def last_tail(first, second, size):
    lane = lax.broadcasted_iota(jnp.int32, (1, LANE), 1)
    spare = LANE - size
    return jnp.where(
        lane < spare, pltpu.roll(first, spare, 1), pltpu.roll(second, 2 * spare, 1)
    )


def in_hbm(*arrays):
    return [pltpu.with_memory_space_constraint(array, pltpu.HBM) for array in arrays]


def in_vmem(*arrays):
    return [pltpu.with_memory_space_constraint(array, pltpu.VMEM) for array in arrays]


def start_all(pairs, sems):
    copies = []
    for number, (source, target) in enumerate(pairs):
        copy = pltpu.make_async_copy(source, target, sems.at[number])
        copy.start()
        copies.append(copy)
    return copies


def wait_all(copies):
    for copy in copies:
        copy.wait()


def any_of(flags):
    found = flags[0]
    for flag in flags[1:]:
        found = found | flag
    return found


def row_of(cluster_number, clusters, halves):
    place = lax.rem(cluster_number, clusters)
    return (cluster_number - place) * halves + place


def begin_kernel(
    clus_count,
    rays_in, history_in, shift_in, trans_in, far_idx_in, far_lag_in, near_idx_in, near_cnt_in,
    near_lag_in, near_frac_in, blocks,
    spectra, message, weights, fresh_weights, kept, kept_weight, kept_plan, near_plan, old_plan,
    rays, history, shift, trans, far_idx, far_lag, near_idx, near_cnt, near_lag, near_frac,
    far_list, outgoing, sem, sems,
):
    small = start_all(
        (
            (far_idx_in, far_idx), (far_lag_in, far_lag), (trans_in, trans),
            (near_idx_in, near_idx), (near_cnt_in, near_cnt), (near_lag_in, near_lag),
            (near_frac_in, near_frac),
        ),
        sems,
    )
    large = start_all(
        ((history_in, history), (shift_in, shift), (rays_in, rays)), sems.at[pl.ds(7, 3)]
    )
    lags, clusters, unknowns = history.shape
    dir_rows = spectra.shape[1]
    entries, groups = far_idx.shape
    slots = near_idx.shape[1]
    halves = pl.cdiv(unknowns, LANE)
    myself = lax.axis_index("slab") * clus_count + lax.axis_index("clus")

    def kept_copy(place, entry):
        source = blocks.at[lax.div(entry, slots), lax.rem(entry, slots)]
        return pltpu.make_async_copy(source, kept.at[place], sem)

    for place in range(3 * KEPT + 1):
        near_plan[place] = 0
    kept_weight[...] = jnp.zeros(kept_weight.shape, jnp.float32)
    kept_plan[...] = jnp.zeros(kept_plan.shape, jnp.int32)
    lane = lax.broadcasted_iota(jnp.int32, (1, LANE), 1)
    outgoing[...] = jnp.zeros(outgoing.shape, jnp.float32)
    fresh_weights[...] = jnp.zeros(fresh_weights.shape, jnp.float32)
    wait_all(small)
    near_plan[0] = 0
    for cluster in range(clusters):
        fresh = [
            (slot < near_cnt[cluster]) & (near_lag[cluster, slot] == 1) for slot in range(slots)
        ]

        @pl.when(any_of(fresh))
        def _(cluster=cluster, fresh=fresh):
            for slot in range(slots):

                @pl.when(fresh[slot])
                def _(slot=slot):
                    count = near_plan[0]
                    entry = jnp.int32(cluster * slots + slot)
                    place = row_of(near_idx[cluster, slot], clusters, halves)
                    near_plan[3 * count + 1] = entry
                    near_plan[3 * count + 2] = jnp.int32(cluster)
                    near_plan[3 * count + 3] = place
                    row = jnp.zeros((1, kept_weight.shape[1]), jnp.float32)
                    kept_weight[pl.ds(count, 1), :] = row + (1.0 - near_frac[cluster, slot])
                    near_plan[0] = count + 1

                    @pl.when(count < KEPT)
                    def _():
                        kept_copy(count, entry).start()
                        fields = jnp.where(lane == 0, entry, jnp.where(lane == 1, cluster, place))
                        kept_plan[pl.ds(count, 1), :] = fields

    kept_plan[...] = jnp.where(
        lax.broadcasted_iota(jnp.int32, kept_plan.shape, 1) == 3, near_plan[0], kept_plan[...]
    )
    def one(group, counts):
        listed = [far_idx[column, group] == myself for column in range(entries)]

        def add(counts):
            place, old_count = counts
            for column in range(entries):
                lag = far_lag[column, group]

                @pl.when(listed[column])
                def _(place=place, lag=lag, column=column, old_count=old_count):
                    row = trans[group, column : column + 1, :].astype(jnp.float32)
                    weight = rows_of(row, dir_rows)
                    weights[place] = weight
                    far_list[2 * place] = group
                    far_list[2 * place + 1] = lag

                    @pl.when(lag == 1)
                    def _():
                        fresh_weights[group] += weight

                    @pl.when(lag > 1)
                    def _():
                        old_plan[3 * old_count + 1] = group
                        old_plan[3 * old_count + 2] = place
                        old_plan[3 * old_count + 3] = lag

                place = place + jnp.where(listed[column], 1, 0)
                old_count = old_count + jnp.where(listed[column] & (lag > 1), 1, 0)
            return place, old_count

        return lax.cond(any_of(listed), add, lambda counts: counts, counts)

    counts = lax.fori_loop(0, groups, one, (jnp.int32(0), jnp.int32(0)))
    old_plan[0] = counts[1]

    wait_all(large)
    total = jnp.zeros((lags, dir_rows * LANE), jnp.float32)
    for cluster in range(clusters):
        past = history[:, cluster, :].astype(jnp.bfloat16)
        total += dot(past, rays[cluster]) * shift[cluster : cluster + 1, :]
    for lag in range(lags):
        spectra[lag] = rows_of(total[lag : lag + 1], dir_rows)

    def add_past(place, carry):
        group, lag = far_list[2 * place], far_list[2 * place + 1]
        outgoing[group, :dir_rows, :] += weights[place] * spectra[lags - lag]
        return carry

    lax.fori_loop(0, counts[0], add_past, 0)
    send = pltpu.make_async_copy(outgoing, message.at[:, :, 0, :], sems.at[0])
    send.start()

    def finish(place, carry):
        kept_copy(place, near_plan[3 * place + 1]).wait()
        return carry

    lax.fori_loop(0, jnp.minimum(near_plan[0], KEPT), finish, 0)
    send.wait()


def near_kernel(step, last, clus_count, lags, *refs):
    (
        near_idx_in, near_cnt_in, near_lag_in, near_frac_in, old_plan_in, incident_in, weights,
        past_spectra, blocks,
    ) = refs[:9]
    newer, refs = refs[9 : 9 + step], refs[9 + step :]
    if step:
        table_in, base, blended, known = refs[:4]
        refs = refs[4:]
    else:
        mid, core_swap, chip_swap, base, blended, known, table_out = refs[:7]
        refs = refs[7:]
    (
        table, held, tall, field, spectra, incident, near_idx, near_cnt, near_lag, near_frac,
        old_plan, sems, more_sems, out_sem,
    ) = refs
    clusters, slots = near_idx.shape
    unknowns = incident.shape[1]
    halves = tall.shape[2] // LANE
    side_rows = table.shape[1] // 3
    slab = lax.axis_index("slab")
    now = lags + max(step - 1, 0)
    chunks = [(first, min(CHUNK, slots - first)) for first in range(0, slots, CHUNK)]

    def block_copy(cluster, number):
        first, size = chunks[number]
        return pltpu.make_async_copy(
            blocks.at[cluster, pl.ds(first, size)],
            held.at[pl.ds(cluster * slots + first, size)],
            sems.at[cluster * len(chunks) + number],
        )

    if step:
        wide_pairs = [(table_in.at[pl.ds(0, now)], table.at[pl.ds(0, now)])]
    else:
        odd = lax.rem(slab, 2)
        wide_pairs = []
        for source, side in ((mid, 1), (core_swap, 2 - 2 * odd), (chip_swap, 2 * odd)):
            start = pl.multiple_of(side * side_rows, side_rows)
            wide_pairs.append((source, table.at[pl.ds(0, lags), pl.ds(start, side_rows)]))
    small = start_all(
        (
            (near_cnt_in, near_cnt), (near_idx_in, near_idx), (near_lag_in, near_lag),
            (near_frac_in, near_frac),
        ),
        more_sems,
    )
    wide = start_all(wide_pairs, more_sems.at[pl.ds(4, 3)])
    pairs = [(incident_in.at[step], incident)]
    if not last:
        pairs.append((old_plan_in, old_plan))
    others = start_all(pairs, more_sems.at[pl.ds(7, 2)])
    for cluster in range(clusters):
        block_copy(cluster, 0).start()
    tall[...] = jnp.zeros(tall.shape, jnp.float32)
    if not last:
        spectra[:lags] = past_spectra[...]
        for back, source in enumerate(newer):
            spectra[lags + back] = source[...]
        known[...] = jnp.zeros(known.shape, jnp.float32)
    wait_all(small)
    most = near_cnt[0]
    for cluster in range(1, clusters):
        most = jnp.maximum(most, near_cnt[cluster])
    for number in range(1, len(chunks)):
        for cluster in range(clusters):

            @pl.when(chunks[number][0] < near_cnt[cluster])
            def _():
                block_copy(cluster, number).start()

    wait_all(wide)
    if not step:
        keep = pltpu.make_async_copy(
            table.at[pl.ds(0, lags)], table_out.at[pl.ds(0, lags)], out_sem
        )
        keep.start()
    first_row = (slab - 1) * side_rows
    newest = lags + step - 2 if step else lags - 1
    for cluster in range(clusters):
        for slot in range(slots):
            row = row_of(near_idx[cluster, slot], clusters, halves) - first_row
            lag_slot = step - near_lag[cluster, slot] + lags
            frac = near_frac[cluster, slot]
            weight = jnp.where(lag_slot > newest, 0.0, 1.0 - frac)
            first_slot = jnp.minimum(lag_slot, newest)
            for half in range(halves):
                at = pl.ds(row + half * clusters, 1)
                tall[cluster, slot : slot + 1, half * LANE : (half + 1) * LANE] = (
                    weight * table[first_slot, at, :] + frac * table[lag_slot - 1, at, :]
                )
    for cluster in range(clusters):
        blended[cluster * slots : (cluster + 1) * slots, :] = tall[cluster, :slots, :]
    wait_all(others)
    if not last:

        def one(place, carry):
            before, total = carry
            group = old_plan[3 * place + 1]
            slot = step + 1 + lags - old_plan[3 * place + 3]
            term = weights[old_plan[3 * place + 2]] * spectra[slot]
            total = jnp.where(group == before, total, 0.0) + term
            known[group] = total
            return group, total

        lax.fori_loop(
            0, old_plan[0], one, (jnp.int32(-1), jnp.zeros(known.shape[1:], jnp.float32))
        )
    which = lax.broadcasted_iota(jnp.int32, (tall.shape[1], unknowns), 0)

    def part(number, cluster):
        first, size = chunks[number]
        values = tall[cluster].astype(jnp.bfloat16)[:, :unknowns]
        sums = jnp.zeros((tall.shape[1], unknowns), jnp.float32)
        for slot in range(first, first + size):
            counts = slot < near_cnt[cluster]
            if step:
                counts = counts & (near_lag[cluster, slot] > 1)
            product = dot_t(values, held[cluster * slots + slot])
            sums = jnp.where(which == jnp.where(counts, slot, -1), product, sums)
        return sums

    for cluster in range(clusters):
        block_copy(cluster, 0).wait()
    for cluster in range(clusters):
        field[cluster] = part(0, cluster)
    for number in range(1, len(chunks)):

        @pl.when(chunks[number][0] < most)
        def _():
            for cluster in range(clusters):

                @pl.when(chunks[number][0] < near_cnt[cluster])
                def _():
                    block_copy(cluster, number).wait()

            for cluster in range(clusters):
                field[cluster] += part(number, cluster)

    for cluster in range(clusters):
        total = jnp.sum(field[cluster], axis=0, keepdims=True)
        base[cluster : cluster + 1, :] = incident[cluster : cluster + 1, :] - total
    if not step:
        keep.wait()


def march_kernel(step, last, clus_count, slab_count, lags, *refs):
    (
        near_plan_in, kept_plan, base, blended, known, kept, kept_weight, rays, inverses, shift,
        fresh_weights, arrived, blocks,
    ) = refs[:13]
    if last:
        _, output = refs[13:15]
        refs = refs[15:]
    elif step:
        _, _, output, table, spectrum, message = refs[13:19]
        refs = refs[19:]
    else:
        output, spectrum, message = refs[13:16]
        refs = refs[16:]
    near_plan, current, values, extra, field, window, outgoing, sem, sems = refs
    clusters, unknowns = base.shape
    slots = blocks.shape[1]
    groups, dir_rows = fresh_weights.shape[:2]
    sent_rows = arrived.shape[0] // groups
    halves = pl.cdiv(unknowns, LANE)
    rows_each = halves * clusters
    tail = unknowns - LANE
    slab = lax.axis_index("slab")
    which = lax.broadcasted_iota(jnp.int32, (clusters, unknowns), 0)
    first_row = (slab - 1) * clus_count * rows_each
    if step:
        for member in range(3 * clus_count):
            side, place = divmod(member, clus_count)
            other = jnp.clip(slab + (side - 1), 0, slab_count - 1)
            start = (other * clus_count + place) * sent_rows
            for row in range(sent_rows):
                window[member * rows_each + row : member * rows_each + row + 1, :] = arrived[
                    start + row
                ]
            window[(member + 1) * rows_each - 1 : (member + 1) * rows_each, :] = last_tail(
                arrived[start + clusters], arrived[start + clusters + 1], tail
            )
    keep = None
    if step and not last:
        keep = pltpu.make_async_copy(window, table.at[lags + step - 1], sems.at[2])
        keep.start()

    def is_near(group):
        return jnp.abs(group // clus_count - slab) <= 1

    sums = [jnp.zeros((1, LANE), jnp.float32) for _ in range(2 * dir_rows)]
    for group in range(groups):
        near = is_near(group)
        for row in range(dir_rows):
            sums[2 * row + group % 2] += jnp.where(near, 0.0, arrived[group * sent_rows + row])
    row_in = jnp.concatenate(
        [sums[2 * row] + sums[2 * row + 1] for row in range(dir_rows)], axis=1
    )
    inbound = (shift[...] * row_in).astype(jnp.bfloat16)
    far = jnp.zeros((clusters, unknowns), jnp.float32)
    for cluster in range(clusters):
        far = jnp.where(which == cluster, dot_t(inbound, rays[cluster]), far)
    remaining = base[...] - far

    def fresh_row(place, entry, row):
        newest = jnp.concatenate(
            [window[pl.ds(row + half * clusters - first_row, 1), :] for half in range(halves)],
            axis=1,
        )
        return blended[pl.ds(entry, 1), :] + kept_weight[pl.ds(place, 1), :] * newest

    if step:
        plan = kept_plan[...]
        count = plan[0, 3]
        values[...] = jnp.zeros(values.shape, jnp.float32)
        for place in range(KEPT):
            row = jnp.where(place < count, plan[place, 2], first_row)
            values[place : place + 1, :] = fresh_row(place, plan[place, 0], row)
        rows = values[...].astype(jnp.bfloat16)[:, :unknowns]
        for place in range(KEPT):
            product = dot_t(rows, kept[place])[place : place + 1]
            cluster = jnp.where(place < count, plan[place, 1], -1)
            remaining = remaining - jnp.where(which == cluster, product, 0.0)
        field[...] = remaining

        @pl.when(count > KEPT)
        def _():
            plan_copy = pltpu.make_async_copy(near_plan_in, near_plan, sems.at[0])
            plan_copy.start()
            plan_copy.wait()

            def one(place, carry):
                entry = near_plan[3 * place + 1]
                cluster = near_plan[3 * place + 2]
                source = blocks.at[cluster, entry - cluster * slots]
                copy = pltpu.make_async_copy(source, extra, sem)
                copy.start()
                row = fresh_row(place, entry, near_plan[3 * place + 3])
                row = jnp.broadcast_to(row, (8, halves * LANE))
                copy.wait()
                product = dot_t(row.astype(jnp.bfloat16)[:, :unknowns], extra[...])
                field[pl.ds(cluster, 1), :] -= product[:1]
                return carry

            lax.fori_loop(KEPT, count, one, 0)

        remaining = field[...]

    right_side = remaining.astype(jnp.bfloat16)
    solved = jnp.zeros((clusters, unknowns), jnp.float32)
    for cluster in range(clusters):
        solved = jnp.where(which == cluster, dot_t(right_side, inverses[cluster]), solved)
    current[...] = solved
    out_copy = pltpu.make_async_copy(current, output.at[step], sems.at[4])
    out_copy.start()
    if not last:
        own = rows_of(padded(solved, halves * LANE), halves)
        rounded = solved.astype(jnp.bfloat16)
        which_dir = lax.broadcasted_iota(jnp.int32, (clusters, dir_rows * LANE), 0)
        ray_vals = jnp.zeros((clusters, dir_rows * LANE), jnp.float32)
        for cluster in range(clusters):
            ray_vals = jnp.where(which_dir == cluster, dot(rounded, rays[cluster]), ray_vals)
        newest = rows_of(jnp.sum(ray_vals * shift[...], axis=0, keepdims=True), dir_rows)
        spectrum[...] = newest
        tails = join_tails(own[clusters:], tail)
        for group in range(groups):
            far_sum = known[group] + fresh_weights[group] * newest
            outgoing[group, :dir_rows, :] = jnp.where(is_near(group), own[:dir_rows], far_sum)
            outgoing[group, dir_rows:, :] = tails
        send = pltpu.make_async_copy(outgoing, message.at[:, :, 0, :], sems.at[1])
        send.start()
        send.wait()
    out_copy.wait()
    if keep is not None:
        keep.wait()


def exchange(block, axis, bit):
    count = lax.axis_size(axis)
    return lax.ppermute(block, axis, [(i, i ^ bit) for i in range(count)])


def local(
    incident,
    history,
    near_blocks,
    near_idx,
    near_cnt,
    near_lag,
    near_frac,
    inverses,
    rays,
    shift,
    far_idx,
    far_lag,
    trans,
):
    f32, i32, bf16 = jnp.float32, jnp.int32, jnp.bfloat16
    shaped = jax.ShapeDtypeStruct
    lags, clusters, unknowns = history.shape
    steps = incident.shape[0]
    slots = near_idx.shape[1]
    groups, entries, dirs = trans.shape
    dir_rows = dirs // LANE
    halves = pl.cdiv(unknowns, LANE)
    msg_rows = halves * clusters
    sent_rows = msg_rows - 1
    wide = halves * LANE
    near_entries = clusters * slots
    far_entries = groups * entries
    slab_count = lax.axis_size("slab")
    clus_count = lax.axis_size("clus")
    clus_index = lax.axis_index("clus")
    params = pltpu.CompilerParams(vmem_limit_bytes=VMEM_LIMIT)
    rays = jnp.swapaxes(rays, 1, 2)

    packed = pl.pallas_call(
        pack_kernel,
        out_shape=shaped((lags, msg_rows, LANE), f32),
        in_specs=[VMEM],
        out_specs=VMEM,
        compiler_params=params,
        name="pack_history",
    )(*in_hbm(history))
    pieces = [packed] + [exchange(packed, "clus", bit) for bit in range(1, clus_count)]
    stacked = jnp.stack(pieces, axis=0)
    mid = jnp.stack(
        [lax.dynamic_index_in_dim(stacked, clus_index ^ c, 0, False) for c in range(clus_count)],
        axis=1,
    )

    smem_lists = [
        pltpu.SMEM((clusters, slots), i32),
        pltpu.SMEM((clusters,), i32),
        pltpu.SMEM((clusters, slots), i32),
        pltpu.SMEM((clusters, slots), f32),
    ]
    dma = pltpu.SemaphoreType.DMA
    near_lists = in_hbm(near_idx, near_cnt, near_lag, near_frac)
    (blocks,) = in_hbm(near_blocks)
    spectra, message, weights, fresh_weights, kept, kept_weight, kept_plan, near_plan, old_plan = (
        pl.pallas_call(
            functools.partial(begin_kernel, clus_count),
            out_shape=(
                shaped((lags, dir_rows, LANE), f32),
                pltpu.HBM((groups, sent_rows, 1, LANE), f32),
                shaped((far_entries, dir_rows, LANE), f32),
                shaped((groups, dir_rows, LANE), f32),
                shaped((KEPT, unknowns, unknowns), bf16),
                shaped((near_entries, wide), f32),
                shaped((8, LANE), i32),
                pltpu.HBM((3 * near_entries + 4,), i32),
                pltpu.HBM((3 * far_entries + 4,), i32),
            ),
            in_specs=[HBM] * 11,
            out_specs=[VMEM, HBM] + [VMEM] * 5 + [SMEM] * 2,
            scratch_shapes=[
                pltpu.VMEM(rays.shape, bf16),
                pltpu.VMEM(history.shape, f32),
                pltpu.VMEM(shift.shape, f32),
                pltpu.VMEM(trans.shape, trans.dtype),
                pltpu.SMEM((entries, groups), i32),
                pltpu.SMEM((entries, groups), i32),
                *smem_lists,
                pltpu.SMEM((2 * far_entries + 2,), i32),
                pltpu.VMEM((groups, sent_rows, LANE), f32),
                dma,
                dma((10,)),
            ],
            compiler_params=params,
            name="past_spectra",
        )(
            *in_hbm(rays, history, shift, trans, far_idx.T, far_lag.T),
            *near_lists,
            blocks,
        )
    )
    mid, message = lax.optimization_barrier((mid, message))
    mid = mid.reshape(lags, clus_count * msg_rows, LANE)
    core_swap = lax.ppermute(mid, "slab", [(i, i ^ 1) for i in range(slab_count)])
    chips = [(i, i + 1) for i in range(1, slab_count - 1, 2)]
    chip_swap = lax.ppermute(mid, "slab", chips + [(b, a) for a, b in chips])

    table_shape = (lags + steps, 3 * clus_count * msg_rows, LANE)
    tall_rows = -(-slots // PACK) * PACK
    newer = []
    for step in range(steps):
        last = step == steps - 1
        arrived = lax.all_to_all(message, ("slab", "clus"), 0, 0, tiled=True)
        arrived = arrived.reshape(groups * sent_rows, 1, LANE)
        out_shape = [
            shaped((clusters, unknowns), f32),
            shaped((near_entries, wide), f32),
            shaped((groups, dir_rows, LANE), f32),
        ]
        currents_in = in_hbm(table) if step else in_hbm(mid, core_swap, chip_swap)
        results = pl.pallas_call(
            functools.partial(near_kernel, step, last, clus_count, lags),
            out_shape=out_shape if step else out_shape + [pltpu.HBM(table_shape, f32)],
            in_specs=[HBM] * 6 + [VMEM] * 2 + [HBM] + [VMEM] * step + [HBM] * len(currents_in),
            out_specs=[VMEM] * 3 + ([] if step else [HBM]),
            scratch_shapes=[
                pltpu.VMEM(table_shape, f32),
                pltpu.VMEM((near_entries, unknowns, unknowns), bf16),
                pltpu.VMEM((clusters, tall_rows, wide), f32),
                pltpu.VMEM((clusters, tall_rows, unknowns), f32),
                pltpu.VMEM((lags + steps, dir_rows, LANE), f32),
                pltpu.VMEM((clusters, unknowns), f32),
                *smem_lists,
                pltpu.SMEM(old_plan.shape, i32),
                dma((near_entries,)),
                dma((9,)),
                dma,
            ],
            compiler_params=params,
            cost_estimate=pl.CostEstimate(
                flops=2 * near_blocks.size, bytes_accessed=3 * near_blocks.size, transcendentals=0
            ),
            name=f"known_near_field_{step}",
        )(
            *near_lists,
            *in_hbm(old_plan, incident),
            *in_vmem(weights, spectra),
            blocks,
            *in_vmem(*newer),
            *currents_in,
        )
        base, blended, known = results[:3]
        if not step:
            table = results[3]
        out_shape = [pltpu.HBM(incident.shape, f32)]
        changed = []
        if step:
            changed.append(output)
        if step and not last:
            changed.append(table)
            out_shape.append(pltpu.HBM(table_shape, f32))
        whole = len(out_shape)
        if not last:
            out_shape += [shaped((dir_rows, LANE), f32), pltpu.HBM(message.shape, f32)]
        results = pl.pallas_call(
            functools.partial(march_kernel, step, last, clus_count, slab_count, lags),
            out_shape=out_shape,
            in_specs=[HBM] + [VMEM] * 11 + [HBM] * (1 + len(changed)),
            out_specs=[HBM] * whole + ([] if last else [VMEM, HBM]),
            scratch_shapes=[
                pltpu.SMEM(near_plan.shape, i32),
                pltpu.VMEM((clusters, unknowns), f32),
                pltpu.VMEM((8, wide), f32),
                pltpu.VMEM((unknowns, unknowns), bf16),
                pltpu.VMEM((clusters, unknowns), f32),
                pltpu.VMEM((3 * clus_count * msg_rows, LANE), f32),
                pltpu.VMEM((groups, sent_rows, LANE), f32),
                dma,
                dma((5,)),
            ],
            input_output_aliases={13 + number: number for number in range(len(changed))},
            compiler_params=params,
            name=f"march_{step}",
        )(
            *in_hbm(near_plan),
            *in_vmem(
                kept_plan, base, blended, known, kept, kept_weight, rays, inverses, shift,
                fresh_weights, arrived,
            ),
            blocks,
            *in_hbm(*changed),
        )
        output = results[0]
        if last:
            return output
        if step:
            table = results[1]
        spectrum, message = results[-2:]
        newer.append(spectrum)


def solution(mesh):
    both = ("slab", "clus")
    in_specs = (
        P(None, both, None),
        P(None, both, None),
        P(both, None, None, None),
        P(both, None),
        P(both),
        P(both, None),
        P(both, None),
        P(both, None, None),
        P(both, None, None),
        P(both, None),
        P(),
        P(),
        P(),
    )
    out_specs = P(None, both, None)
    return jax.shard_map(local, mesh=mesh, in_specs=in_specs, out_specs=out_specs, check_vma=False)
```

```python
import functools

import jax
import jax.numpy as jnp
from jax import lax
from jax.experimental import pallas as pl
from jax.experimental.pallas import tpu as pltpu
from jax.sharding import PartitionSpec as P

LANE = 128
PACK = 16
KEPT = 8
CHUNK = 3
VMEM_LIMIT = 24 * 1024 * 1024
HBM = pl.BlockSpec(memory_space=pltpu.HBM)
ANY = pl.BlockSpec(memory_space=pl.ANY)
VMEM = pl.BlockSpec(memory_space=pltpu.VMEM)
SMEM = pl.BlockSpec(memory_space=pltpu.SMEM)


def rows_of(wide, count):
    return jnp.concatenate([wide[:, r * LANE : (r + 1) * LANE] for r in range(count)], axis=0)


def padded(wide, width):
    return jnp.concatenate(
        [wide, jnp.zeros((wide.shape[0], width - wide.shape[1]), wide.dtype)], axis=1
    )


def dot(left, right):
    return jnp.dot(left, right, preferred_element_type=jnp.float32)


def dot_t(left, right):
    return lax.dot_general(
        left, right, (((1,), (1,)), ((), ())), preferred_element_type=jnp.float32
    )


def pack_kernel(history, packed):
    lags, clusters, unknowns = history.shape
    halves = packed.shape[1] // clusters
    for half in range(halves):
        low, high = half * LANE, min(unknowns, (half + 1) * LANE)
        part = history[:, :, low:high]
        if high - low < LANE:
            part = jnp.concatenate(
                [part, jnp.zeros((lags, clusters, LANE - (high - low)), jnp.float32)], axis=2
            )
        packed[:, half * clusters : (half + 1) * clusters, :] = part


def join_tails(tails, size):
    lane = lax.broadcasted_iota(jnp.int32, (1, LANE), 1)
    spare = LANE - size
    rest = tails[3:4]
    return jnp.concatenate(
        [
            jnp.where(lane < size, tails[0:1], pltpu.roll(rest, size, 1)),
            jnp.where(lane < size, tails[1:2], pltpu.roll(rest, size - spare, 1)),
            tails[2:3],
        ],
        axis=0,
    )


def last_tail(first, second, size):
    lane = lax.broadcasted_iota(jnp.int32, (1, LANE), 1)
    spare = LANE - size
    return jnp.where(
        lane < spare, pltpu.roll(first, spare, 1), pltpu.roll(second, 2 * spare, 1)
    )


def in_hbm(*arrays):
    return [pltpu.with_memory_space_constraint(array, pltpu.HBM) for array in arrays]


def in_vmem(*arrays):
    return [pltpu.with_memory_space_constraint(array, pltpu.VMEM) for array in arrays]


def start_all(pairs, sems):
    copies = []
    for number, (source, target) in enumerate(pairs):
        copy = pltpu.make_async_copy(source, target, sems.at[number])
        copy.start()
        copies.append(copy)
    return copies


def wait_all(copies):
    for copy in copies:
        copy.wait()


def any_of(flags):
    found = flags[0]
    for flag in flags[1:]:
        found = found | flag
    return found


def row_of(cluster_number, clusters, halves):
    if clusters & (clusters - 1):
        place = lax.rem(cluster_number, clusters)
    else:
        place = cluster_number & (clusters - 1)
    return (cluster_number - place) * halves + place


def begin_kernel(
    clus_count,
    rays_in, history_in, shift_in, trans_in, far_idx_in, far_lag_in, near_idx_in, near_cnt_in,
    near_lag_in, near_frac_in, blocks,
    spectra, message, weights, fresh_weights, kept, kept_weight, kept_plan, near_plan_out,
    old_plan_out, rays, history, shift, trans, far_idx, far_lag, near_idx, near_cnt, near_lag, near_frac,
    far_list, outgoing, near_plan, old_plan, sem, sems,
):
    small = start_all(
        (
            (far_idx_in, far_idx), (far_lag_in, far_lag), (trans_in, trans),
            (near_idx_in, near_idx), (near_cnt_in, near_cnt), (near_lag_in, near_lag),
            (near_frac_in, near_frac),
        ),
        sems,
    )
    large = start_all(
        ((history_in, history), (shift_in, shift), (rays_in, rays)), sems.at[pl.ds(7, 3)]
    )
    lags, clusters, unknowns = history.shape
    dir_rows = spectra.shape[1]
    entries, groups = far_idx.shape
    slots = near_idx.shape[1]
    halves = pl.cdiv(unknowns, LANE)
    myself = lax.axis_index("slab") * clus_count + lax.axis_index("clus")

    def kept_copy(place, entry):
        source = blocks.at[lax.div(entry, slots), lax.rem(entry, slots)]
        return pltpu.make_async_copy(source, kept.at[place], sem)

    for place in range(3 * KEPT + 1):
        near_plan[place] = 0
    kept_weight[...] = jnp.zeros(kept_weight.shape, jnp.float32)
    kept_plan[...] = jnp.zeros(kept_plan.shape, jnp.int32)
    lane = lax.broadcasted_iota(jnp.int32, (1, LANE), 1)
    outgoing[...] = jnp.zeros(outgoing.shape, jnp.float32)
    fresh_weights[...] = jnp.zeros(fresh_weights.shape, jnp.float32)
    wait_all(small)
    near_plan[0] = 0
    for cluster in range(clusters):
        fresh = [
            (slot < near_cnt[cluster]) & (near_lag[cluster, slot] == 1) for slot in range(slots)
        ]

        @pl.when(any_of(fresh))
        def _(cluster=cluster, fresh=fresh):
            for slot in range(slots):

                @pl.when(fresh[slot])
                def _(slot=slot):
                    count = near_plan[0]
                    entry = jnp.int32(cluster * slots + slot)
                    place = row_of(near_idx[cluster, slot], clusters, halves)
                    near_plan[3 * count + 1] = entry
                    near_plan[3 * count + 2] = jnp.int32(cluster)
                    near_plan[3 * count + 3] = place
                    row = jnp.zeros((1, kept_weight.shape[1]), jnp.float32)
                    kept_weight[pl.ds(count, 1), :] = row + (1.0 - near_frac[cluster, slot])
                    near_plan[0] = count + 1

                    @pl.when(count < KEPT)
                    def _():
                        kept_copy(count, entry).start()
                        fields = jnp.where(lane == 0, entry, jnp.where(lane == 1, cluster, place))
                        kept_plan[pl.ds(count, 1), :] = fields

    kept_plan[...] = jnp.where(
        lax.broadcasted_iota(jnp.int32, kept_plan.shape, 1) == 3, near_plan[0], kept_plan[...]
    )
    def one(group, counts):
        listed = [far_idx[column, group] == myself for column in range(entries)]

        def add(counts):
            place, old_count = counts
            for column in range(entries):
                lag = far_lag[column, group]

                @pl.when(listed[column])
                def _(place=place, lag=lag, column=column, old_count=old_count):
                    row = trans[group, column : column + 1, :].astype(jnp.float32)
                    weight = rows_of(row, dir_rows)
                    weights[place] = weight
                    far_list[2 * place] = group
                    far_list[2 * place + 1] = lag

                    @pl.when(lag == 1)
                    def _():
                        fresh_weights[group] += weight

                    @pl.when(lag > 1)
                    def _():
                        old_plan[3 * old_count + 1] = group
                        old_plan[3 * old_count + 2] = place
                        old_plan[3 * old_count + 3] = lag

                place = place + jnp.where(listed[column], 1, 0)
                old_count = old_count + jnp.where(listed[column] & (lag > 1), 1, 0)
            return place, old_count

        return lax.cond(any_of(listed), add, lambda counts: counts, counts)

    counts = lax.fori_loop(0, groups, one, (jnp.int32(0), jnp.int32(0)))
    old_plan[0] = counts[1]

    sends = start_all(
        ((near_plan, near_plan_out), (old_plan, old_plan_out)), sems.at[pl.ds(10, 2)]
    )
    wait_all(large)
    total = jnp.zeros((lags, dir_rows * LANE), jnp.float32)
    for cluster in range(clusters):
        past = history[:, cluster, :].astype(jnp.bfloat16)
        total += dot(past, rays[cluster]) * shift[cluster : cluster + 1, :]
    for lag in range(lags):
        spectra[lag] = rows_of(total[lag : lag + 1], dir_rows)

    def add_past(place, carry):
        group, lag = far_list[2 * place], far_list[2 * place + 1]
        outgoing[group, :dir_rows, :] += weights[place] * spectra[lags - lag]
        return carry

    lax.fori_loop(0, counts[0], add_past, 0)
    sends += start_all(((outgoing, message.at[:, :, 0, :]),), sems.at[pl.ds(12, 1)])

    def finish(place, carry):
        kept_copy(place, near_plan[3 * place + 1]).wait()
        return carry

    lax.fori_loop(0, jnp.minimum(near_plan[0], KEPT), finish, 0)
    wait_all(sends)


def near_kernel(step, last, clus_count, lags, *refs):
    (
        near_idx_in, near_cnt_in, near_lag_in, near_frac_in, old_plan_in, incident_in, weights,
        past_spectra, blocks,
    ) = refs[:9]
    newer, refs = refs[9 : 9 + step], refs[9 + step :]
    if step:
        table_in, base, blended, known = refs[:4]
        refs = refs[4:]
    else:
        mid, core_swap, chip_swap, base, blended, known, table_out = refs[:7]
        refs = refs[7:]
    (
        table, held, tall, field, spectra, incident, near_idx, near_cnt, near_lag, near_frac,
        old_plan, sems, more_sems, out_sem,
    ) = refs
    clusters, slots = near_idx.shape
    unknowns = incident.shape[1]
    halves = tall.shape[2] // LANE
    side_rows = table.shape[1] // 3
    slab = lax.axis_index("slab")
    now = lags + max(step - 1, 0)
    chunks = [(first, min(CHUNK, slots - first)) for first in range(0, slots, CHUNK)]

    def block_copy(cluster, number):
        first, size = chunks[number]
        return pltpu.make_async_copy(
            blocks.at[cluster, pl.ds(first, size)],
            held.at[pl.ds(cluster * slots + first, size)],
            sems.at[cluster * len(chunks) + number],
        )

    if step:
        wide_pairs = [(table_in.at[pl.ds(0, now)], table.at[pl.ds(0, now)])]
    else:
        odd = lax.rem(slab, 2)
        wide_pairs = []
        for source, side in ((mid, 1), (core_swap, 2 - 2 * odd), (chip_swap, 2 * odd)):
            start = pl.multiple_of(side * side_rows, side_rows)
            wide_pairs.append((source, table.at[pl.ds(0, lags), pl.ds(start, side_rows)]))
    small = start_all(
        (
            (near_cnt_in, near_cnt), (near_idx_in, near_idx), (near_lag_in, near_lag),
            (near_frac_in, near_frac),
        ),
        more_sems,
    )
    wide = start_all(wide_pairs, more_sems.at[pl.ds(4, 3)])
    pairs = [(incident_in.at[step], incident)]
    if not last:
        pairs.append((old_plan_in, old_plan))
    others = start_all(pairs, more_sems.at[pl.ds(7, 2)])
    for cluster in range(clusters):
        block_copy(cluster, 0).start()
    tall[...] = jnp.zeros(tall.shape, jnp.float32)
    if not last:
        spectra[:lags] = past_spectra[...]
        for back, source in enumerate(newer):
            spectra[lags + back] = source[...]
        known[...] = jnp.zeros(known.shape, jnp.float32)
    wait_all(small)
    most = near_cnt[0]
    for cluster in range(1, clusters):
        most = jnp.maximum(most, near_cnt[cluster])
    for number in range(1, len(chunks)):
        for cluster in range(clusters):

            @pl.when(chunks[number][0] < near_cnt[cluster])
            def _():
                block_copy(cluster, number).start()

    wait_all(others)
    if not last:

        def one(place, carry):
            before, total = carry
            group = old_plan[3 * place + 1]
            slot = step + 1 + lags - old_plan[3 * place + 3]
            term = weights[old_plan[3 * place + 2]] * spectra[slot]
            total = jnp.where(group == before, total, 0.0) + term
            known[group] = total
            return group, total

        lax.fori_loop(
            0, old_plan[0], one, (jnp.int32(-1), jnp.zeros(known.shape[1:], jnp.float32))
        )
    wait_all(wide)
    if not step:
        keep = pltpu.make_async_copy(
            table.at[pl.ds(0, lags)], table_out.at[pl.ds(0, lags)], out_sem
        )
        keep.start()
    first_row = (slab - 1) * side_rows
    newest = lags + step - 2 if step else lags - 1
    for cluster in range(clusters):
        for slot in range(slots):
            row = row_of(near_idx[cluster, slot], clusters, halves) - first_row
            lag_slot = step - near_lag[cluster, slot] + lags
            frac = near_frac[cluster, slot]
            weight = jnp.where(lag_slot > newest, 0.0, 1.0 - frac)
            first_slot = jnp.minimum(lag_slot, newest)
            for half in range(halves):
                at = pl.ds(row + half * clusters, 1)
                tall[cluster, slot : slot + 1, half * LANE : (half + 1) * LANE] = (
                    weight * table[first_slot, at, :] + frac * table[lag_slot - 1, at, :]
                )
    for cluster in range(clusters):
        blended[cluster * slots : (cluster + 1) * slots, :] = tall[cluster, :slots, :]
    which = lax.broadcasted_iota(jnp.int32, (tall.shape[1], unknowns), 0)

    def part(number, cluster):
        first, size = chunks[number]
        values = tall[cluster].astype(jnp.bfloat16)[:, :unknowns]
        sums = jnp.zeros((tall.shape[1], unknowns), jnp.float32)
        for slot in range(first, first + size):
            counts = slot < near_cnt[cluster]
            if step:
                counts = counts & (near_lag[cluster, slot] > 1)
            product = dot_t(values, held[cluster * slots + slot])
            sums = jnp.where(which == jnp.where(counts, slot, -1), product, sums)
        return sums

    for cluster in range(clusters):
        block_copy(cluster, 0).wait()
    for cluster in range(clusters):
        field[cluster] = part(0, cluster)
    for number in range(1, len(chunks)):

        @pl.when(chunks[number][0] < most)
        def _():
            for cluster in range(clusters):

                @pl.when(chunks[number][0] < near_cnt[cluster])
                def _():
                    block_copy(cluster, number).wait()

            for cluster in range(clusters):
                field[cluster] += part(number, cluster)

    for cluster in range(clusters):
        total = jnp.sum(field[cluster], axis=0, keepdims=True)
        base[cluster : cluster + 1, :] = incident[cluster : cluster + 1, :] - total
    if not step:
        keep.wait()


def march_kernel(step, last, clus_count, slab_count, lags, *refs):
    (
        near_plan_in, kept_plan, base, blended, known, kept, kept_weight, rays, inverses, shift,
        fresh_weights, arrived, blocks,
    ) = refs[:13]
    if last:
        _, output = refs[13:15]
        refs = refs[15:]
    elif step:
        _, _, output, table, spectrum, message = refs[13:19]
        refs = refs[19:]
    else:
        output, spectrum, message = refs[13:16]
        refs = refs[16:]
    near_plan, current, values, extra, field, window, outgoing, sem, sems = refs
    clusters, unknowns = base.shape
    slots = blocks.shape[1]
    groups, dir_rows = fresh_weights.shape[:2]
    sent_rows = arrived.shape[0] // groups
    halves = pl.cdiv(unknowns, LANE)
    rows_each = halves * clusters
    tail = unknowns - LANE
    slab = lax.axis_index("slab")
    which = lax.broadcasted_iota(jnp.int32, (clusters, unknowns), 0)
    first_row = (slab - 1) * clus_count * rows_each
    if step:
        for member in range(3 * clus_count):
            side, place = divmod(member, clus_count)
            other = jnp.clip(slab + (side - 1), 0, slab_count - 1)
            start = (other * clus_count + place) * sent_rows
            for row in range(sent_rows):
                window[member * rows_each + row : member * rows_each + row + 1, :] = arrived[
                    start + row
                ]
            window[(member + 1) * rows_each - 1 : (member + 1) * rows_each, :] = last_tail(
                arrived[start + clusters], arrived[start + clusters + 1], tail
            )
    keep = None
    if step and not last:
        keep = pltpu.make_async_copy(window, table.at[lags + step - 1], sems.at[2])
        keep.start()

    def is_near(group):
        return jnp.abs(group // clus_count - slab) <= 1

    sums = [jnp.zeros((1, LANE), jnp.float32) for _ in range(2 * dir_rows)]
    for group in range(groups):
        near = is_near(group)
        for row in range(dir_rows):
            sums[2 * row + group % 2] += jnp.where(near, 0.0, arrived[group * sent_rows + row])
    row_in = jnp.concatenate(
        [sums[2 * row] + sums[2 * row + 1] for row in range(dir_rows)], axis=1
    )
    inbound = (shift[...] * row_in).astype(jnp.bfloat16)
    far = jnp.zeros((clusters, unknowns), jnp.float32)
    for cluster in range(clusters):
        far = jnp.where(which == cluster, dot_t(inbound, rays[cluster]), far)
    remaining = base[...] - far

    def fresh_row(place, entry, row):
        newest = jnp.concatenate(
            [window[pl.ds(row + half * clusters - first_row, 1), :] for half in range(halves)],
            axis=1,
        )
        return blended[pl.ds(entry, 1), :] + kept_weight[pl.ds(place, 1), :] * newest

    if step:
        plan = kept_plan[...]
        count = plan[0, 3]
        values[...] = jnp.zeros(values.shape, jnp.float32)
        for place in range(KEPT):
            row = jnp.where(place < count, plan[place, 2], first_row)
            values[place : place + 1, :] = fresh_row(place, plan[place, 0], row)
        rows = values[...].astype(jnp.bfloat16)[:, :unknowns]
        for place in range(KEPT):
            product = dot_t(rows, kept[place])[place : place + 1]
            cluster = jnp.where(place < count, plan[place, 1], -1)
            remaining = remaining - jnp.where(which == cluster, product, 0.0)
        field[...] = remaining

        @pl.when(count > KEPT)
        def _():
            plan_copy = pltpu.make_async_copy(near_plan_in, near_plan, sems.at[0])
            plan_copy.start()
            plan_copy.wait()

            def one(place, carry):
                entry = near_plan[3 * place + 1]
                cluster = near_plan[3 * place + 2]
                source = blocks.at[cluster, entry - cluster * slots]
                copy = pltpu.make_async_copy(source, extra, sem)
                copy.start()
                row = fresh_row(place, entry, near_plan[3 * place + 3])
                row = jnp.broadcast_to(row, (8, halves * LANE))
                copy.wait()
                product = dot_t(row.astype(jnp.bfloat16)[:, :unknowns], extra[...])
                field[pl.ds(cluster, 1), :] -= product[:1]
                return carry

            lax.fori_loop(KEPT, count, one, 0)

        remaining = field[...]

    right_side = remaining.astype(jnp.bfloat16)
    solved = jnp.zeros((clusters, unknowns), jnp.float32)
    for cluster in range(clusters):
        solved = jnp.where(which == cluster, dot_t(right_side, inverses[cluster]), solved)
    current[...] = solved
    out_copy = pltpu.make_async_copy(current, output.at[step], sems.at[4])
    out_copy.start()
    if not last:
        own = rows_of(padded(solved, halves * LANE), halves)
        rounded = solved.astype(jnp.bfloat16)
        which_dir = lax.broadcasted_iota(jnp.int32, (clusters, dir_rows * LANE), 0)
        ray_vals = jnp.zeros((clusters, dir_rows * LANE), jnp.float32)
        for cluster in range(clusters):
            ray_vals = jnp.where(which_dir == cluster, dot(rounded, rays[cluster]), ray_vals)
        newest = rows_of(jnp.sum(ray_vals * shift[...], axis=0, keepdims=True), dir_rows)
        spectrum[...] = newest
        tails = join_tails(own[clusters:], tail)
        for group in range(groups):
            far_sum = known[group] + fresh_weights[group] * newest
            outgoing[group, :dir_rows, :] = jnp.where(is_near(group), own[:dir_rows], far_sum)
            outgoing[group, dir_rows:, :] = tails
        send = pltpu.make_async_copy(outgoing, message.at[:, :, 0, :], sems.at[1])
        send.start()
        send.wait()
    out_copy.wait()
    if keep is not None:
        keep.wait()


def exchange(block, axis, bit):
    count = lax.axis_size(axis)
    return lax.ppermute(block, axis, [(i, i ^ bit) for i in range(count)])


def local(
    incident,
    history,
    near_blocks,
    near_idx,
    near_cnt,
    near_lag,
    near_frac,
    inverses,
    rays,
    shift,
    far_idx,
    far_lag,
    trans,
):
    f32, i32, bf16 = jnp.float32, jnp.int32, jnp.bfloat16
    shaped = jax.ShapeDtypeStruct
    lags, clusters, unknowns = history.shape
    steps = incident.shape[0]
    slots = near_idx.shape[1]
    groups, entries, dirs = trans.shape
    dir_rows = dirs // LANE
    halves = pl.cdiv(unknowns, LANE)
    msg_rows = halves * clusters
    sent_rows = msg_rows - 1
    wide = halves * LANE
    near_entries = clusters * slots
    far_entries = groups * entries
    slab_count = lax.axis_size("slab")
    clus_count = lax.axis_size("clus")
    clus_index = lax.axis_index("clus")
    params = pltpu.CompilerParams(vmem_limit_bytes=VMEM_LIMIT)
    rays = jnp.swapaxes(rays, 1, 2)

    packed = pl.pallas_call(
        pack_kernel,
        out_shape=shaped((lags, msg_rows, LANE), f32),
        in_specs=[VMEM],
        out_specs=VMEM,
        compiler_params=params,
        name="pack_history",
    )(*in_hbm(history))
    pieces = [packed] + [exchange(packed, "clus", bit) for bit in range(1, clus_count)]
    stacked = jnp.stack(pieces, axis=0)
    mid = jnp.stack(
        [lax.dynamic_index_in_dim(stacked, clus_index ^ c, 0, False) for c in range(clus_count)],
        axis=1,
    )

    smem_lists = [
        pltpu.SMEM((clusters, slots), i32),
        pltpu.SMEM((clusters,), i32),
        pltpu.SMEM((clusters, slots), i32),
        pltpu.SMEM((clusters, slots), f32),
    ]
    dma = pltpu.SemaphoreType.DMA
    near_lists = in_hbm(near_idx, near_cnt, near_lag, near_frac)
    (blocks,) = in_hbm(near_blocks)
    spectra, message, weights, fresh_weights, kept, kept_weight, kept_plan, near_plan, old_plan = (
        pl.pallas_call(
            functools.partial(begin_kernel, clus_count),
            out_shape=(
                shaped((lags, dir_rows, LANE), f32),
                pltpu.HBM((groups, sent_rows, 1, LANE), f32),
                shaped((far_entries, dir_rows, LANE), f32),
                shaped((groups, dir_rows, LANE), f32),
                shaped((KEPT, unknowns, unknowns), bf16),
                shaped((near_entries, wide), f32),
                shaped((8, LANE), i32),
                pltpu.HBM((3 * near_entries + 4,), i32),
                pltpu.HBM((3 * far_entries + 4,), i32),
            ),
            in_specs=[HBM] * 11,
            out_specs=[VMEM, HBM] + [VMEM] * 5 + [HBM] * 2,
            scratch_shapes=[
                pltpu.VMEM(rays.shape, bf16),
                pltpu.VMEM(history.shape, f32),
                pltpu.VMEM(shift.shape, f32),
                pltpu.VMEM(trans.shape, trans.dtype),
                pltpu.SMEM((entries, groups), i32),
                pltpu.SMEM((entries, groups), i32),
                *smem_lists,
                pltpu.SMEM((2 * far_entries + 2,), i32),
                pltpu.VMEM((groups, sent_rows, LANE), f32),
                pltpu.SMEM((3 * near_entries + 4,), i32),
                pltpu.SMEM((3 * far_entries + 4,), i32),
                dma,
                dma((13,)),
            ],
            compiler_params=params,
            name="past_spectra",
        )(
            *in_hbm(rays, history, shift, trans, far_idx.T, far_lag.T),
            *near_lists,
            blocks,
        )
    )
    mid, message = lax.optimization_barrier((mid, message))
    mid = mid.reshape(lags, clus_count * msg_rows, LANE)
    core_swap = lax.ppermute(mid, "slab", [(i, i ^ 1) for i in range(slab_count)])
    chips = [(i, i + 1) for i in range(1, slab_count - 1, 2)]
    chip_swap = lax.ppermute(mid, "slab", chips + [(b, a) for a, b in chips])

    table_shape = (lags + steps, 3 * clus_count * msg_rows, LANE)
    tall_rows = -(-slots // PACK) * PACK
    newer = []
    for step in range(steps):
        last = step == steps - 1
        arrived = lax.all_to_all(message, ("slab", "clus"), 0, 0, tiled=True)
        arrived = arrived.reshape(groups * sent_rows, 1, LANE)
        out_shape = [
            shaped((clusters, unknowns), f32),
            shaped((near_entries, wide), f32),
            shaped((groups, dir_rows, LANE), f32),
        ]
        currents_in = in_hbm(table) if step else in_hbm(mid, core_swap, chip_swap)
        results = pl.pallas_call(
            functools.partial(near_kernel, step, last, clus_count, lags),
            out_shape=out_shape if step else out_shape + [pltpu.HBM(table_shape, f32)],
            in_specs=[HBM] * 6 + [VMEM] * 2 + [HBM] + [VMEM] * step + [HBM] * len(currents_in),
            out_specs=[VMEM] * 3 + ([] if step else [HBM]),
            scratch_shapes=[
                pltpu.VMEM(table_shape, f32),
                pltpu.VMEM((near_entries, unknowns, unknowns), bf16),
                pltpu.VMEM((clusters, tall_rows, wide), f32),
                pltpu.VMEM((clusters, tall_rows, unknowns), f32),
                pltpu.VMEM((lags + steps, dir_rows, LANE), f32),
                pltpu.VMEM((clusters, unknowns), f32),
                *smem_lists,
                pltpu.SMEM(old_plan.shape, i32),
                dma((near_entries,)),
                dma((9,)),
                dma,
            ],
            compiler_params=params,
            cost_estimate=pl.CostEstimate(
                flops=2 * near_blocks.size, bytes_accessed=3 * near_blocks.size, transcendentals=0
            ),
            name=f"known_near_field_{step}",
        )(
            *near_lists,
            *in_hbm(old_plan, incident),
            *in_vmem(weights, spectra),
            blocks,
            *in_vmem(*newer),
            *currents_in,
        )
        base, blended, known = results[:3]
        if not step:
            table = results[3]
        out_shape = [pltpu.HBM(incident.shape, f32)]
        changed = []
        if step:
            changed.append(output)
        if step and not last:
            changed.append(table)
            out_shape.append(pltpu.HBM(table_shape, f32))
        whole = len(out_shape)
        if not last:
            out_shape += [shaped((dir_rows, LANE), f32), pltpu.HBM(message.shape, f32)]
        results = pl.pallas_call(
            functools.partial(march_kernel, step, last, clus_count, slab_count, lags),
            out_shape=out_shape,
            in_specs=[HBM] + [VMEM] * 11 + [HBM] * (1 + len(changed)),
            out_specs=[HBM] * whole + ([] if last else [VMEM, HBM]),
            scratch_shapes=[
                pltpu.SMEM(near_plan.shape, i32),
                pltpu.VMEM((clusters, unknowns), f32),
                pltpu.VMEM((8, wide), f32),
                pltpu.VMEM((unknowns, unknowns), bf16),
                pltpu.VMEM((clusters, unknowns), f32),
                pltpu.VMEM((3 * clus_count * msg_rows, LANE), f32),
                pltpu.VMEM((groups, sent_rows, LANE), f32),
                dma,
                dma((5,)),
            ],
            input_output_aliases={13 + number: number for number in range(len(changed))},
            compiler_params=params,
            name=f"march_{step}",
        )(
            *in_hbm(near_plan),
            *in_vmem(
                kept_plan, base, blended, known, kept, kept_weight, rays, inverses, shift,
                fresh_weights, arrived,
            ),
            blocks,
            *in_hbm(*changed),
        )
        output = results[0]
        if last:
            return output
        if step:
            table = results[1]
        spectrum, message = results[-2:]
        newer.append(spectrum)


def solution(mesh):
    both = ("slab", "clus")
    in_specs = (
        P(None, both, None),
        P(None, both, None),
        P(both, None, None, None),
        P(both, None),
        P(both),
        P(both, None),
        P(both, None),
        P(both, None, None),
        P(both, None, None),
        P(both, None),
        P(),
        P(),
        P(),
    )
    out_specs = P(None, both, None)
    return jax.shard_map(local, mesh=mesh, in_specs=in_specs, out_specs=out_specs, check_vma=False)
```

```python
import functools

import jax
import jax.numpy as jnp
from jax import lax
from jax.experimental import pallas as pl
from jax.experimental.pallas import tpu as pltpu
from jax.sharding import PartitionSpec as P

LANE = 128
PACK = 16
KEPT = 8
CHUNK = 6
VMEM_LIMIT = 24 * 1024 * 1024
HBM = pl.BlockSpec(memory_space=pltpu.HBM)
ANY = pl.BlockSpec(memory_space=pl.ANY)
VMEM = pl.BlockSpec(memory_space=pltpu.VMEM)
SMEM = pl.BlockSpec(memory_space=pltpu.SMEM)


def rows_of(wide, count):
    return jnp.concatenate([wide[:, r * LANE : (r + 1) * LANE] for r in range(count)], axis=0)


def padded(wide, width):
    return jnp.concatenate(
        [wide, jnp.zeros((wide.shape[0], width - wide.shape[1]), wide.dtype)], axis=1
    )


def dot(left, right):
    return jnp.dot(left, right, preferred_element_type=jnp.float32)


def dot_t(left, right):
    return lax.dot_general(
        left, right, (((1,), (1,)), ((), ())), preferred_element_type=jnp.float32
    )


def pack_kernel(history, packed):
    lags, clusters, unknowns = history.shape
    halves = packed.shape[1] // clusters
    for half in range(halves):
        low, high = half * LANE, min(unknowns, (half + 1) * LANE)
        part = history[:, :, low:high]
        if high - low < LANE:
            part = jnp.concatenate(
                [part, jnp.zeros((lags, clusters, LANE - (high - low)), jnp.float32)], axis=2
            )
        packed[:, half * clusters : (half + 1) * clusters, :] = part


def join_tails(tails, size):
    lane = lax.broadcasted_iota(jnp.int32, (1, LANE), 1)
    spare = LANE - size
    rest = tails[3:4]
    return jnp.concatenate(
        [
            jnp.where(lane < size, tails[0:1], pltpu.roll(rest, size, 1)),
            jnp.where(lane < size, tails[1:2], pltpu.roll(rest, size - spare, 1)),
            tails[2:3],
        ],
        axis=0,
    )


def last_tail(first, second, size):
    lane = lax.broadcasted_iota(jnp.int32, (1, LANE), 1)
    spare = LANE - size
    return jnp.where(
        lane < spare, pltpu.roll(first, spare, 1), pltpu.roll(second, 2 * spare, 1)
    )


def in_hbm(*arrays):
    return [pltpu.with_memory_space_constraint(array, pltpu.HBM) for array in arrays]


def in_vmem(*arrays):
    return [pltpu.with_memory_space_constraint(array, pltpu.VMEM) for array in arrays]


def start_all(pairs, sems):
    copies = []
    for number, (source, target) in enumerate(pairs):
        copy = pltpu.make_async_copy(source, target, sems.at[number])
        copy.start()
        copies.append(copy)
    return copies


def wait_all(copies):
    for copy in copies:
        copy.wait()


def any_of(flags):
    found = flags[0]
    for flag in flags[1:]:
        found = found | flag
    return found


def row_of(cluster_number, clusters, halves):
    if clusters & (clusters - 1):
        place = lax.rem(cluster_number, clusters)
    else:
        place = cluster_number & (clusters - 1)
    return (cluster_number - place) * halves + place


def begin_kernel(
    clus_count,
    rays_in, history_in, shift_in, trans_in, far_idx_in, far_lag_in, near_idx_in, near_cnt_in,
    near_lag_in, near_frac_in, blocks,
    spectra, message, weights, fresh_weights, kept, kept_weight, kept_plan, near_plan_out,
    old_plan_out, rays, history, shift, trans, far_idx, far_lag, near_idx, near_cnt, near_lag, near_frac,
    far_list, outgoing, near_plan, old_plan, sem, sems,
):
    small = start_all(
        (
            (far_idx_in, far_idx), (far_lag_in, far_lag), (trans_in, trans),
            (near_idx_in, near_idx), (near_cnt_in, near_cnt), (near_lag_in, near_lag),
            (near_frac_in, near_frac),
        ),
        sems,
    )
    large = start_all(
        ((history_in, history), (shift_in, shift), (rays_in, rays)), sems.at[pl.ds(7, 3)]
    )
    lags, clusters, unknowns = history.shape
    dir_rows = spectra.shape[1]
    entries, groups = far_idx.shape
    slots = near_idx.shape[1]
    halves = pl.cdiv(unknowns, LANE)
    myself = lax.axis_index("slab") * clus_count + lax.axis_index("clus")

    def kept_copy(place, entry):
        source = blocks.at[lax.div(entry, slots), lax.rem(entry, slots)]
        return pltpu.make_async_copy(source, kept.at[place], sem)

    for place in range(3 * KEPT + 1):
        near_plan[place] = 0
    kept_weight[...] = jnp.zeros(kept_weight.shape, jnp.float32)
    kept_plan[...] = jnp.zeros(kept_plan.shape, jnp.int32)
    lane = lax.broadcasted_iota(jnp.int32, (1, LANE), 1)
    outgoing[...] = jnp.zeros(outgoing.shape, jnp.float32)
    fresh_weights[...] = jnp.zeros(fresh_weights.shape, jnp.float32)
    wait_all(small)
    near_plan[0] = 0
    for cluster in range(clusters):
        fresh = [
            (slot < near_cnt[cluster]) & (near_lag[cluster, slot] == 1) for slot in range(slots)
        ]

        @pl.when(any_of(fresh))
        def _(cluster=cluster, fresh=fresh):
            for slot in range(slots):

                @pl.when(fresh[slot])
                def _(slot=slot):
                    count = near_plan[0]
                    entry = jnp.int32(cluster * slots + slot)
                    place = row_of(near_idx[cluster, slot], clusters, halves)
                    near_plan[3 * count + 1] = entry
                    near_plan[3 * count + 2] = jnp.int32(cluster)
                    near_plan[3 * count + 3] = place
                    row = jnp.zeros((1, kept_weight.shape[1]), jnp.float32)
                    kept_weight[pl.ds(count, 1), :] = row + (1.0 - near_frac[cluster, slot])
                    near_plan[0] = count + 1

                    @pl.when(count < KEPT)
                    def _():
                        kept_copy(count, entry).start()
                        fields = jnp.where(lane == 0, entry, jnp.where(lane == 1, cluster, place))
                        kept_plan[pl.ds(count, 1), :] = fields

    kept_plan[...] = jnp.where(
        lax.broadcasted_iota(jnp.int32, kept_plan.shape, 1) == 3, near_plan[0], kept_plan[...]
    )
    def one(group, counts):
        listed = [far_idx[column, group] == myself for column in range(entries)]

        def add(counts):
            place, old_count = counts
            for column in range(entries):
                lag = far_lag[column, group]

                @pl.when(listed[column])
                def _(place=place, lag=lag, column=column, old_count=old_count):
                    row = trans[group, column : column + 1, :].astype(jnp.float32)
                    weight = rows_of(row, dir_rows)
                    weights[place] = weight
                    far_list[2 * place] = group
                    far_list[2 * place + 1] = lag

                    @pl.when(lag == 1)
                    def _():
                        fresh_weights[group] += weight

                    @pl.when(lag > 1)
                    def _():
                        old_plan[3 * old_count + 1] = group
                        old_plan[3 * old_count + 2] = place
                        old_plan[3 * old_count + 3] = lag

                place = place + jnp.where(listed[column], 1, 0)
                old_count = old_count + jnp.where(listed[column] & (lag > 1), 1, 0)
            return place, old_count

        return lax.cond(any_of(listed), add, lambda counts: counts, counts)

    counts = lax.fori_loop(0, groups, one, (jnp.int32(0), jnp.int32(0)))
    old_plan[0] = counts[1]

    sends = start_all(
        ((near_plan, near_plan_out), (old_plan, old_plan_out)), sems.at[pl.ds(10, 2)]
    )
    wait_all(large)
    total = jnp.zeros((lags, dir_rows * LANE), jnp.float32)
    for cluster in range(clusters):
        past = history[:, cluster, :].astype(jnp.bfloat16)
        total += dot(past, rays[cluster]) * shift[cluster : cluster + 1, :]
    for lag in range(lags):
        spectra[lag] = rows_of(total[lag : lag + 1], dir_rows)

    def add_past(place, carry):
        group, lag = far_list[2 * place], far_list[2 * place + 1]
        outgoing[group, :dir_rows, :] += weights[place] * spectra[lags - lag]
        return carry

    lax.fori_loop(0, counts[0], add_past, 0)
    sends += start_all(((outgoing, message.at[:, :, 0, :]),), sems.at[pl.ds(12, 1)])

    def finish(place, carry):
        kept_copy(place, near_plan[3 * place + 1]).wait()
        return carry

    lax.fori_loop(0, jnp.minimum(near_plan[0], KEPT), finish, 0)
    wait_all(sends)


def near_kernel(step, last, clus_count, lags, *refs):
    (
        near_idx_in, near_cnt_in, near_lag_in, near_frac_in, old_plan_in, incident_in, weights,
        past_spectra, blocks,
    ) = refs[:9]
    newer, refs = refs[9 : 9 + step], refs[9 + step :]
    if step:
        table_in, base, blended, known = refs[:4]
        refs = refs[4:]
    else:
        mid, core_swap, chip_swap, base, blended, known, table_out = refs[:7]
        refs = refs[7:]
    (
        table, held, tall, field, spectra, incident, near_idx, near_cnt, near_lag, near_frac,
        old_plan, sems, more_sems, out_sem,
    ) = refs
    clusters, slots = near_idx.shape
    unknowns = incident.shape[1]
    halves = tall.shape[2] // LANE
    side_rows = table.shape[1] // 3
    slab = lax.axis_index("slab")
    now = lags + max(step - 1, 0)
    chunks = [(first, min(CHUNK, slots - first)) for first in range(0, slots, CHUNK)]

    def block_copy(cluster, number):
        first, size = chunks[number]
        return pltpu.make_async_copy(
            blocks.at[cluster, pl.ds(first, size)],
            held.at[pl.ds(cluster * slots + first, size)],
            sems.at[cluster * len(chunks) + number],
        )

    if step:
        wide_pairs = [(table_in.at[pl.ds(0, now)], table.at[pl.ds(0, now)])]
    else:
        odd = lax.rem(slab, 2)
        wide_pairs = []
        for source, side in ((mid, 1), (core_swap, 2 - 2 * odd), (chip_swap, 2 * odd)):
            start = pl.multiple_of(side * side_rows, side_rows)
            wide_pairs.append((source, table.at[pl.ds(0, lags), pl.ds(start, side_rows)]))
    small = start_all(
        (
            (near_cnt_in, near_cnt), (near_idx_in, near_idx), (near_lag_in, near_lag),
            (near_frac_in, near_frac),
        ),
        more_sems,
    )
    wide = start_all(wide_pairs, more_sems.at[pl.ds(4, 3)])
    pairs = [(incident_in.at[step], incident)]
    if not last:
        pairs.append((old_plan_in, old_plan))
    others = start_all(pairs, more_sems.at[pl.ds(7, 2)])
    for cluster in range(clusters):
        block_copy(cluster, 0).start()
    tall[...] = jnp.zeros(tall.shape, jnp.float32)
    if not last:
        spectra[:lags] = past_spectra[...]
        for back, source in enumerate(newer):
            spectra[lags + back] = source[...]
        known[...] = jnp.zeros(known.shape, jnp.float32)
    wait_all(small)
    most = near_cnt[0]
    for cluster in range(1, clusters):
        most = jnp.maximum(most, near_cnt[cluster])
    for number in range(1, len(chunks)):
        for cluster in range(clusters):

            @pl.when(chunks[number][0] < near_cnt[cluster])
            def _():
                block_copy(cluster, number).start()

    wait_all(others)
    if not last:

        def one(place, carry):
            before, total = carry
            group = old_plan[3 * place + 1]
            slot = step + 1 + lags - old_plan[3 * place + 3]
            term = weights[old_plan[3 * place + 2]] * spectra[slot]
            total = jnp.where(group == before, total, 0.0) + term
            known[group] = total
            return group, total

        lax.fori_loop(
            0, old_plan[0], one, (jnp.int32(-1), jnp.zeros(known.shape[1:], jnp.float32))
        )
    wait_all(wide)
    if not step:
        keep = pltpu.make_async_copy(
            table.at[pl.ds(0, lags)], table_out.at[pl.ds(0, lags)], out_sem
        )
        keep.start()
    first_row = (slab - 1) * side_rows
    newest = lags + step - 2 if step else lags - 1
    for cluster in range(clusters):
        for slot in range(slots):
            row = row_of(near_idx[cluster, slot], clusters, halves) - first_row
            lag_slot = step - near_lag[cluster, slot] + lags
            frac = near_frac[cluster, slot]
            weight = jnp.where(lag_slot > newest, 0.0, 1.0 - frac)
            first_slot = jnp.minimum(lag_slot, newest)
            for half in range(halves):
                at = pl.ds(row + half * clusters, 1)
                tall[cluster, slot : slot + 1, half * LANE : (half + 1) * LANE] = (
                    weight * table[first_slot, at, :] + frac * table[lag_slot - 1, at, :]
                )
    for cluster in range(clusters):
        blended[cluster * slots : (cluster + 1) * slots, :] = tall[cluster, :slots, :]
    which = lax.broadcasted_iota(jnp.int32, (tall.shape[1], unknowns), 0)

    def part(number, cluster):
        first, size = chunks[number]
        values = tall[cluster].astype(jnp.bfloat16)[:, :unknowns]
        sums = jnp.zeros((tall.shape[1], unknowns), jnp.float32)
        for slot in range(first, first + size):
            counts = slot < near_cnt[cluster]
            if step:
                counts = counts & (near_lag[cluster, slot] > 1)
            product = dot_t(values, held[cluster * slots + slot])
            sums = jnp.where(which == jnp.where(counts, slot, -1), product, sums)
        return sums

    for cluster in range(clusters):
        block_copy(cluster, 0).wait()
    for cluster in range(clusters):
        field[cluster] = part(0, cluster)
    for number in range(1, len(chunks)):

        @pl.when(chunks[number][0] < most)
        def _():
            for cluster in range(clusters):

                @pl.when(chunks[number][0] < near_cnt[cluster])
                def _():
                    block_copy(cluster, number).wait()

            for cluster in range(clusters):
                field[cluster] += part(number, cluster)

    for cluster in range(clusters):
        total = jnp.sum(field[cluster], axis=0, keepdims=True)
        base[cluster : cluster + 1, :] = incident[cluster : cluster + 1, :] - total
    if not step:
        keep.wait()


def march_kernel(step, last, clus_count, slab_count, lags, *refs):
    (
        near_plan_in, kept_plan, base, blended, known, kept, kept_weight, rays, inverses, shift,
        fresh_weights, arrived, blocks,
    ) = refs[:13]
    if last:
        _, output = refs[13:15]
        refs = refs[15:]
    elif step:
        _, _, output, table, spectrum, message = refs[13:19]
        refs = refs[19:]
    else:
        output, spectrum, message = refs[13:16]
        refs = refs[16:]
    near_plan, current, values, extra, field, window, outgoing, sem, sems = refs
    clusters, unknowns = base.shape
    slots = blocks.shape[1]
    groups, dir_rows = fresh_weights.shape[:2]
    sent_rows = arrived.shape[0] // groups
    halves = pl.cdiv(unknowns, LANE)
    rows_each = halves * clusters
    tail = unknowns - LANE
    slab = lax.axis_index("slab")
    which = lax.broadcasted_iota(jnp.int32, (clusters, unknowns), 0)
    first_row = (slab - 1) * clus_count * rows_each
    if step:
        for member in range(3 * clus_count):
            side, place = divmod(member, clus_count)
            other = jnp.clip(slab + (side - 1), 0, slab_count - 1)
            start = (other * clus_count + place) * sent_rows
            for row in range(sent_rows):
                window[member * rows_each + row : member * rows_each + row + 1, :] = arrived[
                    start + row
                ]
            window[(member + 1) * rows_each - 1 : (member + 1) * rows_each, :] = last_tail(
                arrived[start + clusters], arrived[start + clusters + 1], tail
            )
    keep = None
    if step and not last:
        keep = pltpu.make_async_copy(window, table.at[lags + step - 1], sems.at[2])
        keep.start()

    def is_near(group):
        return jnp.abs(group // clus_count - slab) <= 1

    sums = [jnp.zeros((1, LANE), jnp.float32) for _ in range(2 * dir_rows)]
    for group in range(groups):
        near = is_near(group)
        for row in range(dir_rows):
            sums[2 * row + group % 2] += jnp.where(near, 0.0, arrived[group * sent_rows + row])
    row_in = jnp.concatenate(
        [sums[2 * row] + sums[2 * row + 1] for row in range(dir_rows)], axis=1
    )
    inbound = (shift[...] * row_in).astype(jnp.bfloat16)
    far = jnp.zeros((clusters, unknowns), jnp.float32)
    for cluster in range(clusters):
        far = jnp.where(which == cluster, dot_t(inbound, rays[cluster]), far)
    remaining = base[...] - far

    def fresh_row(place, entry, row):
        newest = jnp.concatenate(
            [window[pl.ds(row + half * clusters - first_row, 1), :] for half in range(halves)],
            axis=1,
        )
        return blended[pl.ds(entry, 1), :] + kept_weight[pl.ds(place, 1), :] * newest

    if step:
        plan = kept_plan[...]
        count = plan[0, 3]
        values[...] = jnp.zeros(values.shape, jnp.float32)
        for place in range(KEPT):
            row = jnp.where(place < count, plan[place, 2], first_row)
            values[place : place + 1, :] = fresh_row(place, plan[place, 0], row)
        rows = values[...].astype(jnp.bfloat16)[:, :unknowns]
        for place in range(KEPT):
            product = dot_t(rows, kept[place])[place : place + 1]
            cluster = jnp.where(place < count, plan[place, 1], -1)
            remaining = remaining - jnp.where(which == cluster, product, 0.0)
        field[...] = remaining

        @pl.when(count > KEPT)
        def _():
            plan_copy = pltpu.make_async_copy(near_plan_in, near_plan, sems.at[0])
            plan_copy.start()
            plan_copy.wait()

            def one(place, carry):
                entry = near_plan[3 * place + 1]
                cluster = near_plan[3 * place + 2]
                source = blocks.at[cluster, entry - cluster * slots]
                copy = pltpu.make_async_copy(source, extra, sem)
                copy.start()
                row = fresh_row(place, entry, near_plan[3 * place + 3])
                row = jnp.broadcast_to(row, (8, halves * LANE))
                copy.wait()
                product = dot_t(row.astype(jnp.bfloat16)[:, :unknowns], extra[...])
                field[pl.ds(cluster, 1), :] -= product[:1]
                return carry

            lax.fori_loop(KEPT, count, one, 0)

        remaining = field[...]

    right_side = remaining.astype(jnp.bfloat16)
    solved = jnp.zeros((clusters, unknowns), jnp.float32)
    for cluster in range(clusters):
        solved = jnp.where(which == cluster, dot_t(right_side, inverses[cluster]), solved)
    current[...] = solved
    out_copy = pltpu.make_async_copy(current, output.at[step], sems.at[4])
    out_copy.start()
    if not last:
        own = rows_of(padded(solved, halves * LANE), halves)
        rounded = solved.astype(jnp.bfloat16)
        which_dir = lax.broadcasted_iota(jnp.int32, (clusters, dir_rows * LANE), 0)
        ray_vals = jnp.zeros((clusters, dir_rows * LANE), jnp.float32)
        for cluster in range(clusters):
            ray_vals = jnp.where(which_dir == cluster, dot(rounded, rays[cluster]), ray_vals)
        newest = rows_of(jnp.sum(ray_vals * shift[...], axis=0, keepdims=True), dir_rows)
        spectrum[...] = newest
        tails = join_tails(own[clusters:], tail)
        for group in range(groups):
            far_sum = known[group] + fresh_weights[group] * newest
            outgoing[group, :dir_rows, :] = jnp.where(is_near(group), own[:dir_rows], far_sum)
            outgoing[group, dir_rows:, :] = tails
        send = pltpu.make_async_copy(outgoing, message.at[:, :, 0, :], sems.at[1])
        send.start()
        send.wait()
    out_copy.wait()
    if keep is not None:
        keep.wait()


def exchange(block, axis, bit):
    count = lax.axis_size(axis)
    return lax.ppermute(block, axis, [(i, i ^ bit) for i in range(count)])


def local(
    incident,
    history,
    near_blocks,
    near_idx,
    near_cnt,
    near_lag,
    near_frac,
    inverses,
    rays,
    shift,
    far_idx,
    far_lag,
    trans,
):
    f32, i32, bf16 = jnp.float32, jnp.int32, jnp.bfloat16
    shaped = jax.ShapeDtypeStruct
    lags, clusters, unknowns = history.shape
    steps = incident.shape[0]
    slots = near_idx.shape[1]
    groups, entries, dirs = trans.shape
    dir_rows = dirs // LANE
    halves = pl.cdiv(unknowns, LANE)
    msg_rows = halves * clusters
    sent_rows = msg_rows - 1
    wide = halves * LANE
    near_entries = clusters * slots
    far_entries = groups * entries
    slab_count = lax.axis_size("slab")
    clus_count = lax.axis_size("clus")
    clus_index = lax.axis_index("clus")
    params = pltpu.CompilerParams(vmem_limit_bytes=VMEM_LIMIT)
    rays = jnp.swapaxes(rays, 1, 2)

    packed = pl.pallas_call(
        pack_kernel,
        out_shape=shaped((lags, msg_rows, LANE), f32),
        in_specs=[VMEM],
        out_specs=VMEM,
        compiler_params=params,
        name="pack_history",
    )(*in_hbm(history))
    pieces = [packed] + [exchange(packed, "clus", bit) for bit in range(1, clus_count)]
    stacked = jnp.stack(pieces, axis=0)
    mid = jnp.stack(
        [lax.dynamic_index_in_dim(stacked, clus_index ^ c, 0, False) for c in range(clus_count)],
        axis=1,
    )

    smem_lists = [
        pltpu.SMEM((clusters, slots), i32),
        pltpu.SMEM((clusters,), i32),
        pltpu.SMEM((clusters, slots), i32),
        pltpu.SMEM((clusters, slots), f32),
    ]
    dma = pltpu.SemaphoreType.DMA
    near_lists = in_hbm(near_idx, near_cnt, near_lag, near_frac)
    (blocks,) = in_hbm(near_blocks)
    spectra, message, weights, fresh_weights, kept, kept_weight, kept_plan, near_plan, old_plan = (
        pl.pallas_call(
            functools.partial(begin_kernel, clus_count),
            out_shape=(
                shaped((lags, dir_rows, LANE), f32),
                pltpu.HBM((groups, sent_rows, 1, LANE), f32),
                shaped((far_entries, dir_rows, LANE), f32),
                shaped((groups, dir_rows, LANE), f32),
                shaped((KEPT, unknowns, unknowns), bf16),
                shaped((near_entries, wide), f32),
                shaped((8, LANE), i32),
                pltpu.HBM((3 * near_entries + 4,), i32),
                pltpu.HBM((3 * far_entries + 4,), i32),
            ),
            in_specs=[HBM] * 11,
            out_specs=[VMEM, HBM] + [VMEM] * 5 + [HBM] * 2,
            scratch_shapes=[
                pltpu.VMEM(rays.shape, bf16),
                pltpu.VMEM(history.shape, f32),
                pltpu.VMEM(shift.shape, f32),
                pltpu.VMEM(trans.shape, trans.dtype),
                pltpu.SMEM((entries, groups), i32),
                pltpu.SMEM((entries, groups), i32),
                *smem_lists,
                pltpu.SMEM((2 * far_entries + 2,), i32),
                pltpu.VMEM((groups, sent_rows, LANE), f32),
                pltpu.SMEM((3 * near_entries + 4,), i32),
                pltpu.SMEM((3 * far_entries + 4,), i32),
                dma,
                dma((13,)),
            ],
            compiler_params=params,
            name="past_spectra",
        )(
            *in_hbm(rays, history, shift, trans, far_idx.T, far_lag.T),
            *near_lists,
            blocks,
        )
    )
    mid, message = lax.optimization_barrier((mid, message))
    mid = mid.reshape(lags, clus_count * msg_rows, LANE)
    core_swap = lax.ppermute(mid, "slab", [(i, i ^ 1) for i in range(slab_count)])
    chips = [(i, i + 1) for i in range(1, slab_count - 1, 2)]
    chip_swap = lax.ppermute(mid, "slab", chips + [(b, a) for a, b in chips])

    table_shape = (lags + steps, 3 * clus_count * msg_rows, LANE)
    tall_rows = -(-slots // PACK) * PACK
    newer = []
    for step in range(steps):
        last = step == steps - 1
        arrived = lax.all_to_all(message, ("slab", "clus"), 0, 0, tiled=True)
        arrived = arrived.reshape(groups * sent_rows, 1, LANE)
        out_shape = [
            shaped((clusters, unknowns), f32),
            shaped((near_entries, wide), f32),
            shaped((groups, dir_rows, LANE), f32),
        ]
        currents_in = in_hbm(table) if step else in_hbm(mid, core_swap, chip_swap)
        results = pl.pallas_call(
            functools.partial(near_kernel, step, last, clus_count, lags),
            out_shape=out_shape if step else out_shape + [pltpu.HBM(table_shape, f32)],
            in_specs=[HBM] * 6 + [VMEM] * 2 + [HBM] + [VMEM] * step + [HBM] * len(currents_in),
            out_specs=[VMEM] * 3 + ([] if step else [HBM]),
            scratch_shapes=[
                pltpu.VMEM(table_shape, f32),
                pltpu.VMEM((near_entries, unknowns, unknowns), bf16),
                pltpu.VMEM((clusters, tall_rows, wide), f32),
                pltpu.VMEM((clusters, tall_rows, unknowns), f32),
                pltpu.VMEM((lags + steps, dir_rows, LANE), f32),
                pltpu.VMEM((clusters, unknowns), f32),
                *smem_lists,
                pltpu.SMEM(old_plan.shape, i32),
                dma((near_entries,)),
                dma((9,)),
                dma,
            ],
            compiler_params=params,
            cost_estimate=pl.CostEstimate(
                flops=2 * near_blocks.size, bytes_accessed=3 * near_blocks.size, transcendentals=0
            ),
            name=f"known_near_field_{step}",
        )(
            *near_lists,
            *in_hbm(old_plan, incident),
            *in_vmem(weights, spectra),
            blocks,
            *in_vmem(*newer),
            *currents_in,
        )
        base, blended, known = results[:3]
        if not step:
            table = results[3]
        out_shape = [pltpu.HBM(incident.shape, f32)]
        changed = []
        if step:
            changed.append(output)
        if step and not last:
            changed.append(table)
            out_shape.append(pltpu.HBM(table_shape, f32))
        whole = len(out_shape)
        if not last:
            out_shape += [shaped((dir_rows, LANE), f32), pltpu.HBM(message.shape, f32)]
        results = pl.pallas_call(
            functools.partial(march_kernel, step, last, clus_count, slab_count, lags),
            out_shape=out_shape,
            in_specs=[HBM] + [VMEM] * 11 + [HBM] * (1 + len(changed)),
            out_specs=[HBM] * whole + ([] if last else [VMEM, HBM]),
            scratch_shapes=[
                pltpu.SMEM(near_plan.shape, i32),
                pltpu.VMEM((clusters, unknowns), f32),
                pltpu.VMEM((8, wide), f32),
                pltpu.VMEM((unknowns, unknowns), bf16),
                pltpu.VMEM((clusters, unknowns), f32),
                pltpu.VMEM((3 * clus_count * msg_rows, LANE), f32),
                pltpu.VMEM((groups, sent_rows, LANE), f32),
                dma,
                dma((5,)),
            ],
            input_output_aliases={13 + number: number for number in range(len(changed))},
            compiler_params=params,
            name=f"march_{step}",
        )(
            *in_hbm(near_plan),
            *in_vmem(
                kept_plan, base, blended, known, kept, kept_weight, rays, inverses, shift,
                fresh_weights, arrived,
            ),
            blocks,
            *in_hbm(*changed),
        )
        output = results[0]
        if last:
            return output
        if step:
            table = results[1]
        spectrum, message = results[-2:]
        newer.append(spectrum)


def solution(mesh):
    both = ("slab", "clus")
    in_specs = (
        P(None, both, None),
        P(None, both, None),
        P(both, None, None, None),
        P(both, None),
        P(both),
        P(both, None),
        P(both, None),
        P(both, None, None),
        P(both, None, None),
        P(both, None),
        P(),
        P(),
        P(),
    )
    out_specs = P(None, both, None)
    return jax.shard_map(local, mesh=mesh, in_specs=in_specs, out_specs=out_specs, check_vma=False)
```
